32 devices in a mesh: blk: 16 (over z, x, core), node: 2 (over y).
Axes of the slice: x: 2, y: 2, z: 4, core: 2. Of those that a mesh axis runs over, the one named last changes fastest.
Arguments:
- image_embeds: bfloat16 [5120, 1152], P(('blk', 'node')), may hold values from -0.1796875 to 0.1796875
- text_embeds: bfloat16 [5120, 1152], P(('blk', 'node')), may hold values from -0.1796875 to 0.1796875
- pair_text: int32 [5120], replicated, may hold values from 0 to 5119, as said below
- similarity_scale: float32 [1], replicated, may hold values from 5 to 15
- logit_bias: float32 [1], replicated, may hold values from -6 to -2
Outputs:
- image_grads: float32 [5120, 1152], P(('blk', 'node'))
- text_grads: float32 [5120, 1152], P(('blk', 'node'))
The draws below stay inside these ranges and needn't reach their ends.
Inputs may be any that keep to these rules, and one draw needn't show every extreme that they name: pair_text is a permutation that maps each image to a report of its own group of 320 consecutive pairs.
All inputs are finite; a program needn't handle non-finite values.
Results may differ from the reference program's by a relative error of at most 0.0043.
Values may be sent and summed in bfloat16 or wider, within the bound.
No kernel may reach another device: no remote copies, remote signals or barrier semaphores. Data moves between devices by JAX's collectives and lax.ppermute only.
A program may use at most 64 MiB of HBM per device.

```python
import math
import jax
import jax.numpy as jnp
from jax import lax

D = 1152
TURNS = 3
GROUP = 320
PAIRS = 5120


def group_order(key):
    return jax.random.permutation(key, GROUP).astype(jnp.int32)


def draw_pair_text(key, part):
    group_count = PAIRS // GROUP
    keys = jax.random.split(jax.random.fold_in(key, 17), group_count)
    orders = jax.vmap(group_order)(keys)
    offsets = jnp.arange(group_count, dtype=jnp.int32)[:, None] * GROUP
    return (orders + offsets).reshape(PAIRS).astype(jnp.int32)


def level_of(rng, extent, pieces, least, high):
    def one(axis_at, parts):
        heights = jax.random.uniform(jax.random.fold_in(jax.random.fold_in(rng, 6), axis_at), (parts,), jnp.float32, least / len(pieces), high / len(pieces))
        return jnp.repeat(jnp.exp(heights), extent[axis_at] // parts).reshape((-1,) + (1,) * (len(extent) - axis_at - 1))

    level = one(*pieces[0])
    for cut in pieces[1:]:
        level = level * one(*cut)
    return level


def gaussian(own_key, shape, scale, most, cuts=(), kind=jnp.bfloat16):
    factor_of = level_of(own_key, shape, cuts, -0.22, 0.18) if cuts else 1.0
    result = jax.random.normal(own_key, shape, jnp.float32) * scale * factor_of
    return jnp.minimum(jnp.maximum(result, -most), most).astype(kind)


def setup_inputs(seed: int = 0) -> dict:
    streams_of = jax.random.split(jax.random.key(seed), 6)
    image_embeds = gaussian(streams_of[0], (PAIRS, D), 0.03, 0.1796875, ((0, 32),))
    text_embeds = gaussian(streams_of[1], (PAIRS, D), 0.03, 0.1796875, ((0, 32),))
    pair_text = draw_pair_text(jax.random.fold_in(streams_of[5], 71), 0)
    similarity_scale = jnp.clip(jnp.exp(jax.random.uniform(streams_of[3], (1,), jnp.float32, math.log(5.0), math.log(15.0))), 5.0, 15.0)
    logit_bias = jnp.clip(jax.random.uniform(streams_of[4], (1,), jnp.float32, -6.0, -2.0), -6.0, -2.0)
    return {"image_embeds": image_embeds, "text_embeds": text_embeds, "pair_text": pair_text, "similarity_scale": similarity_scale, "logit_bias": logit_bias}


def unit_rows(raw_rows):
    values = raw_rows.astype(jnp.float32)
    inverse = lax.rsqrt(lax.optimization_barrier(jnp.sum(values * values, axis=1, keepdims=True)) + 1e-06)
    return (values * inverse, inverse)

def tangent_part(gradient, unit_rows_f, inverse):
    return (gradient - unit_rows_f * lax.optimization_barrier(jnp.sum(unit_rows_f * gradient, axis=1, keepdims=True))) * inverse

def reference(image_embeds, text_embeds, pair_text, similarity_scale, logit_bias):
    image_unit, image_inv = unit_rows(image_embeds)
    text_unit, text_inv = unit_rows(text_embeds)
    image_half = image_unit.astype(jnp.bfloat16)
    text_half = text_unit.astype(jnp.bfloat16)
    softness_factor = similarity_scale[0]
    shift_amount_value = logit_bias[0]
    group_count = PAIRS // GROUP
    columns = jnp.arange(GROUP, dtype=jnp.int32)

    def one_group(text_total, group_index):
        row_start = (group_index * GROUP).astype(jnp.int32)
        picture_row_block = lax.dynamic_slice_in_dim(image_half, row_start, GROUP, 0)
        targets = lax.dynamic_slice_in_dim(pair_text, row_start, GROUP, 0)
        image_dir = jnp.zeros((GROUP, D), jnp.float32)
        for turn in range(TURNS):
            text_start = ((group_index + turn) % group_count * GROUP).astype(jnp.int32)
            report_vectors = lax.dynamic_slice_in_dim(text_half, text_start, GROUP, 0)
            pair_logit_matrix = softness_factor * jnp.dot(picture_row_block, report_vectors.T, preferred_element_type=jnp.float32) + shift_amount_value
            pair_label_polarity = jnp.where(targets[:, None] == (text_start + columns)[None, :], 1.0, -1.0).astype(jnp.float32)
            weight_panel = (-pair_label_polarity * softness_factor * jax.nn.sigmoid(-pair_label_polarity * pair_logit_matrix)).astype(jnp.bfloat16)
            image_dir = image_dir + jnp.dot(weight_panel, report_vectors, preferred_element_type=jnp.float32)
            previous = lax.dynamic_slice_in_dim(text_total, text_start, GROUP, 0)
            updated = previous + jnp.dot(weight_panel.T, picture_row_block, preferred_element_type=jnp.float32)
            text_total = lax.dynamic_update_slice_in_dim(text_total, updated, text_start, 0)
        return (text_total, image_dir)
    text_dir, image_parts = lax.scan(one_group, jnp.zeros((PAIRS, D), jnp.float32), jnp.arange(group_count, dtype=jnp.int32))
    image_dir = image_parts.reshape(PAIRS, D)
    image_grads = tangent_part(image_dir, image_unit, image_inv)
    text_grads = tangent_part(text_dir, text_unit, text_inv)
    return (image_grads, text_grads)
```

```python
import jax
import jax.numpy as jnp
from jax import lax
from jax.sharding import PartitionSpec as P

TURNS = 3


def shifted(block, axis, distance):
    count = lax.axis_size(axis)
    route = [(i, (i + distance) % count) for i in range(count)]
    return lax.ppermute(block, axis, route)


def unit_rows(raw_rows):
    values = raw_rows.astype(jnp.float32)
    inverse = lax.rsqrt(jnp.sum(values * values, axis=1, keepdims=True) + 1e-06)
    return (values * inverse, inverse)


def tangent_part(gradient, unit_rows_f, inverse):
    return (
        gradient - unit_rows_f * jnp.sum(unit_rows_f * gradient, axis=1, keepdims=True)
    ) * inverse


def local(image_embeds, text_embeds, pair_text, similarity_scale, logit_bias):
    rows = image_embeds.shape[0]
    node_count = lax.axis_size("node")
    node_index = lax.axis_index("node")
    cycle_index = lax.axis_index("blk")
    scale = similarity_scale[0]
    bias = logit_bias[0]

    visitors = [image_embeds] + [shifted(image_embeds, "blk", t) for t in range(1, TURNS)]
    texts = [text_embeds] + [shifted(text_embeds, "node", -k) for k in range(1, node_count)]

    image_unit, image_inv = unit_rows(image_embeds)
    text_unit, text_inv = unit_rows(text_embeds)
    image_halves = [image_unit.astype(jnp.bfloat16)] + [
        unit_rows(v)[0].astype(jnp.bfloat16) for v in visitors[1:]
    ]
    text_halves = [text_unit.astype(jnp.bfloat16)] + [
        unit_rows(v)[0].astype(jnp.bfloat16) for v in texts[1:]
    ]
    text_all = jnp.concatenate(text_halves, axis=0)

    targets = lax.dynamic_slice_in_dim(
        pair_text, (cycle_index * node_count + node_index) * rows, rows, 0
    )
    columns = jnp.concatenate(
        [
            (cycle_index * node_count + (node_index + k) % node_count) * rows
            + jnp.arange(rows, dtype=jnp.int32)
            for k in range(node_count)
        ]
    )
    paired = targets[:, None] == columns[None, :]

    image_dir = None
    back = []
    text_terms = 0.0
    for t in range(TURNS):
        logits = (
            scale
            * lax.dot_general(
                image_halves[t],
                text_all,
                (((1,), (1,)), ((), ())),
                preferred_element_type=jnp.float32,
            )
            + bias
        )
        if t == 0:
            weights = jnp.where(paired, -scale, scale) * jax.nn.sigmoid(
                jnp.where(paired, -logits, logits)
            )
        else:
            weights = scale * jax.nn.sigmoid(logits)
        weights = weights.astype(jnp.bfloat16)
        term = jnp.dot(weights, text_all, preferred_element_type=jnp.float32)
        if t == 0:
            image_dir = term
        else:
            back.append(shifted(term.astype(jnp.bfloat16), "blk", -t))
        text_terms = text_terms + lax.dot_general(
            weights,
            image_halves[t],
            (((0,), (0,)), ((), ())),
            preferred_element_type=jnp.float32,
        )
    text_dir = text_terms[:rows]
    for k in range(1, node_count):
        part = text_terms[k * rows : (k + 1) * rows].astype(jnp.bfloat16)
        text_dir = text_dir + shifted(part, "node", k).astype(jnp.float32)
    for part in back:
        image_dir = image_dir + part.astype(jnp.float32)
    image_grads = tangent_part(image_dir, image_unit, image_inv)
    text_grads = tangent_part(text_dir, text_unit, text_inv)
    return (image_grads, text_grads)


def solution(mesh):
    return jax.shard_map(
        local,
        mesh=mesh,
        in_specs=(P(("blk", "node"), None), P(("blk", "node"), None), P(), P(), P()),
        out_specs=(P(("blk", "node"), None), P(("blk", "node"), None)),
        check_vma=False,
    )
```

```python
import jax
import jax.numpy as jnp
from jax import lax
from jax.sharding import PartitionSpec as P

TURNS = 3


def unit_rows(raw_rows):
    values = raw_rows.astype(jnp.float32)
    inverse = lax.rsqrt(jnp.sum(values * values, axis=1, keepdims=True) + 1e-06)
    return (values * inverse, inverse)


def half_rows(raw_rows):
    return unit_rows(raw_rows)[0].astype(jnp.bfloat16)


def tangent_part(gradient, unit_rows_f, inverse):
    return (
        gradient - unit_rows_f * jnp.sum(unit_rows_f * gradient, axis=1, keepdims=True)
    ) * inverse


def local(image_embeds, text_embeds, pair_text, similarity_scale, logit_bias):
    rows = image_embeds.shape[0]
    cycle_count = lax.axis_size("blk")
    node_count = lax.axis_size("node")
    cycle_index = lax.axis_index("blk")
    node_index = lax.axis_index("node")
    first_core = cycle_index % 2 == 0
    scale = similarity_scale[0]
    bias = logit_bias[0]

    def send(block, parity, ahead, across=0):
        route = [
            (
                g * node_count + n,
                (g + ahead) % cycle_count * node_count + (n + across) % node_count,
            )
            for g in range(parity, cycle_count, 2)
            for n in range(node_count)
        ]
        return lax.ppermute(block, ("blk", "node"), route)

    visit_b = send(image_embeds, 1, 1)
    far_b = [send(text_embeds, 1, -1, -k) for k in range(1, node_count)]
    visit_a = send(image_embeds, 0, 2)
    far_a = [send(text_embeds, 0, 0, -k) for k in range(1, node_count)]
    mate_image = send(image_embeds, 1, -1)
    mate_text = send(text_embeds, 1, -1)

    image_unit, image_inv = unit_rows(image_embeds)
    text_unit, text_inv = unit_rows(text_embeds)

    text_a = jnp.concatenate([text_unit.astype(jnp.bfloat16)] + [half_rows(f) for f in far_a])
    text_b = jnp.concatenate([half_rows(mate_text)] + [half_rows(f) for f in far_b])
    text_ab = jnp.concatenate([text_a, text_b])
    span = text_a.shape[0]

    def weigh(images, texts, start=None, at=None):
        logits = (
            scale
            * lax.dot_general(
                images, texts, (((1,), (1,)), ((), ())), preferred_element_type=jnp.float32
            )
            + bias
        )
        if start is None:
            return (scale * jax.nn.sigmoid(logits)).astype(jnp.bfloat16)
        targets = lax.dynamic_slice_in_dim(pair_text, start, rows, 0)
        columns = jnp.concatenate(
            [
                (at * node_count + (node_index + k) % node_count) * rows
                + jnp.arange(rows, dtype=jnp.int32)
                for k in range(node_count)
            ]
        )
        paired = targets[:, None] == columns[None, :]
        return (
            jnp.where(paired, -scale, scale)
            * jax.nn.sigmoid(jnp.where(paired, -logits, logits))
        ).astype(jnp.bfloat16)

    def combine(weights, vectors):
        return jnp.dot(weights, vectors, preferred_element_type=jnp.float32)

    def gather_terms(weights, vectors):
        return lax.dot_general(
            weights, vectors, (((0,), (0,)), ((), ())), preferred_element_type=jnp.float32
        )

    group_a = cycle_index - cycle_index % 2
    va, vb = half_rows(visit_a), half_rows(visit_b)
    ia, ib = image_unit.astype(jnp.bfloat16), half_rows(mate_image)
    w_va = weigh(va, text_a)
    w_vb = weigh(vb, text_ab)
    back_a = send(combine(w_va, text_a).astype(jnp.bfloat16), 0, -2)
    back_b = send(combine(w_vb, text_ab).astype(jnp.bfloat16), 0, -1)

    start = (group_a * node_count + node_index) * rows
    w_ia = jnp.concatenate([weigh(ia, text_a, start, group_a), weigh(ia, text_b)], axis=1)
    w_ib = weigh(ib, text_b, start + node_count * rows, group_a + 1)
    terms_a = gather_terms(
        jnp.concatenate([w_ia[:, :span], w_va, w_vb[:, :span]]), jnp.concatenate([ia, va, vb])
    )
    terms_b = gather_terms(
        jnp.concatenate([w_ia[:, span:], w_ib, w_vb[:, span:]]), jnp.concatenate([ia, ib, vb])
    )

    text_back = 0.0
    for k in range(1, node_count):
        part = slice(k * rows, (k + 1) * rows)
        text_back = (
            text_back
            + send(terms_b[part].astype(jnp.bfloat16), 0, 1, k).astype(jnp.float32)
            + send(terms_a[part].astype(jnp.bfloat16), 0, 0, k).astype(jnp.float32)
        )
    image_b = send(combine(w_ib, text_b).astype(jnp.bfloat16), 0, 1)
    text_own_b = send(terms_b[:rows].astype(jnp.bfloat16), 0, 1)
    image_a = combine(w_ia, text_ab)

    image_dir = (
        jnp.where(first_core, image_a, image_b.astype(jnp.float32))
        + back_a.astype(jnp.float32)
        + back_b.astype(jnp.float32)
    )
    text_dir = jnp.where(first_core, terms_a[:rows], text_own_b.astype(jnp.float32)) + text_back
    image_grads = tangent_part(image_dir, image_unit, image_inv)
    text_grads = tangent_part(text_dir, text_unit, text_inv)
    return (image_grads, text_grads)


def solution(mesh):
    return jax.shard_map(
        local,
        mesh=mesh,
        in_specs=(P(("blk", "node"), None), P(("blk", "node"), None), P(), P(), P()),
        out_specs=(P(("blk", "node"), None), P(("blk", "node"), None)),
        check_vma=False,
    )
```

```python
import functools

import jax
import jax.numpy as jnp
from jax import lax
from jax.experimental import pallas as pl
from jax.experimental.pallas import tpu as pltpu
from jax.sharding import PartitionSpec as P

HALF = jnp.bfloat16
FULL = jnp.float32
VMEM_LIMIT = 40 * 1024 * 1024


def half_rows(raw_ref):
    values = raw_ref[...].astype(FULL)
    inverse = lax.rsqrt(jnp.sum(values * values, axis=1, keepdims=True) + 1e-06)
    return (values * inverse).astype(HALF)


def logits_of(images, texts, params):
    dots = lax.dot_general(images, texts, (((1,), (1,)), ((), ())), preferred_element_type=FULL)
    return params[0:1, 0:1] * dots + params[1:2, 0:1]


def weigh(images, texts, params):
    return (params[0:1, 0:1] * jax.nn.sigmoid(logits_of(images, texts, params))).astype(HALF)


def weigh_own(images, texts, params, targets, node):
    rows = texts.shape[0]
    logits = logits_of(images, texts, params)
    columns = lax.broadcasted_iota(jnp.int32, logits.shape, 1) + node * rows
    paired = targets == columns
    scale = params[0:1, 0:1]
    return (
        jnp.where(paired, -scale, scale) * jax.nn.sigmoid(jnp.where(paired, -logits, logits))
    ).astype(HALF)


def mix(weights, vectors):
    return jnp.dot(weights, vectors, preferred_element_type=FULL)


def mix_back(weights, vectors):
    return lax.dot_general(weights, vectors, (((0,), (0,)), ((), ())), preferred_element_type=FULL)


def roles():
    return lax.rem(lax.axis_index("blk"), 2) == 0, lax.axis_index("node")


def early_kernel(
    scale, bias, image, text, mate_image, mate_text, targets,
    params, image_h, text_h, mate_image_h, mate_text_h, image_dir, text_dir,
):
    first, node = roles()
    row = lax.broadcasted_iota(jnp.int32, params.shape, 0)
    params[...] = jnp.where(row == 0, scale[0], bias[0])
    image_h[...] = half_rows(image)
    text_h[...] = half_rows(text)
    mate_image_h[...] = half_rows(mate_image)
    mate_text_h[...] = half_rows(mate_text)
    own = weigh_own(image_h[...], text_h[...], params, targets[...], node)
    image_dir[...] = mix(own, text_h[...])
    text_dir[...] = mix_back(own, image_h[...])

    @pl.when(first)
    def _():
        cross = weigh(image_h[...], mate_text_h[...], params)
        image_dir[...] += mix(cross, mate_text_h[...])

    @pl.when(jnp.logical_not(first))
    def _():
        cross = weigh(mate_image_h[...], text_h[...], params)
        text_dir[...] += mix_back(cross, mate_image_h[...])


def first_kernel(
    far, params, targets, image_h, text_h, mate_image_h, visit_a, visit_b, *refs
):
    far_a, far_b = refs[:far], refs[far : 2 * far]
    visit_h, far_h, weights, back = refs[2 * far :]
    first, node = roles()
    nodes = far + 1

    @pl.when(first)
    def _():
        visit_h[...] = half_rows(visit_a)
        own = weigh(visit_h[...], text_h[...], params)
        weights[1, 0] = own
        total = mix(own, text_h[...])
        for k in range(far):
            far_h[k] = half_rows(far_a[k])
            outer = weigh(visit_h[...], far_h[k], params)
            weights[1, k + 1] = outer
            total += mix(outer, far_h[k])
        back[0] = total.astype(HALF)

    @pl.when(jnp.logical_not(first))
    def _():
        visit_h[...] = half_rows(visit_b)
        for k in range(far):
            far_h[k] = half_rows(far_b[k])
            one = weigh_own(
                image_h[...], far_h[k], params, targets[...], lax.rem(node + k + 1, nodes)
            )
            two = weigh(visit_h[...], far_h[k], params)
            three = weigh(mate_image_h[...], far_h[k], params)
            weights[0, k + 1] = one
            weights[1, k + 1] = two
            total = mix_back(one, image_h[...])
            total += mix_back(two, visit_h[...])
            total += mix_back(three, mate_image_h[...])
            back[k] = total.astype(HALF)


def second_kernel(
    far, params, targets, image_h, text_h, mate_text_h, visit_h, far_h, weights, relay_visit, *refs
):
    relay_far = refs[:far]
    third_h, more, back = refs[far:]
    first, node = roles()
    nodes = far + 1

    @pl.when(first)
    def _():
        third_h[...] = half_rows(relay_visit)
        more[2, 0] = weigh(third_h[...], text_h[...], params)
        for k in range(far):
            one = weigh_own(
                image_h[...], far_h[k], params, targets[...], lax.rem(node + k + 1, nodes)
            )
            three = weigh(third_h[...], far_h[k], params)
            more[0, k + 1] = one
            total = mix_back(one, image_h[...])
            total += mix_back(weights[1, k + 1], visit_h[...])
            total += mix_back(three, third_h[...])
            back[k] = total.astype(HALF)

    @pl.when(jnp.logical_not(first))
    def _():
        own = weigh(visit_h[...], text_h[...], params)
        more[1, 0] = own
        total = mix(own, text_h[...])
        total += mix(weigh(visit_h[...], mate_text_h[...], params), mate_text_h[...])
        for k in range(far):
            total += mix(weights[1, k + 1], far_h[k])
            beyond = half_rows(relay_far[k])
            total += mix(weigh(visit_h[...], beyond, params), beyond)
        back[0] = total.astype(HALF)


def third_kernel(
    far, params, image_h, visit_h, third_h, far_h, weights, more, image_part, text_part, *refs
):
    mate_far = refs[:far]
    image_dir, text_dir = refs[far:]
    first, _ = roles()

    @pl.when(first)
    def _():
        total = text_part[...] + mix_back(weights[1, 0], visit_h[...])
        text_dir[...] = total + mix_back(more[2, 0], third_h[...])
        total = image_part[...]
        for k in range(far):
            total += mix(more[0, k + 1], far_h[k])
            beyond = half_rows(mate_far[k])
            total += mix(weigh(image_h[...], beyond, params), beyond)
        image_dir[...] = total

    @pl.when(jnp.logical_not(first))
    def _():
        text_dir[...] = text_part[...] + mix_back(more[1, 0], visit_h[...])
        total = image_part[...]
        for k in range(far):
            total += mix(weights[0, k + 1], far_h[k])
        image_dir[...] = total


def last_kernel(far, image, text, image_dir, text_dir, *refs):
    one, two = refs[:far], refs[far : 2 * far]
    image_grads, text_grads = refs[2 * far :]
    first, _ = roles()

    def summed(parts):
        total = parts[0][...].astype(FULL)
        for part in parts[1:]:
            total += part[...].astype(FULL)
        return total

    def tangent(raw, gradient):
        values = raw[...].astype(FULL)
        inverse = lax.rsqrt(jnp.sum(values * values, axis=1, keepdims=True) + 1e-06)
        unit = values * inverse
        return (gradient - unit * jnp.sum(unit * gradient, axis=1, keepdims=True)) * inverse

    @pl.when(first)
    def _():
        image_grads[...] = tangent(image, image_dir[...] + one[0][...].astype(FULL))
        text_grads[...] = tangent(text, text_dir[...] + summed(two))

    @pl.when(jnp.logical_not(first))
    def _():
        image_grads[...] = tangent(image, image_dir[...] + two[0][...].astype(FULL))
        text_grads[...] = tangent(text, text_dir[...] + summed(one))


def call(kernel, name, operands, shapes, smem=0, flops=0, result_in_vmem=True):
    place = pltpu.VMEM if result_in_vmem else (lambda s, d: jax.ShapeDtypeStruct(s, d))
    operands = list(operands)
    size = sum(x.size * x.dtype.itemsize for x in operands)
    return pl.pallas_call(
        kernel,
        name=name,
        out_shape=[place(s, d) for s, d in shapes],
        in_specs=[pl.BlockSpec(memory_space=pltpu.SMEM)] * smem
        + [pl.BlockSpec(memory_space=pltpu.VMEM)] * (len(operands) - smem),
        out_specs=[pl.BlockSpec(memory_space=pltpu.VMEM)] * len(shapes),
        compiler_params=pltpu.CompilerParams(vmem_limit_bytes=VMEM_LIMIT),
        cost_estimate=pl.CostEstimate(flops=flops, bytes_accessed=size, transcendentals=0),
    )(*operands)


def local(image_embeds, text_embeds, pair_text, similarity_scale, logit_bias):
    rows, width = image_embeds.shape
    cycle_count = lax.axis_size("blk")
    node_count = lax.axis_size("node")
    far = node_count - 1
    cycle_index = lax.axis_index("blk")
    node_index = lax.axis_index("node")

    def send(block, even, odd):
        route = []
        for g in range(cycle_count):
            ahead, across = odd if g % 2 else even
            for n in range(node_count):
                to = (g + ahead) % cycle_count * node_count + (n + across) % node_count
                route.append((g * node_count + n, to))
        return lax.ppermute(block, ("blk", "node"), route)

    stay = (0, 0)

    def swap(block):
        return send(block, (1, 0), (-1, 0))

    mate_text = swap(text_embeds)
    mate_image = swap(image_embeds)
    visit_b = send(image_embeds, stay, (2, 0))
    far_a = [send(text_embeds, (0, -k), stay) for k in range(1, node_count)]
    visit_a = send(image_embeds, (2, 0), stay)
    far_b = [send(text_embeds, stay, (0, -k)) for k in range(1, node_count)]

    start = (cycle_index * node_count + node_index) * rows
    targets = lax.dynamic_slice_in_dim(pair_text, start, rows, 0)
    targets = (targets - cycle_index * node_count * rows)[:, None]

    block_h = ((rows, width), HALF)
    block_f = ((rows, width), FULL)
    params, image_h, text_h, mate_image_h, mate_text_h, image_part, text_part = call(
        early_kernel,
        "early",
        [similarity_scale, logit_bias, image_embeds, text_embeds, mate_image, mate_text, targets],
        [((8, 128), FULL), block_h, block_h, block_h, block_h, block_f, block_f],
        smem=2,
    )
    relay_visit = swap(visit_b)
    relay_far = [swap(block) for block in far_a]
    tiles = ((3, node_count, rows, rows), HALF)
    returns = ((far, rows, width), HALF)
    visit_h, far_h, weights, back = call(
        functools.partial(first_kernel, far),
        "first",
        [params, targets, image_h, text_h, mate_image_h, visit_a, visit_b, *far_a, *far_b],
        [block_h, ((far, rows, width), HALF), tiles, returns],
    )
    one = [send(back[0], (-2, 0), (0, 1))] + [
        send(back[k], stay, (0, k + 1)) for k in range(1, far)
    ]
    mate_far = [swap(block) for block in far_b]
    third_h, more, back = call(
        functools.partial(second_kernel, far),
        "second",
        [params, targets, image_h, text_h, mate_text_h, visit_h, far_h, weights, relay_visit]
        + relay_far,
        [block_h, tiles, returns],
    )
    two = [send(back[0], (0, 1), (-2, 0))] + [
        send(back[k], (0, k + 1), stay) for k in range(1, far)
    ]
    image_dir, text_dir = call(
        functools.partial(third_kernel, far),
        "third",
        [params, image_h, visit_h, third_h, far_h, weights, more, image_part, text_part]
        + mate_far,
        [block_f, block_f],
    )
    return tuple(
        call(
            functools.partial(last_kernel, far),
            "last",
            [image_embeds, text_embeds, image_dir, text_dir, *one, *two],
            [block_f, block_f],
            result_in_vmem=False,
        )
    )


def solution(mesh):
    return jax.shard_map(
        local,
        mesh=mesh,
        in_specs=(P(("blk", "node"), None), P(("blk", "node"), None), P(), P(), P()),
        out_specs=(P(("blk", "node"), None), P(("blk", "node"), None)),
        check_vma=False,
    )
```

```python
import functools

import jax
import jax.numpy as jnp
from jax import lax
from jax.experimental import pallas as pl
from jax.experimental.pallas import tpu as pltpu
from jax.sharding import PartitionSpec as P

HALF = jnp.bfloat16
FULL = jnp.float32
VMEM_LIMIT = 40 * 1024 * 1024


def roles():
    return lax.rem(lax.axis_index("blk"), 2) == 0, lax.axis_index("node")


def by_role(on_first, on_second):
    first, node = roles()
    pl.when(first)(functools.partial(on_first, node))
    pl.when(jnp.logical_not(first))(functools.partial(on_second, node))


def logits_of(images, texts, params):
    dots = lax.dot_general(images, texts, (((1,), (1,)), ((), ())), preferred_element_type=FULL)
    return params[0:1, 0:1] * dots + params[1:2, 0:1]


def weigh(images, texts, params):
    return (params[0:1, 0:1] * jax.nn.sigmoid(logits_of(images, texts, params))).astype(HALF)


def weigh_own(images, texts, params, targets, node):
    rows = texts.shape[0]
    logits = logits_of(images, texts, params)
    columns = lax.broadcasted_iota(jnp.int32, logits.shape, 1) + node * rows
    paired = targets == columns
    scale = params[0:1, 0:1]
    return (
        jnp.where(paired, -scale, scale) * jax.nn.sigmoid(jnp.where(paired, -logits, logits))
    ).astype(HALF)


def mix(weights, vectors):
    return jnp.dot(weights, vectors, preferred_element_type=FULL)


def mix_back(weights, vectors):
    return lax.dot_general(weights, vectors, (((0,), (0,)), ((), ())), preferred_element_type=FULL)


def unit_kernel(image, text, lead_raw, rest_raw, lead, rest, lead_inv, rest_inv, sems):
    rows = lead.shape[0]
    part = rows // 2 if rows % 32 == 0 else rows
    pieces = [pl.ds(at, part) for at in range(0, rows, part)]

    def copies(source, target, base):
        return [
            pltpu.make_async_copy(source.at[piece], target.at[piece], sems.at[base + i])
            for i, piece in enumerate(pieces)
        ]

    def fetch(lead_source, rest_source, node):
        for copy in copies(lead_source, lead_raw, 0) + copies(rest_source, rest_raw, 2):
            copy.start()

    by_role(functools.partial(fetch, text, image), functools.partial(fetch, image, text))
    for base, raw, half, inv in ((0, lead_raw, lead, lead_inv), (2, rest_raw, rest, rest_inv)):
        for piece, copy in zip(pieces, copies(image, raw, base)):
            copy.wait()
            values = raw[piece, :].astype(FULL)
            inverse = lax.rsqrt(jnp.sum(values * values, axis=1, keepdims=True) + 1e-06)
            half[piece, :] = (values * inverse).astype(HALF)
            inv[piece, :] = inverse


def half_rows(raw):
    values = raw[...].astype(FULL)
    inverse = lax.rsqrt(jnp.sum(values * values, axis=1, keepdims=True) + 1e-06)
    return (values * inverse).astype(HALF)


def early_kernel(
    scale, bias, targets, lead, rest, mate_image, mate_text,
    params, mate_lead, mate_rest, lead_part, rest_part,
):
    row = lax.broadcasted_iota(jnp.int32, params.shape, 0)
    params[...] = jnp.where(row == 0, scale[0], bias[0])

    def on_first(node):
        mate_rest[...] = half_rows(mate_text)
        own = weigh_own(rest[...], lead[...], params, targets[...], node)
        cross = weigh(rest[...], mate_rest[...], params)
        rest_part[...] = mix(own, lead[...]) + mix(cross, mate_rest[...])
        lead_part[...] = mix_back(own, rest[...])

    def on_second(node):
        mate_rest[...] = half_rows(mate_image)
        mate_lead[...] = half_rows(mate_text)
        own = weigh_own(lead[...], rest[...], params, targets[...], node)
        cross = weigh(mate_rest[...], rest[...], params)
        lead_part[...] = mix(own, rest[...])
        rest_part[...] = mix_back(own, lead[...]) + mix_back(cross, mate_rest[...])

    by_role(on_first, on_second)


def first_kernel(far, params, targets, lead, rest, mate_rest, *refs):
    got1, got2 = refs[:far], refs[far : 2 * far]
    weights, back = refs[2 * far :]

    def on_first(node):
        visit = got2[0][...]
        own = weigh(visit, lead[...], params)
        weights[1, 0] = own
        total = mix(own, lead[...])
        for k in range(far):
            outer = weigh(visit, got1[k][...], params)
            weights[1, k + 1] = outer
            total += mix(outer, got1[k][...])
        back[0] = total.astype(HALF)

    def on_second(node):
        visit = got1[0][...]
        for k in range(far):
            texts = got2[k][...]
            one = weigh_own(
                lead[...], texts, params, targets[...], lax.rem(node + k + 1, far + 1)
            )
            two = weigh(visit, texts, params)
            three = weigh(mate_rest[...], texts, params)
            weights[0, k + 1] = one
            weights[1, k + 1] = two
            total = mix_back(one, lead[...]) + mix_back(two, visit)
            back[k] = (total + mix_back(three, mate_rest[...])).astype(HALF)

    by_role(on_first, on_second)


def second_kernel(far, params, targets, lead, rest, mate_lead, weights, *refs):
    got1, got2, relay1 = refs[:far], refs[far : 2 * far], refs[2 * far : 3 * far]
    more, back = refs[3 * far :]

    def on_first(node):
        third = relay1[0][...]
        for k in range(far):
            texts = got1[k][...]
            one = weigh_own(
                rest[...], texts, params, targets[...], lax.rem(node + k + 1, far + 1)
            )
            three = weigh(third, texts, params)
            more[0, k + 1] = one
            total = mix_back(one, rest[...]) + mix_back(weights[1, k + 1], got2[0][...])
            back[k] = (total + mix_back(three, third)).astype(HALF)

    def on_second(node):
        visit = got1[0][...]
        own = weigh(visit, rest[...], params)
        more[1, 0] = own
        total = mix(own, rest[...]) + mix(weigh(visit, mate_lead[...], params), mate_lead[...])
        for k in range(far):
            total += mix(weights[1, k + 1], got2[k][...])
            beyond = relay1[k][...]
            total += mix(weigh(visit, beyond, params), beyond)
        back[0] = total.astype(HALF)

    by_role(on_first, on_second)


def third_kernel(far, params, lead, rest, weights, more, lead_part, rest_part, *refs):
    got1, got2 = refs[:far], refs[far : 2 * far]
    relay1, relay2 = refs[2 * far : 3 * far], refs[3 * far : 4 * far]
    lead_dir, rest_dir = refs[4 * far :]

    def on_first(node):
        total = rest_part[...]
        for k in range(far):
            total += mix(more[0, k + 1], got1[k][...])
            beyond = relay2[k][...]
            total += mix(weigh(rest[...], beyond, params), beyond)
        rest_dir[...] = total
        third = relay1[0][...]
        total = lead_part[...] + mix_back(weights[1, 0], got2[0][...])
        lead_dir[...] = total + mix_back(weigh(third, lead[...], params), third)

    def on_second(node):
        rest_dir[...] = rest_part[...] + mix_back(more[1, 0], got1[0][...])
        total = lead_part[...]
        for k in range(far):
            total += mix(weights[0, k + 1], got2[k][...])
        lead_dir[...] = total

    by_role(on_first, on_second)


def tangent_kernel(far, sums_on_first, raw, inverse, direction, *refs):
    parts = refs[:far]
    image_grads, text_grads, held, sems = refs[-4:]
    rows = raw.shape[0]
    part = rows // 5 if rows % 80 == 0 else rows
    pieces = [pl.ds(at, part) for at in range(0, rows, part)]

    def run(out, count, node):
        copies = []
        for i, piece in enumerate(pieces):
            gradient = direction[piece, :]
            for k in range(count):
                gradient += parts[k][piece, :].astype(FULL)
            inv = inverse[piece, :]
            unit = raw[piece, :].astype(FULL) * inv
            along = jnp.sum(unit * gradient, axis=1, keepdims=True)
            held[piece, :] = (gradient - unit * along) * inv
            copy = pltpu.make_async_copy(held.at[piece], out.at[piece], sems.at[i])
            copy.start()
            copies.append(copy)
        for copy in copies:
            copy.wait()

    if sums_on_first:
        by_role(
            functools.partial(run, text_grads, far), functools.partial(run, image_grads, 1)
        )
    else:
        by_role(
            functools.partial(run, image_grads, 1), functools.partial(run, text_grads, far)
        )


def call(kernel, name, operands, shapes, smem=0, anywhere=0, scratch=(), flops=0, **more):
    operands = list(operands)
    size = sum(x.size * x.dtype.itemsize for x in operands)
    held = pl.BlockSpec(memory_space=pltpu.VMEM)
    for i in range(smem, smem + anywhere):
        operands[i] = pltpu.with_memory_space_constraint(operands[i], pltpu.HBM)
    return pl.pallas_call(
        kernel,
        name=name,
        out_shape=[pltpu.VMEM(s, d) for s, d in shapes],
        in_specs=[pl.BlockSpec(memory_space=pltpu.SMEM)] * smem
        + [pl.BlockSpec(memory_space=pltpu.HBM)] * anywhere
        + [held] * (len(operands) - smem - anywhere),
        out_specs=[held] * len(shapes),
        scratch_shapes=scratch,
        compiler_params=pltpu.CompilerParams(vmem_limit_bytes=VMEM_LIMIT),
        cost_estimate=pl.CostEstimate(flops=flops, bytes_accessed=size, transcendentals=0),
        **more,
    )(*operands)


def tangent(far, sums_on_first, operands, grads, block):
    rows = block[0][0]
    anywhere = pl.BlockSpec(memory_space=pl.ANY)
    count = len(operands)
    return pl.pallas_call(
        functools.partial(tangent_kernel, far, sums_on_first),
        name="tangent",
        out_shape=[jax.ShapeDtypeStruct(*block)] * 2,
        in_specs=[pl.BlockSpec(memory_space=pltpu.VMEM)] * count + [anywhere] * len(grads),
        out_specs=[anywhere] * 2,
        scratch_shapes=[pltpu.VMEM(*block), pltpu.SemaphoreType.DMA((5,))],
        input_output_aliases={count + i: i for i in range(len(grads))},
        compiler_params=pltpu.CompilerParams(vmem_limit_bytes=VMEM_LIMIT),
    )(*operands, *grads)


def local(image_embeds, text_embeds, pair_text, similarity_scale, logit_bias):
    rows, width = image_embeds.shape
    cycle_count = lax.axis_size("blk")
    node_count = lax.axis_size("node")
    far = node_count - 1
    cycle_index = lax.axis_index("blk")
    node_index = lax.axis_index("node")

    def send(block, even, odd):
        route = []
        for g in range(cycle_count):
            ahead, across = odd if g % 2 else even
            for n in range(node_count):
                to = (g + ahead) % cycle_count * node_count + (n + across) % node_count
                route.append((g * node_count + n, to))
        return lax.ppermute(block, ("blk", "node"), route)

    def swap(block):
        return send(block, (1, 0), (-1, 0))

    stay = (0, 0)
    ahead, behind = (2, 0), (-2, 0)
    block_h = ((rows, width), HALF)
    block_f = ((rows, width), FULL)
    column = ((rows, 1), FULL)
    tiles = ((3, node_count, rows, rows), HALF)
    returns = ((far, rows, width), HALF)

    mate_image = swap(image_embeds)
    mate_text = swap(text_embeds)
    lead_raw, rest_raw, lead, rest, lead_inv, rest_inv = call(
        unit_kernel,
        "unit",
        [image_embeds, text_embeds],
        [block_h, block_h, block_h, block_h, column, column],
        anywhere=2,
        scratch=[pltpu.SemaphoreType.DMA((4,))],
    )
    got1 = [send(lead, (0, -k), ahead if k == 1 else stay) for k in range(1, node_count)]
    got2 = [send(rest, ahead if k == 1 else stay, (0, -k)) for k in range(1, node_count)]

    start = (cycle_index * node_count + node_index) * rows
    targets = lax.dynamic_slice_in_dim(pair_text, start, rows, 0)
    targets = (targets - cycle_index * node_count * rows)[:, None]

    params, mate_lead, mate_rest, lead_part, rest_part = call(
        early_kernel,
        "early",
        [similarity_scale, logit_bias, targets, lead, rest, mate_image, mate_text],
        [((8, 128), FULL), block_h, block_h, block_f, block_f],
        smem=2,
    )
    *got2, params = lax.optimization_barrier((*got2, params))
    relay1 = [swap(block) for block in got1]
    relay2 = [swap(block) for block in got2]
    weights, back = call(
        functools.partial(first_kernel, far),
        "first",
        [params, targets, lead, rest, mate_rest, *got1, *got2],
        [tiles, returns],
    )
    one = [
        send(back[k], behind if k == 0 else stay, (0, k + 1)) for k in range(far)
    ]
    more, back = call(
        functools.partial(second_kernel, far),
        "second",
        [params, targets, lead, rest, mate_lead, weights, *got1, *got2, *relay1],
        [tiles, returns],
    )
    two = [
        send(back[k], (0, k + 1), behind if k == 0 else stay) for k in range(far)
    ]
    lead_dir, rest_dir = call(
        functools.partial(third_kernel, far),
        "third",
        [params, lead, rest, weights, more, lead_part, rest_part, *got1, *got2, *relay1, *relay2],
        [block_f, block_f],
    )
    grads = tangent(far, False, [rest_raw, rest_inv, rest_dir, *one], [], block_f)
    return tuple(tangent(far, True, [lead_raw, lead_inv, lead_dir, *two], grads, block_f))


def solution(mesh):
    return jax.shard_map(
        local,
        mesh=mesh,
        in_specs=(P(("blk", "node"), None), P(("blk", "node"), None), P(), P(), P()),
        out_specs=(P(("blk", "node"), None), P(("blk", "node"), None)),
        check_vma=False,
    )
```

```python
import functools

import jax
import jax.numpy as jnp
from jax import lax
from jax.experimental import pallas as pl
from jax.experimental.pallas import tpu as pltpu
from jax.sharding import PartitionSpec as P

HALF = jnp.bfloat16
FULL = jnp.float32
VMEM_LIMIT = 40 * 1024 * 1024


def roles():
    return lax.rem(lax.axis_index("blk"), 2) == 0, lax.axis_index("node")


def by_role(on_first, on_second):
    first, node = roles()
    pl.when(first)(functools.partial(on_first, node))
    pl.when(jnp.logical_not(first))(functools.partial(on_second, node))


def logits_of(images, texts, params):
    dots = lax.dot_general(images, texts, (((1,), (1,)), ((), ())), preferred_element_type=FULL)
    return params[0:1, 0:1] * dots + params[1:2, 0:1]


def weigh(images, texts, params):
    return (params[0:1, 0:1] * jax.nn.sigmoid(logits_of(images, texts, params))).astype(HALF)


def weigh_own(images, texts, params, targets, node):
    rows = texts.shape[0]
    logits = logits_of(images, texts, params)
    columns = lax.broadcasted_iota(jnp.int32, logits.shape, 1) + node * rows
    paired = targets == columns
    scale = params[0:1, 0:1]
    return (
        jnp.where(paired, -scale, scale) * jax.nn.sigmoid(jnp.where(paired, -logits, logits))
    ).astype(HALF)


def mix(weights, vectors):
    return jnp.dot(weights, vectors, preferred_element_type=FULL)


def mix_back(weights, vectors):
    return lax.dot_general(weights, vectors, (((0,), (0,)), ((), ())), preferred_element_type=FULL)


def unit_kernel(image, text, lead_raw, rest_raw, lead, rest, lead_inv, rest_inv, sems):
    rows = lead.shape[0]
    part = rows // 2 if rows % 32 == 0 else rows
    pieces = [pl.ds(at, part) for at in range(0, rows, part)]

    def copies(source, target, base):
        return [
            pltpu.make_async_copy(source.at[piece], target.at[piece], sems.at[base + i])
            for i, piece in enumerate(pieces)
        ]

    def fetch(lead_source, rest_source, node):
        for copy in copies(lead_source, lead_raw, 0) + copies(rest_source, rest_raw, 2):
            copy.start()

    by_role(functools.partial(fetch, text, image), functools.partial(fetch, image, text))
    for base, raw, half, inv in ((0, lead_raw, lead, lead_inv), (2, rest_raw, rest, rest_inv)):
        for piece, copy in zip(pieces, copies(image, raw, base)):
            copy.wait()
            values = raw[piece, :].astype(FULL)
            inverse = lax.rsqrt(jnp.sum(values * values, axis=1, keepdims=True) + 1e-06)
            half[piece, :] = (values * inverse).astype(HALF)
            inv[piece, :] = inverse


def early_kernel(
    scale, bias, targets, lead, rest, mate_rest, params, lead_part, rest_part
):
    row = lax.broadcasted_iota(jnp.int32, params.shape, 0)
    params[...] = jnp.where(row == 0, scale[0], bias[0])

    def on_first(node):
        own = weigh_own(rest[...], lead[...], params, targets[...], node)
        cross = weigh(rest[...], mate_rest[...], params)
        rest_part[...] = mix(own, lead[...]) + mix(cross, mate_rest[...])
        lead_part[...] = mix_back(own, rest[...])

    def on_second(node):
        own = weigh_own(lead[...], rest[...], params, targets[...], node)
        cross = weigh(mate_rest[...], rest[...], params)
        lead_part[...] = mix(own, rest[...])
        rest_part[...] = mix_back(own, lead[...]) + mix_back(cross, mate_rest[...])

    by_role(on_first, on_second)


def first_kernel(far, params, targets, lead, rest, mate_rest, *refs):
    got1, got2 = refs[:far], refs[far : 2 * far]
    weights, back = refs[2 * far :]

    def on_first(node):
        visit = got2[0][...]
        own = weigh(visit, lead[...], params)
        weights[1, 0] = own
        total = mix(own, lead[...])
        for k in range(far):
            outer = weigh(visit, got1[k][...], params)
            weights[1, k + 1] = outer
            total += mix(outer, got1[k][...])
        back[0] = total.astype(HALF)

    def on_second(node):
        visit = got1[0][...]
        for k in range(far):
            texts = got2[k][...]
            one = weigh_own(
                lead[...], texts, params, targets[...], lax.rem(node + k + 1, far + 1)
            )
            two = weigh(visit, texts, params)
            three = weigh(mate_rest[...], texts, params)
            weights[0, k + 1] = one
            weights[1, k + 1] = two
            total = mix_back(one, lead[...]) + mix_back(two, visit)
            back[k] = (total + mix_back(three, mate_rest[...])).astype(HALF)

    by_role(on_first, on_second)


def second_kernel(far, params, targets, lead, rest, mate_lead, weights, *refs):
    got1, got2, relay1 = refs[:far], refs[far : 2 * far], refs[2 * far : 3 * far]
    more, back = refs[3 * far :]

    def on_first(node):
        third = relay1[0][...]
        for k in range(far):
            texts = got1[k][...]
            one = weigh_own(
                rest[...], texts, params, targets[...], lax.rem(node + k + 1, far + 1)
            )
            three = weigh(third, texts, params)
            more[0, k + 1] = one
            total = mix_back(one, rest[...]) + mix_back(weights[1, k + 1], got2[0][...])
            back[k] = (total + mix_back(three, third)).astype(HALF)

    def on_second(node):
        visit = got1[0][...]
        own = weigh(visit, rest[...], params)
        more[1, 0] = own
        total = mix(own, rest[...]) + mix(weigh(visit, mate_lead[...], params), mate_lead[...])
        for k in range(far):
            total += mix(weights[1, k + 1], got2[k][...])
            beyond = relay1[k][...]
            total += mix(weigh(visit, beyond, params), beyond)
        back[0] = total.astype(HALF)

    by_role(on_first, on_second)


def third_kernel(far, params, lead, rest, weights, more, lead_part, rest_part, *refs):
    got1, got2 = refs[:far], refs[far : 2 * far]
    relay1, relay2 = refs[2 * far : 3 * far], refs[3 * far : 4 * far]
    lead_dir, rest_dir = refs[4 * far :]

    def on_first(node):
        total = rest_part[...]
        for k in range(far):
            total += mix(more[0, k + 1], got1[k][...])
            beyond = relay2[k][...]
            total += mix(weigh(rest[...], beyond, params), beyond)
        rest_dir[...] = total
        third = relay1[0][...]
        total = lead_part[...] + mix_back(weights[1, 0], got2[0][...])
        lead_dir[...] = total + mix_back(weigh(third, lead[...], params), third)

    def on_second(node):
        rest_dir[...] = rest_part[...] + mix_back(more[1, 0], got1[0][...])
        total = lead_part[...]
        for k in range(far):
            total += mix(weights[0, k + 1], got2[k][...])
        lead_dir[...] = total

    by_role(on_first, on_second)


def tangent_kernel(far, sums_on_first, raw, inverse, direction, *refs):
    parts = refs[:far]
    image_grads, text_grads, held, sems = refs[-4:]
    rows = raw.shape[0]
    part = rows // 5 if rows % 80 == 0 else rows
    pieces = [pl.ds(at, part) for at in range(0, rows, part)]

    def run(out, count, node):
        copies = []
        for i, piece in enumerate(pieces):
            gradient = direction[piece, :]
            for k in range(count):
                gradient += parts[k][piece, :].astype(FULL)
            inv = inverse[piece, :]
            unit = raw[piece, :].astype(FULL) * inv
            along = jnp.sum(unit * gradient, axis=1, keepdims=True)
            held[piece, :] = (gradient - unit * along) * inv
            copy = pltpu.make_async_copy(held.at[piece], out.at[piece], sems.at[i])
            copy.start()
            copies.append(copy)
        for copy in copies:
            copy.wait()

    if sums_on_first:
        by_role(
            functools.partial(run, text_grads, far), functools.partial(run, image_grads, 1)
        )
    else:
        by_role(
            functools.partial(run, image_grads, 1), functools.partial(run, text_grads, far)
        )


def call(kernel, name, operands, shapes, smem=0, anywhere=0, scratch=(), flops=0, **more):
    operands = list(operands)
    size = sum(x.size * x.dtype.itemsize for x in operands)
    held = pl.BlockSpec(memory_space=pltpu.VMEM)
    for i in range(smem, smem + anywhere):
        operands[i] = pltpu.with_memory_space_constraint(operands[i], pltpu.HBM)
    return pl.pallas_call(
        kernel,
        name=name,
        out_shape=[pltpu.VMEM(s, d) for s, d in shapes],
        in_specs=[pl.BlockSpec(memory_space=pltpu.SMEM)] * smem
        + [pl.BlockSpec(memory_space=pltpu.HBM)] * anywhere
        + [held] * (len(operands) - smem - anywhere),
        out_specs=[held] * len(shapes),
        scratch_shapes=scratch,
        compiler_params=pltpu.CompilerParams(vmem_limit_bytes=VMEM_LIMIT),
        cost_estimate=pl.CostEstimate(flops=flops, bytes_accessed=size, transcendentals=0),
        **more,
    )(*operands)


def tangent(far, sums_on_first, operands, grads, block):
    rows = block[0][0]
    anywhere = pl.BlockSpec(memory_space=pl.ANY)
    count = len(operands)
    return pl.pallas_call(
        functools.partial(tangent_kernel, far, sums_on_first),
        name="tangent",
        out_shape=[jax.ShapeDtypeStruct(*block)] * 2,
        in_specs=[pl.BlockSpec(memory_space=pltpu.VMEM)] * count + [anywhere] * len(grads),
        out_specs=[anywhere] * 2,
        scratch_shapes=[pltpu.VMEM(*block), pltpu.SemaphoreType.DMA((5,))],
        input_output_aliases={count + i: i for i in range(len(grads))},
        compiler_params=pltpu.CompilerParams(vmem_limit_bytes=VMEM_LIMIT),
    )(*operands, *grads)


def local(image_embeds, text_embeds, pair_text, similarity_scale, logit_bias):
    rows, width = image_embeds.shape
    cycle_count = lax.axis_size("blk")
    node_count = lax.axis_size("node")
    far = node_count - 1
    cycle_index = lax.axis_index("blk")
    node_index = lax.axis_index("node")

    def send(block, even, odd):
        route = []
        for g in range(cycle_count):
            ahead, across = odd if g % 2 else even
            for n in range(node_count):
                to = (g + ahead) % cycle_count * node_count + (n + across) % node_count
                route.append((g * node_count + n, to))
        return lax.ppermute(block, ("blk", "node"), route)

    def swap(block):
        return send(block, (1, 0), (-1, 0))

    stay = (0, 0)
    ahead, behind = (2, 0), (-2, 0)
    block_h = ((rows, width), HALF)
    block_f = ((rows, width), FULL)
    column = ((rows, 1), FULL)
    tiles = ((3, node_count, rows, rows), HALF)
    returns = ((far, rows, width), HALF)

    lead_raw, rest_raw, lead, rest, lead_inv, rest_inv = call(
        unit_kernel,
        "unit",
        [image_embeds, text_embeds],
        [block_h, block_h, block_h, block_h, column, column],
        anywhere=2,
        scratch=[pltpu.SemaphoreType.DMA((4,))],
    )
    got1 = [send(lead, (0, -k), ahead if k == 1 else stay) for k in range(1, node_count)]
    got2 = [send(rest, ahead if k == 1 else stay, (0, -k)) for k in range(1, node_count)]
    mate_rest = swap(rest)
    mate_lead = swap(lead)

    start = (cycle_index * node_count + node_index) * rows
    targets = lax.dynamic_slice_in_dim(pair_text, start, rows, 0)
    targets = (targets - cycle_index * node_count * rows)[:, None]

    params, lead_part, rest_part = call(
        early_kernel,
        "early",
        [similarity_scale, logit_bias, targets, lead, rest, mate_rest],
        [((8, 128), FULL), block_f, block_f],
        smem=2,
    )
    *got1, params = lax.optimization_barrier((*got1, params))
    relay1 = [swap(block) for block in got1]
    *got2, params = lax.optimization_barrier((*got2, params))
    relay2 = [swap(block) for block in got2]
    weights, back = call(
        functools.partial(first_kernel, far),
        "first",
        [params, targets, lead, rest, mate_rest, *got1, *got2],
        [tiles, returns],
    )
    one = [
        send(back[k], behind if k == 0 else stay, (0, k + 1)) for k in range(far)
    ]
    more, back = call(
        functools.partial(second_kernel, far),
        "second",
        [params, targets, lead, rest, mate_lead, weights, *got1, *got2, *relay1],
        [tiles, returns],
    )
    two = [
        send(back[k], (0, k + 1), behind if k == 0 else stay) for k in range(far)
    ]
    lead_dir, rest_dir = call(
        functools.partial(third_kernel, far),
        "third",
        [params, lead, rest, weights, more, lead_part, rest_part, *got1, *got2, *relay1, *relay2],
        [block_f, block_f],
    )
    grads = tangent(far, False, [rest_raw, rest_inv, rest_dir, *one], [], block_f)
    return tuple(tangent(far, True, [lead_raw, lead_inv, lead_dir, *two], grads, block_f))


def solution(mesh):
    return jax.shard_map(
        local,
        mesh=mesh,
        in_specs=(P(("blk", "node"), None), P(("blk", "node"), None), P(), P(), P()),
        out_specs=(P(("blk", "node"), None), P(("blk", "node"), None)),
        check_vma=False,
    )
```

```python
import functools

import jax
import jax.numpy as jnp
from jax import lax
from jax.experimental import pallas as pl
from jax.experimental.pallas import tpu as pltpu
from jax.sharding import PartitionSpec as P

HALF = jnp.bfloat16
FULL = jnp.float32
VMEM_LIMIT = 40 * 1024 * 1024


def roles():
    return lax.rem(lax.axis_index("blk"), 2) == 0, lax.axis_index("node")


def by_role(on_first, on_second):
    first, node = roles()
    pl.when(first)(functools.partial(on_first, node))
    pl.when(jnp.logical_not(first))(functools.partial(on_second, node))


def drawn(params, rows, partners, paired=None):
    vectors = jnp.concatenate([partner[...] for partner in partners], axis=0)
    dots = lax.dot_general(
        rows[...], vectors, (((1,), (1,)), ((), ())), preferred_element_type=FULL
    )
    scale, bias = params[0:1, 0:1], params[1:2, 0:1]
    logits = scale * dots + bias
    if paired is None:
        weights = scale * jax.nn.sigmoid(logits)
    else:
        pairs = paired(logits.shape)
        weights = jnp.where(pairs, -scale, scale) * jax.nn.sigmoid(
            jnp.where(pairs, -logits, logits)
        )
    return jnp.dot(weights.astype(HALF), vectors, preferred_element_type=FULL)


def text_pairs(targets, node):
    def paired(shape):
        rows = shape[0]
        return lax.broadcasted_iota(jnp.int32, shape, 0) + node * rows == targets[...]

    return paired


def image_pairs(targets, node, nodes):
    def paired(shape):
        rows = shape[0]
        columns = lax.broadcasted_iota(jnp.int32, shape, 1)
        names = jnp.where(columns < nodes * rows, columns, -1 - nodes * rows)
        for k in range(nodes):
            here = jnp.logical_and(columns >= k * rows, columns < (k + 1) * rows)
            shift = (lax.rem(node + k, nodes) - k) * rows
            names = jnp.where(here, columns + shift, names)
        return names == targets[...]

    return paired


def unit_kernel(lead, image, text, raw, half, inv, sems):
    rows = half.shape[0]
    part = rows // 2 if rows % 32 == 0 else rows
    pieces = [pl.ds(at, part) for at in range(0, rows, part)]

    def copies(source):
        return [
            pltpu.make_async_copy(source.at[piece], raw.at[piece], sems.at[i])
            for i, piece in enumerate(pieces)
        ]

    def fetch(source, node):
        for copy in copies(source):
            copy.start()

    sources = (text, image) if lead else (image, text)
    by_role(*[functools.partial(fetch, source) for source in sources])
    for piece, copy in zip(pieces, copies(image)):
        copy.wait()
        values = raw[piece, :].astype(FULL)
        inverse = lax.rsqrt(jnp.sum(values * values, axis=1, keepdims=True) + 1e-06)
        half[piece, :] = (values * inverse).astype(HALF)
        inv[piece, :] = inverse


def first_kernel(far, params, row_targets, lead, mate_rest, *refs):
    got1, got2, back = refs[:far], refs[far : 2 * far], refs[2 * far]

    def on_first(node):
        back[0] = drawn(params, got2[0], [lead, *got1]).astype(HALF)

    def on_second(node):
        for k in range(far):
            pairs = text_pairs(row_targets, lax.rem(node + k + 1, far + 1))
            images = [lead, mate_rest, got1[0]]
            back[k] = drawn(params, got2[k], images, pairs).astype(HALF)

    by_role(on_first, on_second)


def second_kernel(far, params, row_targets, rest, mate_lead, *refs):
    got1, got2, relay1 = refs[:far], refs[far : 2 * far], refs[2 * far : 3 * far]
    back = refs[3 * far]

    def on_first(node):
        for k in range(far):
            pairs = text_pairs(row_targets, lax.rem(node + k + 1, far + 1))
            images = [rest, got2[0], relay1[0]]
            back[k] = drawn(params, got1[k], images, pairs).astype(HALF)

    def on_second(node):
        back[0] = drawn(params, got1[0], [rest, *got2, mate_lead, *relay1]).astype(HALF)

    by_role(on_first, on_second)


def third_kernel(far, params, row_targets, targets, lead, rest, mate_rest, *refs):
    got1, got2 = refs[:far], refs[far : 2 * far]
    relay1, relay2 = refs[2 * far : 3 * far], refs[3 * far : 4 * far]
    lead_dir, rest_dir = refs[4 * far :]
    nodes = far + 1

    def on_first(node):
        pairs = image_pairs(targets, node, nodes)
        rest_dir[...] = drawn(params, rest, [lead, *got1, mate_rest, *relay2], pairs)
        pairs = text_pairs(row_targets, node)
        lead_dir[...] = drawn(params, lead, [rest, got2[0], relay1[0]], pairs)

    def on_second(node):
        pairs = text_pairs(row_targets, node)
        rest_dir[...] = drawn(params, rest, [lead, mate_rest, got1[0]], pairs)
        pairs = image_pairs(targets, node, nodes)
        lead_dir[...] = drawn(params, lead, [rest, *got2], pairs)

    by_role(on_first, on_second)


def tangent_kernel(far, sums_on_first, raw, inverse, direction, *refs):
    parts = refs[:far]
    image_grads, text_grads, held, sems = refs[-4:]
    rows = raw.shape[0]
    part = rows // 5 if rows % 80 == 0 else rows
    pieces = [pl.ds(at, part) for at in range(0, rows, part)]

    def run(out, count, node):
        copies = []
        for i, piece in enumerate(pieces):
            gradient = direction[piece, :]
            for k in range(count):
                gradient += parts[k][piece, :].astype(FULL)
            inv = inverse[piece, :]
            unit = raw[piece, :].astype(FULL) * inv
            along = jnp.sum(unit * gradient, axis=1, keepdims=True)
            held[piece, :] = (gradient - unit * along) * inv
            copy = pltpu.make_async_copy(held.at[piece], out.at[piece], sems.at[i])
            copy.start()
            copies.append(copy)
        for copy in copies:
            copy.wait()

    if sums_on_first:
        by_role(
            functools.partial(run, text_grads, far), functools.partial(run, image_grads, 1)
        )
    else:
        by_role(
            functools.partial(run, image_grads, 1), functools.partial(run, text_grads, far)
        )


def call(kernel, name, operands, shapes, anywhere=0, scratch=()):
    operands = list(operands)
    held = pl.BlockSpec(memory_space=pltpu.VMEM)
    for i in range(anywhere):
        operands[i] = pltpu.with_memory_space_constraint(operands[i], pltpu.HBM)
    return pl.pallas_call(
        kernel,
        name=name,
        out_shape=[pltpu.VMEM(s, d) for s, d in shapes],
        in_specs=[pl.BlockSpec(memory_space=pltpu.HBM)] * anywhere
        + [held] * (len(operands) - anywhere),
        out_specs=[held] * len(shapes),
        scratch_shapes=scratch,
        compiler_params=pltpu.CompilerParams(vmem_limit_bytes=VMEM_LIMIT),
    )(*operands)


def tangent(far, sums_on_first, operands, grads, block):
    rows = block[0][0]
    anywhere = pl.BlockSpec(memory_space=pl.ANY)
    count = len(operands)
    return pl.pallas_call(
        functools.partial(tangent_kernel, far, sums_on_first),
        name="tangent",
        out_shape=[jax.ShapeDtypeStruct(*block)] * 2,
        in_specs=[pl.BlockSpec(memory_space=pltpu.VMEM)] * count + [anywhere] * len(grads),
        out_specs=[anywhere] * 2,
        scratch_shapes=[pltpu.VMEM(*block), pltpu.SemaphoreType.DMA((5,))],
        input_output_aliases={count + i: i for i in range(len(grads))},
        compiler_params=pltpu.CompilerParams(vmem_limit_bytes=VMEM_LIMIT),
    )(*operands, *grads)


def local(image_embeds, text_embeds, pair_text, similarity_scale, logit_bias):
    rows, width = image_embeds.shape
    cycle_count = lax.axis_size("blk")
    node_count = lax.axis_size("node")
    far = node_count - 1
    cycle_index = lax.axis_index("blk")
    node_index = lax.axis_index("node")

    def send(block, even, odd):
        route = []
        for g in range(cycle_count):
            ahead, across = odd if g % 2 else even
            for n in range(node_count):
                to = (g + ahead) % cycle_count * node_count + (n + across) % node_count
                route.append((g * node_count + n, to))
        return lax.ppermute(block, ("blk", "node"), route)

    def swap(block):
        return send(block, (1, 0), (-1, 0))

    stay = (0, 0)
    ahead, behind = (2, 0), (-2, 0)
    block_h = ((rows, width), HALF)
    block_f = ((rows, width), FULL)
    column = ((rows, 1), FULL)
    returns = ((far, rows, width), HALF)

    def unit(lead, operands):
        return call(
            functools.partial(unit_kernel, lead),
            "unit",
            operands,
            [block_h, block_h, column],
            anywhere=2,
            scratch=[pltpu.SemaphoreType.DMA((2,))],
        )

    lead_raw, lead, lead_inv = unit(True, [image_embeds, text_embeds])
    got1 = [send(lead, (0, -k), ahead if k == 1 else stay) for k in range(1, node_count)]
    image, text, _ = lax.optimization_barrier((image_embeds, text_embeds, lead_inv))
    rest_raw, rest, rest_inv = unit(False, [image, text])
    got2 = [send(rest, ahead if k == 1 else stay, (0, -k)) for k in range(1, node_count)]
    mate_rest = swap(rest)
    mate_lead = swap(lead)

    start = (cycle_index * node_count + node_index) * rows
    targets = lax.dynamic_slice_in_dim(pair_text, start, rows, 0)
    targets = targets - cycle_index * node_count * rows
    row_targets = jnp.pad(targets, (0, 2 * rows), constant_values=-1)[None, :]
    targets = targets[:, None]

    params = jnp.concatenate([similarity_scale, logit_bias])[:, None]
    params = jnp.broadcast_to(params, (2, 128))
    *got1, row_targets, params = lax.optimization_barrier((*got1, row_targets, params))
    relay1 = [swap(block) for block in got1]
    relay2 = [swap(block) for block in got2]
    (back,) = call(
        functools.partial(first_kernel, far),
        "first",
        [params, row_targets, lead, mate_rest, *got1, *got2],
        [returns],
    )
    one = [send(back[k], behind if k == 0 else stay, (0, k + 1)) for k in range(far)]
    (back,) = call(
        functools.partial(second_kernel, far),
        "second",
        [params, row_targets, rest, mate_lead, *got1, *got2, *relay1],
        [returns],
    )
    two = [send(back[k], (0, k + 1), behind if k == 0 else stay) for k in range(far)]
    lead_dir, rest_dir = call(
        functools.partial(third_kernel, far),
        "third",
        [params, row_targets, targets, lead, rest, mate_rest]
        + [*got1, *got2, *relay1, *relay2],
        [block_f, block_f],
    )
    grads = tangent(far, False, [rest_raw, rest_inv, rest_dir, *one], [], block_f)
    return tuple(tangent(far, True, [lead_raw, lead_inv, lead_dir, *two], grads, block_f))


def solution(mesh):
    return jax.shard_map(
        local,
        mesh=mesh,
        in_specs=(P(("blk", "node"), None), P(("blk", "node"), None), P(), P(), P()),
        out_specs=(P(("blk", "node"), None), P(("blk", "node"), None)),
        check_vma=False,
    )
```

```python
import functools

import jax
import jax.numpy as jnp
from jax import lax
from jax.experimental import pallas as pl
from jax.experimental.pallas import tpu as pltpu
from jax.sharding import PartitionSpec as P

HALF = jnp.bfloat16
FULL = jnp.float32
VMEM_LIMIT = 8 * 1024 * 1024


def roles():
    return lax.rem(lax.axis_index("blk"), 2) == 0, lax.axis_index("node")


def by_role(on_first, on_second):
    first, node = roles()
    pl.when(first)(functools.partial(on_first, node))
    pl.when(jnp.logical_not(first))(functools.partial(on_second, node))


def drawn(params, rows, partners, paired=None):
    vectors = jnp.concatenate([partner[...] for partner in partners], axis=0)
    dots = lax.dot_general(
        rows[...], vectors, (((1,), (1,)), ((), ())), preferred_element_type=FULL
    )
    scale, bias = params[0:1, 0:1], params[1:2, 0:1]
    logits = scale * dots + bias
    if paired is None:
        weights = scale * jax.nn.sigmoid(logits)
    else:
        pairs = paired(logits.shape)
        weights = jnp.where(pairs, -scale, scale) * jax.nn.sigmoid(
            jnp.where(pairs, -logits, logits)
        )
    return jnp.dot(weights.astype(HALF), vectors, preferred_element_type=FULL)


def text_pairs(targets, node):
    def paired(shape):
        rows = shape[0]
        return lax.broadcasted_iota(jnp.int32, shape, 0) + node * rows == targets[...]

    return paired


def image_pairs(targets, node, nodes):
    def paired(shape):
        rows = shape[0]
        columns = lax.broadcasted_iota(jnp.int32, shape, 1)
        names = jnp.where(columns < nodes * rows, columns, -1 - nodes * rows)
        for k in range(nodes):
            here = jnp.logical_and(columns >= k * rows, columns < (k + 1) * rows)
            shift = (lax.rem(node + k, nodes) - k) * rows
            names = jnp.where(here, columns + shift, names)
        return names == targets[...]

    return paired


def unit_kernel(lead, image, text, raw, half, inv, sems):
    rows = half.shape[0]
    part = rows // 2 if rows % 32 == 0 else rows
    pieces = [pl.ds(at, part) for at in range(0, rows, part)]

    def copies(source):
        return [
            pltpu.make_async_copy(source.at[piece], raw.at[piece], sems.at[i])
            for i, piece in enumerate(pieces)
        ]

    def fetch(source, node):
        for copy in copies(source):
            copy.start()

    sources = (text, image) if lead else (image, text)
    by_role(*[functools.partial(fetch, source) for source in sources])
    for piece, copy in zip(pieces, copies(image)):
        copy.wait()
        values = raw[piece, :].astype(FULL)
        inverse = lax.rsqrt(jnp.sum(values * values, axis=1, keepdims=True) + 1e-06)
        half[piece, :] = (values * inverse).astype(HALF)
        inv[piece, :] = inverse


def first_kernel(far, params, row_targets, lead, mate_rest, *refs):
    got1, got2, back = refs[:far], refs[far : 2 * far], refs[2 * far]

    def on_first(node):
        back[0] = drawn(params, got2[0], [lead, *got1]).astype(HALF)

    def on_second(node):
        for k in range(far):
            pairs = text_pairs(row_targets, lax.rem(node + k + 1, far + 1))
            images = [lead, mate_rest, got1[0]]
            back[k] = drawn(params, got2[k], images, pairs).astype(HALF)

    by_role(on_first, on_second)


def second_kernel(far, params, row_targets, rest, mate_lead, *refs):
    got1, got2, relay1 = refs[:far], refs[far : 2 * far], refs[2 * far : 3 * far]
    back = refs[3 * far]

    def on_first(node):
        for k in range(far):
            pairs = text_pairs(row_targets, lax.rem(node + k + 1, far + 1))
            images = [rest, got2[0], relay1[0]]
            back[k] = drawn(params, got1[k], images, pairs).astype(HALF)

    def on_second(node):
        back[0] = drawn(params, got1[0], [rest, *got2, mate_lead, *relay1]).astype(HALF)

    by_role(on_first, on_second)


def third_kernel(far, params, row_targets, targets, lead, rest, mate_rest, *refs):
    got1, got2 = refs[:far], refs[far : 2 * far]
    relay1, relay2 = refs[2 * far : 3 * far], refs[3 * far : 4 * far]
    lead_dir, rest_dir = refs[4 * far :]
    nodes = far + 1

    def on_first(node):
        pairs = image_pairs(targets, node, nodes)
        rest_dir[...] = drawn(params, rest, [lead, *got1, mate_rest, *relay2], pairs)
        pairs = text_pairs(row_targets, node)
        lead_dir[...] = drawn(params, lead, [rest, got2[0], relay1[0]], pairs)

    def on_second(node):
        pairs = text_pairs(row_targets, node)
        rest_dir[...] = drawn(params, rest, [lead, mate_rest, got1[0]], pairs)
        pairs = image_pairs(targets, node, nodes)
        lead_dir[...] = drawn(params, lead, [rest, *got2], pairs)

    by_role(on_first, on_second)


def tangent_kernel(far, sums_on_first, raw, inverse, direction, *refs):
    parts = refs[:far]
    image_grads, text_grads, held, sems = refs[-4:]
    rows = raw.shape[0]
    part = rows // 5 if rows % 80 == 0 else rows
    pieces = [pl.ds(at, part) for at in range(0, rows, part)]

    def run(out, count, node):
        copies = []
        for i, piece in enumerate(pieces):
            gradient = direction[piece, :]
            for k in range(count):
                gradient += parts[k][piece, :].astype(FULL)
            inv = inverse[piece, :]
            unit = raw[piece, :].astype(FULL) * inv
            along = jnp.sum(unit * gradient, axis=1, keepdims=True)
            held[piece, :] = (gradient - unit * along) * inv
            copy = pltpu.make_async_copy(held.at[piece], out.at[piece], sems.at[i])
            copy.start()
            copies.append(copy)
        for copy in copies:
            copy.wait()

    if sums_on_first:
        by_role(
            functools.partial(run, text_grads, far), functools.partial(run, image_grads, 1)
        )
    else:
        by_role(
            functools.partial(run, image_grads, 1), functools.partial(run, text_grads, far)
        )


def call(kernel, name, operands, shapes, anywhere=0, scratch=()):
    operands = list(operands)
    held = pl.BlockSpec(memory_space=pltpu.VMEM)
    for i in range(anywhere):
        operands[i] = pltpu.with_memory_space_constraint(operands[i], pltpu.HBM)
    return pl.pallas_call(
        kernel,
        name=name,
        out_shape=[pltpu.VMEM(s, d) for s, d in shapes],
        in_specs=[pl.BlockSpec(memory_space=pltpu.HBM)] * anywhere
        + [held] * (len(operands) - anywhere),
        out_specs=[held] * len(shapes),
        scratch_shapes=scratch,
        compiler_params=pltpu.CompilerParams(vmem_limit_bytes=VMEM_LIMIT),
    )(*operands)


def tangent(far, sums_on_first, operands, grads, block):
    rows = block[0][0]
    anywhere = pl.BlockSpec(memory_space=pl.ANY)
    count = len(operands)
    return pl.pallas_call(
        functools.partial(tangent_kernel, far, sums_on_first),
        name="tangent",
        out_shape=[jax.ShapeDtypeStruct(*block)] * 2,
        in_specs=[pl.BlockSpec(memory_space=pltpu.VMEM)] * count + [anywhere] * len(grads),
        out_specs=[anywhere] * 2,
        scratch_shapes=[pltpu.VMEM(*block), pltpu.SemaphoreType.DMA((5,))],
        input_output_aliases={count + i: i for i in range(len(grads))},
        compiler_params=pltpu.CompilerParams(vmem_limit_bytes=VMEM_LIMIT),
    )(*operands, *grads)


def local(image_embeds, text_embeds, pair_text, similarity_scale, logit_bias):
    rows, width = image_embeds.shape
    cycle_count = lax.axis_size("blk")
    node_count = lax.axis_size("node")
    far = node_count - 1
    cycle_index = lax.axis_index("blk")
    node_index = lax.axis_index("node")

    def send(block, even, odd):
        route = []
        for g in range(cycle_count):
            ahead, across = odd if g % 2 else even
            for n in range(node_count):
                to = (g + ahead) % cycle_count * node_count + (n + across) % node_count
                route.append((g * node_count + n, to))
        return lax.ppermute(block, ("blk", "node"), route)

    def swap(block):
        return send(block, (1, 0), (-1, 0))

    stay = (0, 0)
    ahead, behind = (2, 0), (-2, 0)
    block_h = ((rows, width), HALF)
    block_f = ((rows, width), FULL)
    column = ((rows, 1), FULL)
    returns = ((far, rows, width), HALF)

    def unit(lead, operands):
        return call(
            functools.partial(unit_kernel, lead),
            "unit",
            operands,
            [block_h, block_h, column],
            anywhere=2,
            scratch=[pltpu.SemaphoreType.DMA((2,))],
        )

    lead_raw, lead, lead_inv = unit(True, [image_embeds, text_embeds])
    got1 = [send(lead, (0, -k), ahead if k == 1 else stay) for k in range(1, node_count)]
    image, text, _ = lax.optimization_barrier((image_embeds, text_embeds, lead_inv))
    rest_raw, rest, rest_inv = unit(False, [image, text])
    got2 = [send(rest, ahead if k == 1 else stay, (0, -k)) for k in range(1, node_count)]
    mate_rest = swap(rest)
    mate_lead = swap(lead)

    start = (cycle_index * node_count + node_index) * rows
    targets = lax.dynamic_slice_in_dim(pair_text, start, rows, 0)
    targets = targets - cycle_index * node_count * rows
    row_targets = jnp.pad(targets, (0, 2 * rows), constant_values=-1)[None, :]
    targets = targets[:, None]

    params = jnp.concatenate([similarity_scale, logit_bias])[:, None]
    params = jnp.broadcast_to(params, (2, 128))
    *got1, row_targets, params = lax.optimization_barrier((*got1, row_targets, params))
    relay1 = [swap(block) for block in got1]
    relay2 = [swap(block) for block in got2]
    (back,) = call(
        functools.partial(first_kernel, far),
        "first",
        [params, row_targets, lead, mate_rest, *got1, *got2],
        [returns],
    )
    one = [send(back[k], behind if k == 0 else stay, (0, k + 1)) for k in range(far)]
    (back,) = call(
        functools.partial(second_kernel, far),
        "second",
        [params, row_targets, rest, mate_lead, *got1, *got2, *relay1],
        [returns],
    )
    two = [send(back[k], (0, k + 1), behind if k == 0 else stay) for k in range(far)]
    lead_dir, rest_dir = call(
        functools.partial(third_kernel, far),
        "third",
        [params, row_targets, targets, lead, rest, mate_rest]
        + [*got1, *got2, *relay1, *relay2],
        [block_f, block_f],
    )
    grads = tangent(far, False, [rest_raw, rest_inv, rest_dir, *one], [], block_f)
    return tuple(tangent(far, True, [lead_raw, lead_inv, lead_dir, *two], grads, block_f))


def solution(mesh):
    return jax.shard_map(
        local,
        mesh=mesh,
        in_specs=(P(("blk", "node"), None), P(("blk", "node"), None), P(), P(), P()),
        out_specs=(P(("blk", "node"), None), P(("blk", "node"), None)),
        check_vma=False,
    )
```

```python
import functools

import jax
import jax.numpy as jnp
from jax import lax
from jax.experimental import pallas as pl
from jax.experimental.pallas import tpu as pltpu
from jax.sharding import PartitionSpec as P

HALF = jnp.bfloat16
FULL = jnp.float32
VMEM_LIMIT = 8 * 1024 * 1024


def roles():
    return lax.rem(lax.axis_index("blk"), 2) == 0, lax.axis_index("node")


def by_role(on_first, on_second):
    first, node = roles()
    pl.when(first)(functools.partial(on_first, node))
    pl.when(jnp.logical_not(first))(functools.partial(on_second, node))


def drawn(params, rows, partners, paired=None):
    vectors = jnp.concatenate([partner[...] for partner in partners], axis=0)
    dots = lax.dot_general(
        rows[...], vectors, (((1,), (1,)), ((), ())), preferred_element_type=FULL
    )
    scale, bias = params[0:1, 0:1], params[1:2, 0:1]
    logits = scale * dots + bias
    if paired is None:
        weights = scale * jax.nn.sigmoid(logits)
    else:
        pairs = paired(logits.shape)
        weights = jnp.where(pairs, -scale, scale) * jax.nn.sigmoid(
            jnp.where(pairs, -logits, logits)
        )
    return jnp.dot(weights.astype(HALF), vectors, preferred_element_type=FULL)


def text_pairs(targets, node):
    def paired(shape):
        rows = shape[0]
        return lax.broadcasted_iota(jnp.int32, shape, 0) + node * rows == targets[...]

    return paired


def image_pairs(targets, node, nodes):
    def paired(shape):
        rows = shape[0]
        columns = lax.broadcasted_iota(jnp.int32, shape, 1)
        names = jnp.where(columns < nodes * rows, columns, -1 - nodes * rows)
        for k in range(nodes):
            here = jnp.logical_and(columns >= k * rows, columns < (k + 1) * rows)
            shift = (lax.rem(node + k, nodes) - k) * rows
            names = jnp.where(here, columns + shift, names)
        return names == targets[...]

    return paired


def unit_kernel(image, text, lead_raw, rest_raw, lead, rest, lead_inv, rest_inv, sems):
    rows = lead.shape[0]
    part = rows // 2 if rows % 32 == 0 else rows
    pieces = [pl.ds(at, part) for at in range(0, rows, part)]

    def copies(source, target, base):
        return [
            pltpu.make_async_copy(source.at[piece], target.at[piece], sems.at[base + i])
            for i, piece in enumerate(pieces)
        ]

    def fetch(lead_source, rest_source, node):
        for copy in copies(lead_source, lead_raw, 0) + copies(rest_source, rest_raw, 2):
            copy.start()

    by_role(functools.partial(fetch, text, image), functools.partial(fetch, image, text))
    for base, raw, half, inv in ((0, lead_raw, lead, lead_inv), (2, rest_raw, rest, rest_inv)):
        for piece, copy in zip(pieces, copies(image, raw, base)):
            copy.wait()
            values = raw[piece, :].astype(FULL)
            inverse = lax.rsqrt(jnp.sum(values * values, axis=1, keepdims=True) + 1e-06)
            half[piece, :] = (values * inverse).astype(HALF)
            inv[piece, :] = inverse


def first_kernel(far, params, row_targets, lead, mate_rest, *refs):
    got1, got2, back = refs[:far], refs[far : 2 * far], refs[2 * far]
    refs[-1][...] = jnp.zeros(refs[-1].shape, FULL)

    def on_first(node):
        back[0] = drawn(params, got2[0], [lead, *got1]).astype(HALF)

    def on_second(node):
        for k in range(far):
            pairs = text_pairs(row_targets, lax.rem(node + k + 1, far + 1))
            images = [lead, mate_rest, got1[0]]
            back[k] = drawn(params, got2[k], images, pairs).astype(HALF)

    by_role(on_first, on_second)


def second_kernel(far, params, row_targets, rest, mate_lead, *refs):
    got1, got2, relay1 = refs[:far], refs[far : 2 * far], refs[2 * far : 3 * far]
    back = refs[3 * far]
    refs[-1][...] = jnp.zeros(refs[-1].shape, FULL)

    def on_first(node):
        for k in range(far):
            pairs = text_pairs(row_targets, lax.rem(node + k + 1, far + 1))
            images = [rest, got2[0], relay1[0]]
            back[k] = drawn(params, got1[k], images, pairs).astype(HALF)

    def on_second(node):
        back[0] = drawn(params, got1[0], [rest, *got2, mate_lead, *relay1]).astype(HALF)

    by_role(on_first, on_second)


def third_kernel(far, params, row_targets, targets, lead, rest, mate_rest, *refs):
    got1, got2 = refs[:far], refs[far : 2 * far]
    relay1, relay2 = refs[2 * far : 3 * far], refs[3 * far : 4 * far]
    lead_dir, rest_dir = refs[4 * far :]
    nodes = far + 1

    def on_first(node):
        pairs = image_pairs(targets, node, nodes)
        rest_dir[...] = drawn(params, rest, [lead, *got1, mate_rest, *relay2], pairs)
        pairs = text_pairs(row_targets, node)
        lead_dir[...] = drawn(params, lead, [rest, got2[0], relay1[0]], pairs)

    def on_second(node):
        pairs = text_pairs(row_targets, node)
        rest_dir[...] = drawn(params, rest, [lead, mate_rest, got1[0]], pairs)
        pairs = image_pairs(targets, node, nodes)
        lead_dir[...] = drawn(params, lead, [rest, *got2], pairs)

    by_role(on_first, on_second)


def tangent_kernel(far, sums_on_first, raw, inverse, direction, *refs):
    parts = refs[:far]
    image_grads, text_grads, held, sems = refs[-4:]
    rows = raw.shape[0]
    part = rows // 5 if rows % 80 == 0 else rows
    pieces = [pl.ds(at, part) for at in range(0, rows, part)]

    def run(out, count, node):
        copies = []
        for i, piece in enumerate(pieces):
            gradient = direction[piece, :]
            for k in range(count):
                gradient += parts[k][piece, :].astype(FULL)
            inv = inverse[piece, :]
            unit = raw[piece, :].astype(FULL) * inv
            along = jnp.sum(unit * gradient, axis=1, keepdims=True)
            held[piece, :] = (gradient - unit * along) * inv
            copy = pltpu.make_async_copy(held.at[piece], out.at[piece], sems.at[i])
            copy.start()
            copies.append(copy)
        for copy in copies:
            copy.wait()

    if sums_on_first:
        by_role(
            functools.partial(run, text_grads, far), functools.partial(run, image_grads, 1)
        )
    else:
        by_role(
            functools.partial(run, image_grads, 1), functools.partial(run, text_grads, far)
        )


def call(kernel, name, operands, shapes, anywhere=0, scratch=()):
    operands = list(operands)
    held = pl.BlockSpec(memory_space=pltpu.VMEM)
    for i in range(anywhere):
        operands[i] = pltpu.with_memory_space_constraint(operands[i], pltpu.HBM)
    return pl.pallas_call(
        kernel,
        name=name,
        out_shape=[pltpu.VMEM(s, d) for s, d in shapes],
        in_specs=[pl.BlockSpec(memory_space=pltpu.HBM)] * anywhere
        + [held] * (len(operands) - anywhere),
        out_specs=[held] * len(shapes),
        scratch_shapes=scratch,
        compiler_params=pltpu.CompilerParams(vmem_limit_bytes=VMEM_LIMIT),
    )(*operands)


def tangent(far, sums_on_first, operands, grads, block):
    rows = block[0][0]
    anywhere = pl.BlockSpec(memory_space=pl.ANY)
    count = len(operands)
    return pl.pallas_call(
        functools.partial(tangent_kernel, far, sums_on_first),
        name="tangent",
        out_shape=[jax.ShapeDtypeStruct(*block)] * 2,
        in_specs=[pl.BlockSpec(memory_space=pltpu.VMEM)] * count + [anywhere] * len(grads),
        out_specs=[anywhere] * 2,
        scratch_shapes=[pltpu.VMEM(*block), pltpu.SemaphoreType.DMA((5,))],
        input_output_aliases={count + i: i for i in range(len(grads))},
        compiler_params=pltpu.CompilerParams(vmem_limit_bytes=VMEM_LIMIT),
    )(*operands, *grads)


def local(image_embeds, text_embeds, pair_text, similarity_scale, logit_bias):
    rows, width = image_embeds.shape
    cycle_count = lax.axis_size("blk")
    node_count = lax.axis_size("node")
    far = node_count - 1
    cycle_index = lax.axis_index("blk")
    node_index = lax.axis_index("node")

    def send(block, even, odd):
        route = []
        for g in range(cycle_count):
            ahead, across = odd if g % 2 else even
            for n in range(node_count):
                to = (g + ahead) % cycle_count * node_count + (n + across) % node_count
                route.append((g * node_count + n, to))
        return lax.ppermute(block, ("blk", "node"), route)

    def swap(block):
        return send(block, (1, 0), (-1, 0))

    stay = (0, 0)
    ahead, behind = (2, 0), (-2, 0)
    block_h = ((rows, width), HALF)
    block_f = ((rows, width), FULL)
    column = ((rows, 1), FULL)
    returns = ((far, rows, width), HALF)

    lead_raw, rest_raw, lead, rest, lead_inv, rest_inv = call(
        unit_kernel,
        "unit",
        [image_embeds, text_embeds],
        [block_h, block_h, block_h, block_h, column, column],
        anywhere=2,
        scratch=[pltpu.SemaphoreType.DMA((4,))],
    )
    got1 = [send(lead, (0, -k), ahead if k == 1 else stay) for k in range(1, node_count)]
    got2 = [send(rest, ahead if k == 1 else stay, (0, -k)) for k in range(1, node_count)]
    mate_rest = swap(rest)
    mate_lead = swap(lead)

    start = (cycle_index * node_count + node_index) * rows
    targets = lax.dynamic_slice_in_dim(pair_text, start, rows, 0)
    targets = targets - cycle_index * node_count * rows
    row_targets = jnp.pad(targets, (0, 2 * rows), constant_values=-1)[None, :]
    targets = targets[:, None]

    params = jnp.concatenate([similarity_scale, logit_bias])[:, None]
    params = jnp.broadcast_to(params, (2, 128))
    *got1, row_targets, params = lax.optimization_barrier((*got1, row_targets, params))
    relay1 = [swap(block) for block in got1]
    relay2 = [swap(block) for block in got2]
    back, _ = call(
        functools.partial(first_kernel, far),
        "first",
        [params, row_targets, lead, mate_rest, *got1, *got2],
        [returns, ((8, 128), FULL)],
    )
    one = [send(back[k], behind if k == 0 else stay, (0, k + 1)) for k in range(far)]
    back, _ = call(
        functools.partial(second_kernel, far),
        "second",
        [params, row_targets, rest, mate_lead, *got1, *got2, *relay1],
        [returns, ((8, 128), FULL)],
    )
    two = [send(back[k], (0, k + 1), behind if k == 0 else stay) for k in range(far)]
    lead_dir, rest_dir = call(
        functools.partial(third_kernel, far),
        "third",
        [params, row_targets, targets, lead, rest, mate_rest]
        + [*got1, *got2, *relay1, *relay2],
        [block_f, block_f],
    )
    grads = tangent(far, False, [rest_raw, rest_inv, rest_dir, *one], [], block_f)
    return tuple(tangent(far, True, [lead_raw, lead_inv, lead_dir, *two], grads, block_f))


def solution(mesh):
    return jax.shard_map(
        local,
        mesh=mesh,
        in_specs=(P(("blk", "node"), None), P(("blk", "node"), None), P(), P(), P()),
        out_specs=(P(("blk", "node"), None), P(("blk", "node"), None)),
        check_vma=False,
    )
```

```python
import functools
import math

import jax
import jax.numpy as jnp
from jax import lax
from jax.experimental import pallas as pl
from jax.experimental.pallas import tpu as pltpu
from jax.sharding import PartitionSpec as P

HALF = jnp.bfloat16
FULL = jnp.float32
VMEM_LIMIT = 8 * 1024 * 1024


def roles():
    return lax.rem(lax.axis_index("blk"), 2) == 0, lax.axis_index("node")


def by_role(on_first, on_second):
    first, node = roles()
    pl.when(first)(functools.partial(on_first, node))
    pl.when(jnp.logical_not(first))(functools.partial(on_second, node))


def drawn(params, rows, partners, paired=None):
    vectors = jnp.concatenate([partner[...] for partner in partners], axis=0)
    dots = lax.dot_general(
        rows[...], vectors, (((1,), (1,)), ((), ())), preferred_element_type=FULL
    )
    scale, bias = params[0:1, 0:1], params[1:2, 0:1]
    logits = scale * dots + bias
    if paired is None:
        weights = scale * jax.nn.sigmoid(logits)
    else:
        pairs = paired(logits.shape)
        weights = jnp.where(pairs, -scale, scale) * jax.nn.sigmoid(
            jnp.where(pairs, -logits, logits)
        )
    return jnp.dot(weights.astype(HALF), vectors, preferred_element_type=FULL)


def text_pairs(targets, node):
    def paired(shape):
        rows = shape[0]
        return lax.broadcasted_iota(jnp.int32, shape, 0) + node * rows == targets[...]

    return paired


def image_pairs(targets, node, nodes):
    def paired(shape):
        rows = shape[0]
        columns = lax.broadcasted_iota(jnp.int32, shape, 1)
        names = jnp.where(columns < nodes * rows, columns, -1 - nodes * rows)
        for k in range(nodes):
            here = jnp.logical_and(columns >= k * rows, columns < (k + 1) * rows)
            shift = (lax.rem(node + k, nodes) - k) * rows
            names = jnp.where(here, columns + shift, names)
        return names == targets[...]

    return paired


def unit_kernel(image, text, lead_raw, rest_raw, lead, rest, lead_inv, rest_inv, sems):
    rows = lead.shape[0]
    part = rows // 2 if rows % 32 == 0 else rows
    pieces = [pl.ds(at, part) for at in range(0, rows, part)]

    def copies(source, target, base):
        return [
            pltpu.make_async_copy(source.at[piece], target.at[piece], sems.at[base + i])
            for i, piece in enumerate(pieces)
        ]

    def fetch(lead_source, rest_source, node):
        for copy in copies(lead_source, lead_raw, 0) + copies(rest_source, rest_raw, 2):
            copy.start()

    by_role(functools.partial(fetch, text, image), functools.partial(fetch, image, text))
    for base, raw, half, inv in ((0, lead_raw, lead, lead_inv), (2, rest_raw, rest, rest_inv)):
        for piece, copy in zip(pieces, copies(image, raw, base)):
            copy.wait()
            values = raw[piece, :].astype(FULL)
            inverse = lax.rsqrt(jnp.sum(values * values, axis=1, keepdims=True) + 1e-06)
            half[piece, :] = (values * inverse).astype(HALF)
            inv[piece, :] = inverse


def prep_kernel(
    names, scale, bias, after, params, row_targets, targets, held, sems
):
    copy = pltpu.make_async_copy(names, held, sems.at[0])
    copy.start()
    row = lax.broadcasted_iota(jnp.int32, params.shape, 0)
    params[...] = jnp.where(row == 0, scale[...], bias[...])
    copy.wait()

    rows = targets.shape[0]
    group, node = lax.axis_index("blk"), lax.axis_index("node")
    nodes = lax.axis_size("node")
    start = (group * nodes + node) * rows
    step = math.gcd(rows, 128)
    lines = -(-(128 - step + rows) // 128)
    window = held[pl.ds(start // 128, lines), :]
    window = jnp.concatenate([window[i : i + 1] for i in range(lines)], axis=1)
    mine = window[:, :rows]
    for at in range(step, 128, step):
        mine = jnp.where(lax.rem(start, 128) == at, window[:, at : at + rows], mine)
    mine = mine - group * nodes * rows
    row_targets[...] = jnp.full(row_targets.shape, -1, jnp.int32)
    row_targets[:, :rows] = mine
    square = (rows, rows)
    same = lax.broadcasted_iota(jnp.int32, square, 0) == lax.broadcasted_iota(
        jnp.int32, square, 1
    )
    turned = jnp.sum(jnp.where(same, mine.astype(FULL), 0.0), axis=1, keepdims=True)
    targets[...] = turned.astype(jnp.int32)


def first_kernel(far, params, row_targets, lead, mate_rest, *refs):
    got1, got2, back = refs[:far], refs[far : 2 * far], refs[2 * far]

    def on_first(node):
        back[0] = drawn(params, got2[0], [lead, *got1]).astype(HALF)

    def on_second(node):
        for k in range(far):
            pairs = text_pairs(row_targets, lax.rem(node + k + 1, far + 1))
            images = [lead, mate_rest, got1[0]]
            back[k] = drawn(params, got2[k], images, pairs).astype(HALF)

    by_role(on_first, on_second)


def second_kernel(far, params, row_targets, rest, mate_lead, *refs):
    got1, got2, relay1 = refs[:far], refs[far : 2 * far], refs[2 * far : 3 * far]
    back = refs[3 * far]

    def on_first(node):
        for k in range(far):
            pairs = text_pairs(row_targets, lax.rem(node + k + 1, far + 1))
            images = [rest, got2[0], relay1[0]]
            back[k] = drawn(params, got1[k], images, pairs).astype(HALF)

    def on_second(node):
        back[0] = drawn(params, got1[0], [rest, *got2, mate_lead, *relay1]).astype(HALF)

    by_role(on_first, on_second)


def third_kernel(far, params, row_targets, targets, lead, rest, mate_rest, *refs):
    got1, got2 = refs[:far], refs[far : 2 * far]
    relay1, relay2 = refs[2 * far : 3 * far], refs[3 * far : 4 * far]
    lead_dir, rest_dir = refs[4 * far :]
    nodes = far + 1

    def on_first(node):
        pairs = image_pairs(targets, node, nodes)
        rest_dir[...] = drawn(params, rest, [lead, *got1, mate_rest, *relay2], pairs)
        pairs = text_pairs(row_targets, node)
        lead_dir[...] = drawn(params, lead, [rest, got2[0], relay1[0]], pairs)

    def on_second(node):
        pairs = text_pairs(row_targets, node)
        rest_dir[...] = drawn(params, rest, [lead, mate_rest, got1[0]], pairs)
        pairs = image_pairs(targets, node, nodes)
        lead_dir[...] = drawn(params, lead, [rest, *got2], pairs)

    by_role(on_first, on_second)


def tangent_kernel(far, sums_on_first, raw, inverse, direction, *refs):
    parts = refs[:far]
    image_grads, text_grads, held, sems = refs[-4:]
    rows = raw.shape[0]
    part = rows // 5 if rows % 80 == 0 else rows
    pieces = [pl.ds(at, part) for at in range(0, rows, part)]

    def run(out, count, node):
        copies = []
        for i, piece in enumerate(pieces):
            gradient = direction[piece, :]
            for k in range(count):
                gradient += parts[k][piece, :].astype(FULL)
            inv = inverse[piece, :]
            unit = raw[piece, :].astype(FULL) * inv
            along = jnp.sum(unit * gradient, axis=1, keepdims=True)
            held[piece, :] = (gradient - unit * along) * inv
            copy = pltpu.make_async_copy(held.at[piece], out.at[piece], sems.at[i])
            copy.start()
            copies.append(copy)
        for copy in copies:
            copy.wait()

    if sums_on_first:
        by_role(
            functools.partial(run, text_grads, far), functools.partial(run, image_grads, 1)
        )
    else:
        by_role(
            functools.partial(run, image_grads, 1), functools.partial(run, text_grads, far)
        )


def call(kernel, name, operands, shapes, anywhere=0, scratch=()):
    operands = list(operands)
    held = pl.BlockSpec(memory_space=pltpu.VMEM)
    for i in range(anywhere):
        operands[i] = pltpu.with_memory_space_constraint(operands[i], pltpu.HBM)
    return pl.pallas_call(
        kernel,
        name=name,
        out_shape=[pltpu.VMEM(s, d) for s, d in shapes],
        in_specs=[pl.BlockSpec(memory_space=pltpu.HBM)] * anywhere
        + [held] * (len(operands) - anywhere),
        out_specs=[held] * len(shapes),
        scratch_shapes=scratch,
        compiler_params=pltpu.CompilerParams(vmem_limit_bytes=VMEM_LIMIT),
    )(*operands)


def tangent(far, sums_on_first, operands, grads, block):
    rows = block[0][0]
    anywhere = pl.BlockSpec(memory_space=pl.ANY)
    count = len(operands)
    return pl.pallas_call(
        functools.partial(tangent_kernel, far, sums_on_first),
        name="tangent",
        out_shape=[jax.ShapeDtypeStruct(*block)] * 2,
        in_specs=[pl.BlockSpec(memory_space=pltpu.VMEM)] * count + [anywhere] * len(grads),
        out_specs=[anywhere] * 2,
        scratch_shapes=[pltpu.VMEM(*block), pltpu.SemaphoreType.DMA((5,))],
        input_output_aliases={count + i: i for i in range(len(grads))},
        compiler_params=pltpu.CompilerParams(vmem_limit_bytes=VMEM_LIMIT),
    )(*operands, *grads)


def local(image_embeds, text_embeds, pair_text, similarity_scale, logit_bias):
    rows, width = image_embeds.shape
    cycle_count = lax.axis_size("blk")
    node_count = lax.axis_size("node")
    far = node_count - 1

    def send(block, even, odd):
        route = []
        for g in range(cycle_count):
            ahead, across = odd if g % 2 else even
            for n in range(node_count):
                to = (g + ahead) % cycle_count * node_count + (n + across) % node_count
                route.append((g * node_count + n, to))
        return lax.ppermute(block, ("blk", "node"), route)

    def swap(block):
        return send(block, (1, 0), (-1, 0))

    stay = (0, 0)
    ahead, behind = (2, 0), (-2, 0)
    block_h = ((rows, width), HALF)
    block_f = ((rows, width), FULL)
    column = ((rows, 1), FULL)
    returns = ((far, rows, width), HALF)

    lead_raw, rest_raw, lead, rest, lead_inv, rest_inv = call(
        unit_kernel,
        "unit",
        [image_embeds, text_embeds],
        [block_h, block_h, block_h, block_h, column, column],
        anywhere=2,
        scratch=[pltpu.SemaphoreType.DMA((4,))],
    )
    got1 = [send(lead, (0, -k), ahead if k == 1 else stay) for k in range(1, node_count)]
    got2 = [send(rest, ahead if k == 1 else stay, (0, -k)) for k in range(1, node_count)]
    mate_rest = swap(rest)
    mate_lead = swap(lead)

    names = pair_text.reshape(-1, 128)
    params, row_targets, targets = call(
        prep_kernel,
        "prep",
        [names, similarity_scale[:, None], logit_bias[:, None], rest_inv],
        [((8, 128), FULL), ((1, 3 * rows), jnp.int32), ((rows, 1), jnp.int32)],
        anywhere=1,
        scratch=[pltpu.VMEM(names.shape, jnp.int32), pltpu.SemaphoreType.DMA((1,))],
    )
    *got1, row_targets, params = lax.optimization_barrier((*got1, row_targets, params))
    relay1 = [swap(block) for block in got1]
    relay2 = [swap(block) for block in got2]
    (back,) = call(
        functools.partial(first_kernel, far),
        "first",
        [params, row_targets, lead, mate_rest, *got1, *got2],
        [returns],
    )
    one = [send(back[k], behind if k == 0 else stay, (0, k + 1)) for k in range(far)]
    (back,) = call(
        functools.partial(second_kernel, far),
        "second",
        [params, row_targets, rest, mate_lead, *got1, *got2, *relay1],
        [returns],
    )
    two = [send(back[k], (0, k + 1), behind if k == 0 else stay) for k in range(far)]
    lead_dir, rest_dir = call(
        functools.partial(third_kernel, far),
        "third",
        [params, row_targets, targets, lead, rest, mate_rest]
        + [*got1, *got2, *relay1, *relay2],
        [block_f, block_f],
    )
    grads = tangent(far, False, [rest_raw, rest_inv, rest_dir, *one], [], block_f)
    return tuple(tangent(far, True, [lead_raw, lead_inv, lead_dir, *two], grads, block_f))


def solution(mesh):
    return jax.shard_map(
        local,
        mesh=mesh,
        in_specs=(P(("blk", "node"), None), P(("blk", "node"), None), P(), P(), P()),
        out_specs=(P(("blk", "node"), None), P(("blk", "node"), None)),
        check_vma=False,
    )
```

```python
import functools
import math

import jax
import jax.numpy as jnp
from jax import lax
from jax.experimental import pallas as pl
from jax.experimental.pallas import tpu as pltpu
from jax.sharding import PartitionSpec as P

HALF = jnp.bfloat16
FULL = jnp.float32
VMEM_LIMIT = 8 * 1024 * 1024


def roles():
    return lax.rem(lax.axis_index("blk"), 2) == 0, lax.axis_index("node")


def by_role(on_first, on_second):
    first, node = roles()
    pl.when(first)(functools.partial(on_first, node))
    pl.when(jnp.logical_not(first))(functools.partial(on_second, node))


def drawn(params, rows, partners, paired=None):
    vectors = jnp.concatenate([partner[...] for partner in partners], axis=0)
    dots = lax.dot_general(
        rows[...], vectors, (((1,), (1,)), ((), ())), preferred_element_type=FULL
    )
    scale, bias = params[0:1, 0:1], params[1:2, 0:1]
    logits = scale * dots + bias
    if paired is None:
        weights = scale * jax.nn.sigmoid(logits)
    else:
        pairs = paired(logits.shape)
        weights = jnp.where(pairs, -scale, scale) * jax.nn.sigmoid(
            jnp.where(pairs, -logits, logits)
        )
    return jnp.dot(weights.astype(HALF), vectors, preferred_element_type=FULL)


def text_pairs(targets, node):
    def paired(shape):
        rows = shape[0]
        return lax.broadcasted_iota(jnp.int32, shape, 0) + node * rows == targets[...]

    return paired


def image_pairs(targets, node, nodes):
    def paired(shape):
        rows = shape[0]
        columns = lax.broadcasted_iota(jnp.int32, shape, 1)
        names = jnp.where(columns < nodes * rows, columns, -1 - nodes * rows)
        for k in range(nodes):
            here = jnp.logical_and(columns >= k * rows, columns < (k + 1) * rows)
            shift = (lax.rem(node + k, nodes) - k) * rows
            names = jnp.where(here, columns + shift, names)
        return names == targets[...]

    return paired


def unit_kernel(image, text, lead_raw, rest_raw, lead, rest, lead_inv, rest_inv, sems):
    rows = lead.shape[0]
    part = rows // 2 if rows % 32 == 0 else rows
    pieces = [pl.ds(at, part) for at in range(0, rows, part)]

    def copies(source, target, base):
        return [
            pltpu.make_async_copy(source.at[piece], target.at[piece], sems.at[base + i])
            for i, piece in enumerate(pieces)
        ]

    def fetch(lead_source, rest_source, node):
        for copy in copies(lead_source, lead_raw, 0) + copies(rest_source, rest_raw, 2):
            copy.start()

    by_role(functools.partial(fetch, text, image), functools.partial(fetch, image, text))
    for base, raw, half, inv in ((0, lead_raw, lead, lead_inv), (2, rest_raw, rest, rest_inv)):
        for piece, copy in zip(pieces, copies(image, raw, base)):
            copy.wait()
            values = raw[piece, :].astype(FULL)
            inverse = lax.rsqrt(jnp.sum(values * values, axis=1, keepdims=True) + 1e-06)
            half[piece, :] = (values * inverse).astype(HALF)
            inv[piece, :] = inverse


def prep_kernel(
    names, scale, bias, after, params, row_targets, targets, held, sems
):
    copy = pltpu.make_async_copy(names, held, sems.at[0])
    copy.start()
    row = lax.broadcasted_iota(jnp.int32, params.shape, 0)
    params[...] = jnp.where(row == 0, scale[...], bias[...])
    copy.wait()

    rows = targets.shape[0]
    group, node = lax.axis_index("blk"), lax.axis_index("node")
    nodes = lax.axis_size("node")
    start = (group * nodes + node) * rows
    step = math.gcd(rows, 128)
    lines = -(-(128 - step + rows) // 128)
    window = held[pl.ds(start // 128, lines), :]
    window = jnp.concatenate([window[i : i + 1] for i in range(lines)], axis=1)
    mine = window[:, :rows]
    for at in range(step, 128, step):
        mine = jnp.where(lax.rem(start, 128) == at, window[:, at : at + rows], mine)
    mine = mine - group * nodes * rows
    row_targets[...] = jnp.full(row_targets.shape, -1, jnp.int32)
    row_targets[:, :rows] = mine
    square = (rows, rows)
    same = lax.broadcasted_iota(jnp.int32, square, 0) == lax.broadcasted_iota(
        jnp.int32, square, 1
    )
    turned = jnp.sum(jnp.where(same, mine.astype(FULL), 0.0), axis=1, keepdims=True)
    targets[...] = turned.astype(jnp.int32)


def first_kernel(far, params, row_targets, lead, mate_rest, *refs):
    got1, got2, back = refs[:far], refs[far : 2 * far], refs[2 * far]

    def on_first(node):
        back[0] = drawn(params, got2[0], [lead, *got1]).astype(HALF)

    def on_second(node):
        for k in range(far):
            pairs = text_pairs(row_targets, lax.rem(node + k + 1, far + 1))
            images = [lead, mate_rest, got1[0]]
            back[k] = drawn(params, got2[k], images, pairs).astype(HALF)

    by_role(on_first, on_second)


def second_kernel(far, params, row_targets, rest, mate_lead, *refs):
    got1, got2, relay1 = refs[:far], refs[far : 2 * far], refs[2 * far : 3 * far]
    back = refs[3 * far]

    def on_first(node):
        for k in range(far):
            pairs = text_pairs(row_targets, lax.rem(node + k + 1, far + 1))
            images = [rest, got2[0], relay1[0]]
            back[k] = drawn(params, got1[k], images, pairs).astype(HALF)

    def on_second(node):
        back[0] = drawn(params, got1[0], [rest, *got2, mate_lead, *relay1]).astype(HALF)

    by_role(on_first, on_second)


def third_kernel(far, params, row_targets, targets, lead, rest, mate_rest, *refs):
    got1, got2 = refs[:far], refs[far : 2 * far]
    relay1, relay2 = refs[2 * far : 3 * far], refs[3 * far : 4 * far]
    lead_dir, rest_dir = refs[4 * far :]
    nodes = far + 1

    def on_first(node):
        pairs = image_pairs(targets, node, nodes)
        rest_dir[...] = drawn(params, rest, [lead, *got1, mate_rest, *relay2], pairs)
        pairs = text_pairs(row_targets, node)
        lead_dir[...] = drawn(params, lead, [rest, got2[0], relay1[0]], pairs)

    def on_second(node):
        pairs = text_pairs(row_targets, node)
        rest_dir[...] = drawn(params, rest, [lead, mate_rest, got1[0]], pairs)
        pairs = image_pairs(targets, node, nodes)
        lead_dir[...] = drawn(params, lead, [rest, *got2], pairs)

    by_role(on_first, on_second)


def tangent_kernel(far, sums_on_first, raw, inverse, direction, *refs):
    parts = refs[:far]
    image_grads, text_grads, held, sems = refs[-4:]
    rows = raw.shape[0]
    part = rows // 2 if rows % 32 == 0 else rows
    pieces = [pl.ds(at, part) for at in range(0, rows, part)]

    def run(out, count, node):
        copies = []
        for i, piece in enumerate(pieces):
            gradient = direction[piece, :]
            for k in range(count):
                gradient += parts[k][piece, :].astype(FULL)
            inv = inverse[piece, :]
            unit = raw[piece, :].astype(FULL) * inv
            along = jnp.sum(unit * gradient, axis=1, keepdims=True)
            held[piece, :] = (gradient - unit * along) * inv
            copy = pltpu.make_async_copy(held.at[piece], out.at[piece], sems.at[i])
            copy.start()
            copies.append(copy)
        for copy in copies:
            copy.wait()

    if sums_on_first:
        by_role(
            functools.partial(run, text_grads, far), functools.partial(run, image_grads, 1)
        )
    else:
        by_role(
            functools.partial(run, image_grads, 1), functools.partial(run, text_grads, far)
        )


def call(kernel, name, operands, shapes, anywhere=0, scratch=()):
    operands = list(operands)
    held = pl.BlockSpec(memory_space=pltpu.VMEM)
    for i in range(anywhere):
        operands[i] = pltpu.with_memory_space_constraint(operands[i], pltpu.HBM)
    return pl.pallas_call(
        kernel,
        name=name,
        out_shape=[pltpu.VMEM(s, d) for s, d in shapes],
        in_specs=[pl.BlockSpec(memory_space=pltpu.HBM)] * anywhere
        + [held] * (len(operands) - anywhere),
        out_specs=[held] * len(shapes),
        scratch_shapes=scratch,
        compiler_params=pltpu.CompilerParams(vmem_limit_bytes=VMEM_LIMIT),
    )(*operands)


def tangent(far, sums_on_first, operands, grads, block):
    rows = block[0][0]
    anywhere = pl.BlockSpec(memory_space=pl.ANY)
    count = len(operands)
    return pl.pallas_call(
        functools.partial(tangent_kernel, far, sums_on_first),
        name="tangent",
        out_shape=[jax.ShapeDtypeStruct(*block)] * 2,
        in_specs=[pl.BlockSpec(memory_space=pltpu.VMEM)] * count + [anywhere] * len(grads),
        out_specs=[anywhere] * 2,
        scratch_shapes=[pltpu.VMEM(*block), pltpu.SemaphoreType.DMA((2,))],
        input_output_aliases={count + i: i for i in range(len(grads))},
        compiler_params=pltpu.CompilerParams(vmem_limit_bytes=VMEM_LIMIT),
    )(*operands, *grads)


def local(image_embeds, text_embeds, pair_text, similarity_scale, logit_bias):
    rows, width = image_embeds.shape
    cycle_count = lax.axis_size("blk")
    node_count = lax.axis_size("node")
    far = node_count - 1

    def send(block, even, odd):
        route = []
        for g in range(cycle_count):
            ahead, across = odd if g % 2 else even
            for n in range(node_count):
                to = (g + ahead) % cycle_count * node_count + (n + across) % node_count
                route.append((g * node_count + n, to))
        return lax.ppermute(block, ("blk", "node"), route)

    def swap(block):
        return send(block, (1, 0), (-1, 0))

    stay = (0, 0)
    ahead, behind = (2, 0), (-2, 0)
    block_h = ((rows, width), HALF)
    block_f = ((rows, width), FULL)
    column = ((rows, 1), FULL)
    returns = ((far, rows, width), HALF)

    lead_raw, rest_raw, lead, rest, lead_inv, rest_inv = call(
        unit_kernel,
        "unit",
        [image_embeds, text_embeds],
        [block_h, block_h, block_h, block_h, column, column],
        anywhere=2,
        scratch=[pltpu.SemaphoreType.DMA((4,))],
    )
    got1 = [send(lead, (0, -k), ahead if k == 1 else stay) for k in range(1, node_count)]
    got2 = [send(rest, ahead if k == 1 else stay, (0, -k)) for k in range(1, node_count)]
    mate_rest = swap(rest)
    names = pair_text.reshape(-1, 128)
    params, row_targets, targets = call(
        prep_kernel,
        "prep",
        [names, similarity_scale[:, None], logit_bias[:, None], rest_inv],
        [((8, 128), FULL), ((1, 3 * rows), jnp.int32), ((rows, 1), jnp.int32)],
        anywhere=1,
        scratch=[pltpu.VMEM(names.shape, jnp.int32), pltpu.SemaphoreType.DMA((1,))],
    )
    *got1, late, row_targets, params = lax.optimization_barrier(
        (*got1, lead, row_targets, params)
    )
    mate_lead = swap(late)
    relay1 = [swap(block) for block in got1]
    relay2 = [swap(block) for block in got2]
    (back,) = call(
        functools.partial(first_kernel, far),
        "first",
        [params, row_targets, lead, mate_rest, *got1, *got2],
        [returns],
    )
    one = [send(back[k], behind if k == 0 else stay, (0, k + 1)) for k in range(far)]
    (back,) = call(
        functools.partial(second_kernel, far),
        "second",
        [params, row_targets, rest, mate_lead, *got1, *got2, *relay1],
        [returns],
    )
    two = [send(back[k], (0, k + 1), behind if k == 0 else stay) for k in range(far)]
    lead_dir, rest_dir = call(
        functools.partial(third_kernel, far),
        "third",
        [params, row_targets, targets, lead, rest, mate_rest]
        + [*got1, *got2, *relay1, *relay2],
        [block_f, block_f],
    )
    grads = tangent(far, False, [rest_raw, rest_inv, rest_dir, *one], [], block_f)
    return tuple(tangent(far, True, [lead_raw, lead_inv, lead_dir, *two], grads, block_f))


def solution(mesh):
    return jax.shard_map(
        local,
        mesh=mesh,
        in_specs=(P(("blk", "node"), None), P(("blk", "node"), None), P(), P(), P()),
        out_specs=(P(("blk", "node"), None), P(("blk", "node"), None)),
        check_vma=False,
    )
```

```python
import functools
import math

import jax
import jax.numpy as jnp
from jax import lax
from jax.experimental import pallas as pl
from jax.experimental.pallas import tpu as pltpu
from jax.sharding import PartitionSpec as P

HALF = jnp.bfloat16
FULL = jnp.float32
VMEM_LIMIT = 8 * 1024 * 1024


def roles():
    return lax.rem(lax.axis_index("blk"), 2) == 0, lax.axis_index("node")


def by_role(on_first, on_second):
    first, node = roles()
    pl.when(first)(functools.partial(on_first, node))
    pl.when(jnp.logical_not(first))(functools.partial(on_second, node))


def drawn(params, rows, partners, paired=None):
    vectors = jnp.concatenate([partner[...] for partner in partners], axis=0)
    dots = lax.dot_general(
        rows[...], vectors, (((1,), (1,)), ((), ())), preferred_element_type=FULL
    )
    scale, bias = params[0:1, 0:1], params[1:2, 0:1]
    logits = scale * dots + bias
    if paired is None:
        weights = scale * jax.nn.sigmoid(logits)
    else:
        pairs = paired(logits.shape)
        weights = jnp.where(pairs, -scale, scale) * jax.nn.sigmoid(
            jnp.where(pairs, -logits, logits)
        )
    return jnp.dot(weights.astype(HALF), vectors, preferred_element_type=FULL)


def text_pairs(targets, node):
    def paired(shape):
        rows = shape[0]
        names = lax.broadcasted_iota(jnp.int32, shape, 0) + node * rows
        return names == targets[:, : shape[1]]

    return paired


def image_pairs(targets, node, nodes):
    def paired(shape):
        rows = shape[0]
        columns = lax.broadcasted_iota(jnp.int32, shape, 1)
        names = jnp.where(columns < nodes * rows, columns, -1 - nodes * rows)
        for k in range(nodes):
            here = jnp.logical_and(columns >= k * rows, columns < (k + 1) * rows)
            shift = (lax.rem(node + k, nodes) - k) * rows
            names = jnp.where(here, columns + shift, names)
        return names == targets[...]

    return paired


def unit_kernel(image, text, lead_raw, rest_raw, lead, rest, lead_inv, rest_inv, sems):
    rows = lead.shape[0]
    part = rows // 2 if rows % 32 == 0 else rows
    pieces = [pl.ds(at, part) for at in range(0, rows, part)]

    def copies(source, target, base):
        return [
            pltpu.make_async_copy(source.at[piece], target.at[piece], sems.at[base + i])
            for i, piece in enumerate(pieces)
        ]

    def fetch(lead_source, rest_source, node):
        for copy in copies(lead_source, lead_raw, 0) + copies(rest_source, rest_raw, 2):
            copy.start()

    by_role(functools.partial(fetch, image, text), functools.partial(fetch, text, image))
    for base, raw, half, inv in ((0, lead_raw, lead, lead_inv), (2, rest_raw, rest, rest_inv)):
        for piece, copy in zip(pieces, copies(image, raw, base)):
            copy.wait()
            values = raw[piece, :].astype(FULL)
            inverse = lax.rsqrt(jnp.sum(values * values, axis=1, keepdims=True) + 1e-06)
            half[piece, :] = (values * inverse).astype(HALF)
            inv[piece, :] = inverse


def prep_kernel(
    names, scale, bias, after, params, row_targets, targets, held, sems
):
    copy = pltpu.make_async_copy(names, held, sems.at[0])
    copy.start()
    row = lax.broadcasted_iota(jnp.int32, params.shape, 0)
    params[...] = jnp.where(row == 0, scale[...], bias[...])
    copy.wait()

    rows = targets.shape[0]
    group, node = lax.axis_index("blk"), lax.axis_index("node")
    nodes = lax.axis_size("node")
    start = (group * nodes + node) * rows
    step = math.gcd(rows, 128)
    lines = -(-(128 - step + rows) // 128)
    window = held[pl.ds(start // 128, lines), :]
    window = jnp.concatenate([window[i : i + 1] for i in range(lines)], axis=1)
    mine = window[:, :rows]
    for at in range(step, 128, step):
        mine = jnp.where(lax.rem(start, 128) == at, window[:, at : at + rows], mine)
    mine = mine - group * nodes * rows
    row_targets[...] = jnp.full(row_targets.shape, -1, jnp.int32)
    row_targets[:, :rows] = mine
    square = (rows, rows)
    same = lax.broadcasted_iota(jnp.int32, square, 0) == lax.broadcasted_iota(
        jnp.int32, square, 1
    )
    turned = jnp.sum(jnp.where(same, mine.astype(FULL), 0.0), axis=1, keepdims=True)
    targets[...] = turned.astype(jnp.int32)


def before_kernel(far, params, row_targets, rest, mate_lead, *refs):
    got1, sums = refs[:far], refs[far]

    def on_first(node):
        sums[0] = drawn(params, got1[0], [rest])

    def on_second(node):
        for k in range(far):
            pairs = text_pairs(row_targets, lax.rem(node + k + 1, far + 1))
            sums[k] = drawn(params, got1[k], [rest, mate_lead], pairs)

    by_role(on_first, on_second)


def first_kernel(far, params, sums, *refs):
    got1, got2, back = refs[:far], refs[far : 2 * far], refs[2 * far]

    def on_first(node):
        back[0] = (sums[0] + drawn(params, got1[0], got2)).astype(HALF)

    def on_second(node):
        for k in range(far):
            back[k] = (sums[k] + drawn(params, got1[k], [got2[0]])).astype(HALF)

    by_role(on_first, on_second)


def second_kernel(far, params, row_targets, lead, mate_rest, *refs):
    got1, got2, relay2 = refs[:far], refs[far : 2 * far], refs[2 * far : 3 * far]
    back = refs[3 * far]

    def on_first(node):
        for k in range(far):
            pairs = text_pairs(row_targets, lax.rem(node + k + 1, far + 1))
            images = [lead, got1[0], relay2[0]]
            back[k] = drawn(params, got2[k], images, pairs).astype(HALF)

    def on_second(node):
        back[0] = drawn(params, got2[0], [lead, *got1, mate_rest, *relay2]).astype(HALF)

    by_role(on_first, on_second)


def third_kernel(far, params, row_targets, targets, lead, rest, mate_lead, *refs):
    got1, got2 = refs[:far], refs[far : 2 * far]
    relay1, relay2 = refs[2 * far : 3 * far], refs[3 * far : 4 * far]
    lead_dir, rest_dir = refs[4 * far :]
    nodes = far + 1

    def on_first(node):
        pairs = image_pairs(targets, node, nodes)
        lead_dir[...] = drawn(params, lead, [rest, *got2, mate_lead, *relay1], pairs)
        pairs = text_pairs(row_targets, node)
        rest_dir[...] = drawn(params, rest, [lead, got1[0], relay2[0]], pairs)

    def on_second(node):
        pairs = text_pairs(row_targets, node)
        lead_dir[...] = drawn(params, lead, [rest, mate_lead, got2[0]], pairs)
        pairs = image_pairs(targets, node, nodes)
        rest_dir[...] = drawn(params, rest, [lead, *got1], pairs)

    by_role(on_first, on_second)


def tangent_kernel(far, sums_on_first, raw, inverse, direction, *refs):
    parts = refs[:far]
    image_grads, text_grads, held, sems = refs[-4:]
    rows = raw.shape[0]
    part = rows // 5 if rows % 80 == 0 else rows

    def run(out, count, node):
        gradient = direction[...]
        for k in range(count):
            gradient += parts[k][...].astype(FULL)
        inv = inverse[...]
        unit = raw[...].astype(FULL) * inv
        along = jnp.sum(unit * gradient, axis=1, keepdims=True)
        copies = []
        for i, at in enumerate(range(0, rows, part)):
            piece = slice(at, at + part)
            held[piece, :] = (gradient[piece] - unit[piece] * along[piece]) * inv[piece]
            copy = pltpu.make_async_copy(held.at[piece], out.at[piece], sems.at[i])
            copy.start()
            copies.append(copy)
        for copy in copies:
            copy.wait()

    if sums_on_first:
        by_role(
            functools.partial(run, text_grads, far), functools.partial(run, image_grads, 1)
        )
    else:
        by_role(
            functools.partial(run, image_grads, 1), functools.partial(run, text_grads, far)
        )


def call(kernel, name, operands, shapes, anywhere=0, scratch=()):
    operands = list(operands)
    held = pl.BlockSpec(memory_space=pltpu.VMEM)
    for i in range(anywhere):
        operands[i] = pltpu.with_memory_space_constraint(operands[i], pltpu.HBM)
    return pl.pallas_call(
        kernel,
        name=name,
        out_shape=[pltpu.VMEM(s, d) for s, d in shapes],
        in_specs=[pl.BlockSpec(memory_space=pltpu.HBM)] * anywhere
        + [held] * (len(operands) - anywhere),
        out_specs=[held] * len(shapes),
        scratch_shapes=scratch,
        compiler_params=pltpu.CompilerParams(vmem_limit_bytes=VMEM_LIMIT),
    )(*operands)


def tangent(far, sums_on_first, operands, grads, block):
    rows = block[0][0]
    anywhere = pl.BlockSpec(memory_space=pl.ANY)
    count = len(operands)
    return pl.pallas_call(
        functools.partial(tangent_kernel, far, sums_on_first),
        name="tangent",
        out_shape=[jax.ShapeDtypeStruct(*block)] * 2,
        in_specs=[pl.BlockSpec(memory_space=pltpu.VMEM)] * count + [anywhere] * len(grads),
        out_specs=[anywhere] * 2,
        scratch_shapes=[pltpu.VMEM(*block), pltpu.SemaphoreType.DMA((5,))],
        input_output_aliases={count + i: i for i in range(len(grads))},
        compiler_params=pltpu.CompilerParams(vmem_limit_bytes=VMEM_LIMIT),
    )(*operands, *grads)


def local(image_embeds, text_embeds, pair_text, similarity_scale, logit_bias):
    rows, width = image_embeds.shape
    cycle_count = lax.axis_size("blk")
    node_count = lax.axis_size("node")
    far = node_count - 1

    def send(block, even, odd):
        route = []
        for g in range(cycle_count):
            ahead, across = odd if g % 2 else even
            for n in range(node_count):
                to = (g + ahead) % cycle_count * node_count + (n + across) % node_count
                route.append((g * node_count + n, to))
        return lax.ppermute(block, ("blk", "node"), route)

    def swap(block):
        return send(block, (1, 0), (-1, 0))

    stay = (0, 0)
    ahead, behind = (2, 0), (-2, 0)
    block_h = ((rows, width), HALF)
    block_f = ((rows, width), FULL)
    column = ((rows, 1), FULL)
    returns = ((far, rows, width), HALF)

    lead_raw, rest_raw, lead, rest, lead_inv, rest_inv = call(
        unit_kernel,
        "unit",
        [image_embeds, text_embeds],
        [block_h, block_h, block_h, block_h, column, column],
        anywhere=2,
        scratch=[pltpu.SemaphoreType.DMA((4,))],
    )
    got1 = [send(lead, ahead if k == 1 else stay, (0, -k)) for k in range(1, node_count)]
    mate_lead = swap(lead)
    names = pair_text.reshape(-1, 128)
    params, row_targets, targets = call(
        prep_kernel,
        "prep",
        [names, similarity_scale[:, None], logit_bias[:, None], rest_inv],
        [((8, 128), FULL), ((1, 3 * rows), jnp.int32), ((rows, 1), jnp.int32)],
        anywhere=1,
        scratch=[pltpu.VMEM(names.shape, jnp.int32), pltpu.SemaphoreType.DMA((1,))],
    )
    later, params = lax.optimization_barrier((rest, params))
    got2 = [send(later, (0, -k), ahead if k == 1 else stay) for k in range(1, node_count)]
    mate_rest = swap(later)

    (sums,) = call(
        functools.partial(before_kernel, far),
        "before",
        [params, row_targets, rest, mate_lead, *got1],
        [((far, rows, width), FULL)],
    )
    *got2, sums = lax.optimization_barrier((*got2, sums))
    relay1 = [swap(block) for block in got1]
    relay2 = [swap(block) for block in got2]
    (back,) = call(
        functools.partial(first_kernel, far),
        "first",
        [params, sums, *got1, *got2],
        [returns],
    )
    one = [send(back[k], behind if k == 0 else stay, (0, k + 1)) for k in range(far)]
    (back,) = call(
        functools.partial(second_kernel, far),
        "second",
        [params, row_targets, lead, mate_rest, *got1, *got2, *relay2],
        [returns],
    )
    two = [send(back[k], (0, k + 1), behind if k == 0 else stay) for k in range(far)]
    lead_dir, rest_dir = call(
        functools.partial(third_kernel, far),
        "third",
        [params, row_targets, targets, lead, rest, mate_lead]
        + [*got1, *got2, *relay1, *relay2],
        [block_f, block_f],
    )
    grads = tangent(far, False, [lead_raw, lead_inv, lead_dir, *one], [], block_f)
    return tuple(tangent(far, True, [rest_raw, rest_inv, rest_dir, *two], grads, block_f))


def solution(mesh):
    return jax.shard_map(
        local,
        mesh=mesh,
        in_specs=(P(("blk", "node"), None), P(("blk", "node"), None), P(), P(), P()),
        out_specs=(P(("blk", "node"), None), P(("blk", "node"), None)),
        check_vma=False,
    )
```

```python
import functools
import math

import jax
import jax.numpy as jnp
from jax import lax
from jax.experimental import pallas as pl
from jax.experimental.pallas import tpu as pltpu
from jax.sharding import PartitionSpec as P

HALF = jnp.bfloat16
FULL = jnp.float32
VMEM_LIMIT = 8 * 1024 * 1024


def roles():
    return lax.rem(lax.axis_index("blk"), 2) == 0, lax.axis_index("node")


def by_role(on_first, on_second):
    first, node = roles()
    pl.when(first)(functools.partial(on_first, node))
    pl.when(jnp.logical_not(first))(functools.partial(on_second, node))


def drawn(params, rows, partners, paired=None):
    vectors = jnp.concatenate([partner[...] for partner in partners], axis=0)
    dots = lax.dot_general(
        rows[...], vectors, (((1,), (1,)), ((), ())), preferred_element_type=FULL
    )
    scale, bias = params[0:1, 0:1], params[1:2, 0:1]
    logits = scale * dots + bias
    if paired is None:
        weights = scale * jax.nn.sigmoid(logits)
    else:
        pairs = paired(logits.shape)
        weights = jnp.where(pairs, -scale, scale) * jax.nn.sigmoid(
            jnp.where(pairs, -logits, logits)
        )
    return jnp.dot(weights.astype(HALF), vectors, preferred_element_type=FULL)


def text_pairs(targets, node):
    def paired(shape):
        rows = shape[0]
        names = lax.broadcasted_iota(jnp.int32, shape, 0) + node * rows
        return names == targets[:, : shape[1]]

    return paired


def image_pairs(targets, node, nodes):
    def paired(shape):
        rows = shape[0]
        columns = lax.broadcasted_iota(jnp.int32, shape, 1)
        names = jnp.where(columns < nodes * rows, columns, -1 - nodes * rows)
        for k in range(nodes):
            here = jnp.logical_and(columns >= k * rows, columns < (k + 1) * rows)
            shift = (lax.rem(node + k, nodes) - k) * rows
            names = jnp.where(here, columns + shift, names)
        return names == targets[...]

    return paired


def inverse_of(values):
    return lax.rsqrt(jnp.sum(values * values, axis=1, keepdims=True) + 1e-06)


def half_rows(raw):
    values = raw[...].astype(FULL)
    return (values * inverse_of(values)).astype(HALF)


def unit_kernel(
    image, text, image_raw, text_raw, image_half, text_half, image_inv, text_inv, sems
):
    blocks = ((image, image_raw, image_half, image_inv), (text, text_raw, text_half, text_inv))
    copies = [
        pltpu.make_async_copy(source, raw, sems.at[i])
        for i, (source, raw, _, _) in enumerate(blocks)
    ]
    for copy in copies:
        copy.start()
    for copy, (_, raw, half, inv) in zip(copies, blocks):
        copy.wait()
        values = raw[...].astype(FULL)
        inverse = inverse_of(values)
        half[...] = (values * inverse).astype(HALF)
        inv[...] = inverse


def visit_kernel(raw, after, half):
    half[...] = half_rows(raw)


def prep_kernel(
    names, scale, bias, after, params, row_targets, targets, held, sems
):
    copy = pltpu.make_async_copy(names, held, sems.at[0])
    copy.start()
    row = lax.broadcasted_iota(jnp.int32, params.shape, 0)
    params[...] = jnp.where(row == 0, scale[...], bias[...])
    copy.wait()

    rows = targets.shape[0]
    group, node = lax.axis_index("blk"), lax.axis_index("node")
    nodes = lax.axis_size("node")
    start = (group * nodes + node) * rows
    step = math.gcd(rows, 128)
    lines = -(-(128 - step + rows) // 128)
    window = held[pl.ds(start // 128, lines), :]
    window = jnp.concatenate([window[i : i + 1] for i in range(lines)], axis=1)
    mine = window[:, :rows]
    for at in range(step, 128, step):
        mine = jnp.where(lax.rem(start, 128) == at, window[:, at : at + rows], mine)
    mine = mine - group * nodes * rows
    row_targets[...] = jnp.full(row_targets.shape, -1, jnp.int32)
    row_targets[:, :rows] = mine
    square = (rows, rows)
    same = lax.broadcasted_iota(jnp.int32, square, 0) == lax.broadcasted_iota(
        jnp.int32, square, 1
    )
    turned = jnp.sum(jnp.where(same, mine.astype(FULL), 0.0), axis=1, keepdims=True)
    targets[...] = turned.astype(jnp.int32)


def first_kernel(far, params, row_targets, image, text, mate_image, visit, *refs):
    far_raw, far_text, back = refs[:far], refs[far : 2 * far], refs[2 * far]
    for k in range(far):
        far_text[k][...] = half_rows(far_raw[k])

    def on_first(node):
        back[0] = drawn(params, visit, [text, *far_text]).astype(HALF)

    def on_second(node):
        for k in range(far):
            pairs = text_pairs(row_targets, lax.rem(node + k + 1, far + 1))
            images = [image, mate_image, visit]
            back[k] = drawn(params, far_text[k], images, pairs).astype(HALF)

    by_role(on_first, on_second)


def second_kernel(
    far, params, row_targets, image, text, mate_text, visit, mate_visit, *refs
):
    far_text, relay = refs[:far], refs[far : 2 * far]
    mate_far, back = refs[2 * far : 3 * far], refs[3 * far]

    def on_first(node):
        for k in range(far):
            mate_far[k][...] = half_rows(relay[k])
            pairs = text_pairs(row_targets, lax.rem(node + k + 1, far + 1))
            images = [image, visit, mate_visit]
            back[k] = drawn(params, far_text[k], images, pairs).astype(HALF)

    def on_second(node):
        for k in range(far):
            mate_far[k][...] = half_rows(relay[k])
        texts = [text, *far_text, mate_text, *mate_far]
        back[0] = drawn(params, visit, texts).astype(HALF)

    by_role(on_first, on_second)


def third_kernel(
    far, params, row_targets, targets, image, text, mate_image, mate_text, visit, mate_visit, *refs
):
    far_text, mate_far = refs[:far], refs[far : 2 * far]
    image_dir, text_dir = refs[2 * far :]
    nodes = far + 1

    def on_first(node):
        pairs = image_pairs(targets, node, nodes)
        texts = [text, *far_text, mate_text, *mate_far]
        image_dir[...] = drawn(params, image, texts, pairs)
        pairs = text_pairs(row_targets, node)
        text_dir[...] = drawn(params, text, [image, visit, mate_visit], pairs)

    def on_second(node):
        pairs = text_pairs(row_targets, node)
        text_dir[...] = drawn(params, text, [image, mate_image, visit], pairs)
        pairs = image_pairs(targets, node, nodes)
        image_dir[...] = drawn(params, image, [text, *far_text], pairs)

    by_role(on_first, on_second)


def tangent_kernel(far, image_on_first, *refs):
    image, text, parts = refs[0:3], refs[3:6], refs[6 : 6 + far]
    image_grads, text_grads, held, sems = refs[-4:]
    rows = held.shape[0]
    part = rows // 5 if rows % 80 == 0 else rows

    def run(own, out, count, node):
        raw, inverse, direction = own
        gradient = direction[...]
        for k in range(count):
            gradient += parts[k][...].astype(FULL)
        inv = inverse[...]
        unit = raw[...].astype(FULL) * inv
        along = jnp.sum(unit * gradient, axis=1, keepdims=True)
        copies = []
        for i, at in enumerate(range(0, rows, part)):
            piece = slice(at, at + part)
            held[piece, :] = (gradient[piece] - unit[piece] * along[piece]) * inv[piece]
            copy = pltpu.make_async_copy(held.at[piece], out.at[piece], sems.at[i])
            copy.start()
            copies.append(copy)
        for copy in copies:
            copy.wait()

    on_images = functools.partial(run, image, image_grads, 1)
    on_texts = functools.partial(run, text, text_grads, far)
    if image_on_first:
        by_role(on_images, on_texts)
    else:
        by_role(on_texts, on_images)


def call(kernel, name, operands, shapes, anywhere=0, scratch=()):
    operands = list(operands)
    held = pl.BlockSpec(memory_space=pltpu.VMEM)
    for i in range(anywhere):
        operands[i] = pltpu.with_memory_space_constraint(operands[i], pltpu.HBM)
    return pl.pallas_call(
        kernel,
        name=name,
        out_shape=[pltpu.VMEM(s, d) for s, d in shapes],
        in_specs=[pl.BlockSpec(memory_space=pltpu.HBM)] * anywhere
        + [held] * (len(operands) - anywhere),
        out_specs=[held] * len(shapes),
        scratch_shapes=scratch,
        compiler_params=pltpu.CompilerParams(vmem_limit_bytes=VMEM_LIMIT),
    )(*operands)


def tangent(far, image_on_first, operands, grads, block):
    anywhere = pl.BlockSpec(memory_space=pl.ANY)
    count = len(operands)
    return pl.pallas_call(
        functools.partial(tangent_kernel, far, image_on_first),
        name="tangent",
        out_shape=[jax.ShapeDtypeStruct(*block)] * 2,
        in_specs=[pl.BlockSpec(memory_space=pltpu.VMEM)] * count + [anywhere] * len(grads),
        out_specs=[anywhere] * 2,
        scratch_shapes=[pltpu.VMEM(*block), pltpu.SemaphoreType.DMA((5,))],
        input_output_aliases={count + i: i for i in range(len(grads))},
        compiler_params=pltpu.CompilerParams(vmem_limit_bytes=VMEM_LIMIT),
    )(*operands, *grads)


def local(image_embeds, text_embeds, pair_text, similarity_scale, logit_bias):
    rows, width = image_embeds.shape
    cycle_count = lax.axis_size("blk")
    node_count = lax.axis_size("node")
    far = node_count - 1

    def send(block, even, odd):
        route = []
        for g in range(cycle_count):
            ahead, across = odd if g % 2 else even
            for n in range(node_count):
                to = (g + ahead) % cycle_count * node_count + (n + across) % node_count
                route.append((g * node_count + n, to))
        return lax.ppermute(block, ("blk", "node"), route)

    def swap(block):
        return send(block, (1, 0), (-1, 0))

    stay = (0, 0)
    ahead, behind = (2, 0), (-2, 0)
    block_h = ((rows, width), HALF)
    block_f = ((rows, width), FULL)
    column = ((rows, 1), FULL)
    returns = ((far, rows, width), HALF)

    visit_raw = send(image_embeds, ahead, ahead)
    far_raw = [send(text_embeds, (0, -k), (0, -k)) for k in range(1, node_count)]

    image_raw, text_raw, image, text, image_inv, text_inv = call(
        unit_kernel,
        "unit",
        [image_embeds, text_embeds],
        [block_h, block_h, block_h, block_h, column, column],
        anywhere=2,
        scratch=[pltpu.SemaphoreType.DMA((2,))],
    )
    mate_image = swap(image)
    mate_text = swap(text)
    names = pair_text.reshape(-1, 128)
    params, row_targets, targets = call(
        prep_kernel,
        "prep",
        [names, similarity_scale[:, None], logit_bias[:, None], image_inv],
        [((8, 128), FULL), ((1, 3 * rows), jnp.int32), ((rows, 1), jnp.int32)],
        anywhere=1,
        scratch=[pltpu.VMEM(names.shape, jnp.int32), pltpu.SemaphoreType.DMA((1,))],
    )
    (visit,) = call(visit_kernel, "visit", [visit_raw, params], [block_h])
    mate_visit = swap(visit)
    *far_raw, visit = lax.optimization_barrier((*far_raw, visit))
    relay = [swap(block) for block in far_raw]
    *far_text, back = call(
        functools.partial(first_kernel, far),
        "first",
        [params, row_targets, image, text, mate_image, visit, *far_raw],
        [block_h] * far + [returns],
    )
    one = [send(back[k], behind if k == 0 else stay, (0, k + 1)) for k in range(far)]
    *mate_far, back = call(
        functools.partial(second_kernel, far),
        "second",
        [params, row_targets, image, text, mate_text, visit, mate_visit, *far_text, *relay],
        [block_h] * far + [returns],
    )
    two = [send(back[k], (0, k + 1), behind if k == 0 else stay) for k in range(far)]
    image_dir, text_dir = call(
        functools.partial(third_kernel, far),
        "third",
        [params, row_targets, targets, image, text, mate_image, mate_text, visit, mate_visit]
        + [*far_text, *mate_far],
        [block_f, block_f],
    )
    own = [image_raw, image_inv, image_dir, text_raw, text_inv, text_dir]
    grads = tangent(far, True, [*own, *one], [], block_f)
    return tuple(tangent(far, False, [*own, *two], grads, block_f))


def solution(mesh):
    return jax.shard_map(
        local,
        mesh=mesh,
        in_specs=(P(("blk", "node"), None), P(("blk", "node"), None), P(), P(), P()),
        out_specs=(P(("blk", "node"), None), P(("blk", "node"), None)),
        check_vma=False,
    )
```

```python
import functools
import math

import jax
import jax.numpy as jnp
from jax import lax
from jax.experimental import pallas as pl
from jax.experimental.pallas import tpu as pltpu
from jax.sharding import PartitionSpec as P

HALF = jnp.bfloat16
FULL = jnp.float32
VMEM_LIMIT = 8 * 1024 * 1024


def roles():
    return lax.rem(lax.axis_index("blk"), 2) == 0, lax.axis_index("node")


def by_role(on_first, on_second):
    first, node = roles()
    pl.when(first)(functools.partial(on_first, node))
    pl.when(jnp.logical_not(first))(functools.partial(on_second, node))


def drawn(params, rows, partners, paired=None):
    vectors = jnp.concatenate([partner[...] for partner in partners], axis=0)
    dots = lax.dot_general(
        rows[...], vectors, (((1,), (1,)), ((), ())), preferred_element_type=FULL
    )
    scale, bias = params[0:1, 0:1], params[1:2, 0:1]
    logits = scale * dots + bias
    if paired is None:
        weights = scale * jax.nn.sigmoid(logits)
    else:
        pairs = paired(logits.shape)
        weights = jnp.where(pairs, -scale, scale) * jax.nn.sigmoid(
            jnp.where(pairs, -logits, logits)
        )
    return jnp.dot(weights.astype(HALF), vectors, preferred_element_type=FULL)


def text_pairs(targets, node):
    def paired(shape):
        rows = shape[0]
        names = lax.broadcasted_iota(jnp.int32, shape, 0) + node * rows
        return names == targets[:, : shape[1]]

    return paired


def image_pairs(targets, node, nodes):
    def paired(shape):
        rows = shape[0]
        columns = lax.broadcasted_iota(jnp.int32, shape, 1)
        names = jnp.where(columns < nodes * rows, columns, -1 - nodes * rows)
        for k in range(nodes):
            here = jnp.logical_and(columns >= k * rows, columns < (k + 1) * rows)
            shift = (lax.rem(node + k, nodes) - k) * rows
            names = jnp.where(here, columns + shift, names)
        return names == targets[...]

    return paired


def inverse_of(values):
    return lax.rsqrt(jnp.sum(values * values, axis=1, keepdims=True) + 1e-06)


def half_rows(raw):
    values = raw[...].astype(FULL)
    return (values * inverse_of(values)).astype(HALF)


def unit_kernel(
    image, text, image_raw, text_raw, image_half, text_half, image_inv, text_inv, sems
):
    blocks = ((image, image_raw, image_half, image_inv), (text, text_raw, text_half, text_inv))
    copies = [
        pltpu.make_async_copy(source, raw, sems.at[i])
        for i, (source, raw, _, _) in enumerate(blocks)
    ]
    for copy in copies:
        copy.start()
    for copy, (_, raw, half, inv) in zip(copies, blocks):
        copy.wait()
        values = raw[...].astype(FULL)
        inverse = inverse_of(values)
        half[...] = (values * inverse).astype(HALF)
        inv[...] = inverse


def prep_kernel(
    names, scale, bias, after, params, row_targets, targets, held, sems
):
    copy = pltpu.make_async_copy(names, held, sems.at[0])
    copy.start()
    row = lax.broadcasted_iota(jnp.int32, params.shape, 0)
    params[...] = jnp.where(row == 0, scale[...], bias[...])
    copy.wait()

    rows = targets.shape[0]
    group, node = lax.axis_index("blk"), lax.axis_index("node")
    nodes = lax.axis_size("node")
    start = (group * nodes + node) * rows
    step = math.gcd(rows, 128)
    lines = -(-(128 - step + rows) // 128)
    window = held[pl.ds(start // 128, lines), :]
    window = jnp.concatenate([window[i : i + 1] for i in range(lines)], axis=1)
    mine = window[:, :rows]
    for at in range(step, 128, step):
        mine = jnp.where(lax.rem(start, 128) == at, window[:, at : at + rows], mine)
    mine = mine - group * nodes * rows
    row_targets[...] = jnp.full(row_targets.shape, -1, jnp.int32)
    row_targets[:, :rows] = mine
    square = (rows, rows)
    same = lax.broadcasted_iota(jnp.int32, square, 0) == lax.broadcasted_iota(
        jnp.int32, square, 1
    )
    turned = jnp.sum(jnp.where(same, mine.astype(FULL), 0.0), axis=1, keepdims=True)
    targets[...] = turned.astype(jnp.int32)


def visit_kernel(raw, after, half):
    half[...] = half_rows(raw)


def first_kernel(far, params, row_targets, image, text, mate_image, visit, *refs):
    far_raw, far_text, back = refs[:far], refs[far : 2 * far], refs[2 * far]
    for k in range(far):
        far_text[k][...] = half_rows(far_raw[k])

    def on_first(node):
        back[0] = drawn(params, visit, [text, *far_text]).astype(HALF)

    def on_second(node):
        for k in range(far):
            pairs = text_pairs(row_targets, lax.rem(node + k + 1, far + 1))
            images = [image, mate_image, visit]
            back[k] = drawn(params, far_text[k], images, pairs).astype(HALF)

    by_role(on_first, on_second)


def second_kernel(far, params, row_targets, image, text, mate_text, visit, mate_visit, *refs):
    far_text, mate_far, back = refs[:far], refs[far : 2 * far], refs[2 * far]

    def on_first(node):
        for k in range(far):
            pairs = text_pairs(row_targets, lax.rem(node + k + 1, far + 1))
            images = [image, visit, mate_visit]
            back[k] = drawn(params, far_text[k], images, pairs).astype(HALF)

    def on_second(node):
        texts = [text, *far_text, mate_text, *mate_far]
        back[0] = drawn(params, visit, texts).astype(HALF)

    by_role(on_first, on_second)


def local_part(raw, inverse, direction):
    inv = inverse[...]
    unit = raw[...].astype(FULL) * inv
    along = jnp.sum(unit * direction, axis=1, keepdims=True)
    return (direction - unit * along) * inv


def third_kernel(
    far, params, row_targets, targets, image, text, mate_image, mate_text, visit, mate_visit, *refs
):
    far_text, mate_far = refs[:far], refs[far : 2 * far]
    image_raw, image_inv, text_raw, text_inv, image_part, text_part = refs[2 * far :]
    nodes = far + 1

    def on_first(node):
        pairs = image_pairs(targets, node, nodes)
        texts = [text, *far_text, mate_text, *mate_far]
        direction = drawn(params, image, texts, pairs)
        image_part[...] = local_part(image_raw, image_inv, direction)
        pairs = text_pairs(row_targets, node)
        direction = drawn(params, text, [image, visit, mate_visit], pairs)
        text_part[...] = local_part(text_raw, text_inv, direction)

    def on_second(node):
        pairs = text_pairs(row_targets, node)
        direction = drawn(params, text, [image, mate_image, visit], pairs)
        text_part[...] = local_part(text_raw, text_inv, direction)
        pairs = image_pairs(targets, node, nodes)
        direction = drawn(params, image, [text, *far_text], pairs)
        image_part[...] = local_part(image_raw, image_inv, direction)

    by_role(on_first, on_second)


def tangent_kernel(far, image_on_first, *refs):
    image, text, received = refs[0:3], refs[3:6], refs[6 : 6 + far]
    image_grads, text_grads, held, sems = refs[-4:]
    rows = held.shape[0]
    part = rows // 5 if rows % 80 == 0 else rows

    def run(own, out, count, node):
        raw, inverse, base = own
        gradient = received[0][...].astype(FULL)
        for k in range(1, count):
            gradient += received[k][...].astype(FULL)
        inv = inverse[...]
        values = raw[...].astype(FULL)
        along = jnp.sum(values * gradient, axis=1, keepdims=True) * (inv * inv * inv)
        copies = []
        for i, at in enumerate(range(0, rows, part)):
            piece = slice(at, at + part)
            turned = gradient[piece] * inv[piece] - values[piece] * along[piece]
            held[piece, :] = base[piece, :] + turned
            copy = pltpu.make_async_copy(held.at[piece], out.at[piece], sems.at[i])
            copy.start()
            copies.append(copy)
        for copy in copies:
            copy.wait()

    on_images = functools.partial(run, image, image_grads, 1)
    on_texts = functools.partial(run, text, text_grads, far)
    if image_on_first:
        by_role(on_images, on_texts)
    else:
        by_role(on_texts, on_images)


def call(kernel, name, operands, shapes, anywhere=0, scratch=()):
    operands = list(operands)
    held = pl.BlockSpec(memory_space=pltpu.VMEM)
    for i in range(anywhere):
        operands[i] = pltpu.with_memory_space_constraint(operands[i], pltpu.HBM)
    return pl.pallas_call(
        kernel,
        name=name,
        out_shape=[pltpu.VMEM(s, d) for s, d in shapes],
        in_specs=[pl.BlockSpec(memory_space=pltpu.HBM)] * anywhere
        + [held] * (len(operands) - anywhere),
        out_specs=[held] * len(shapes),
        scratch_shapes=scratch,
        compiler_params=pltpu.CompilerParams(vmem_limit_bytes=VMEM_LIMIT),
    )(*operands)


def tangent(far, image_on_first, operands, grads, block):
    anywhere = pl.BlockSpec(memory_space=pl.ANY)
    count = len(operands)
    return pl.pallas_call(
        functools.partial(tangent_kernel, far, image_on_first),
        name="tangent",
        out_shape=[jax.ShapeDtypeStruct(*block)] * 2,
        in_specs=[pl.BlockSpec(memory_space=pltpu.VMEM)] * count + [anywhere] * len(grads),
        out_specs=[anywhere] * 2,
        scratch_shapes=[pltpu.VMEM(*block), pltpu.SemaphoreType.DMA((5,))],
        input_output_aliases={count + i: i for i in range(len(grads))},
        compiler_params=pltpu.CompilerParams(vmem_limit_bytes=VMEM_LIMIT),
    )(*operands, *grads)


def local(image_embeds, text_embeds, pair_text, similarity_scale, logit_bias):
    rows, width = image_embeds.shape
    cycle_count = lax.axis_size("blk")
    node_count = lax.axis_size("node")
    far = node_count - 1

    def send(block, even, odd):
        route = []
        for g in range(cycle_count):
            ahead, across = odd if g % 2 else even
            for n in range(node_count):
                to = (g + ahead) % cycle_count * node_count + (n + across) % node_count
                route.append((g * node_count + n, to))
        return lax.ppermute(block, ("blk", "node"), route)

    def swap(block):
        return send(block, (1, 0), (-1, 0))

    stay = (0, 0)
    ahead, behind = (2, 0), (-2, 0)
    block_h = ((rows, width), HALF)
    block_f = ((rows, width), FULL)
    column = ((rows, 1), FULL)
    returns = ((far, rows, width), HALF)

    visit_raw = send(image_embeds, ahead, ahead)
    far_raw = [send(text_embeds, (0, -k), (0, -k)) for k in range(1, node_count)]

    image_raw, text_raw, image, text, image_inv, text_inv = call(
        unit_kernel,
        "unit",
        [image_embeds, text_embeds],
        [block_h, block_h, block_h, block_h, column, column],
        anywhere=2,
        scratch=[pltpu.SemaphoreType.DMA((2,))],
    )
    mate_image = swap(image)
    mate_text = swap(text)
    names = pair_text.reshape(-1, 128)
    params, row_targets, targets = call(
        prep_kernel,
        "prep",
        [names, similarity_scale[:, None], logit_bias[:, None], image_inv],
        [((8, 128), FULL), ((1, 3 * rows), jnp.int32), ((rows, 1), jnp.int32)],
        anywhere=1,
        scratch=[pltpu.VMEM(names.shape, jnp.int32), pltpu.SemaphoreType.DMA((1,))],
    )
    (visit,) = call(visit_kernel, "visit", [visit_raw, params], [block_h])
    *far_raw, visit = lax.optimization_barrier((*far_raw, visit))
    *far_text, back = call(
        functools.partial(first_kernel, far),
        "first",
        [params, row_targets, image, text, mate_image, visit, *far_raw],
        [block_h] * far + [returns],
    )
    one = [send(back[k], behind if k == 0 else stay, (0, k + 1)) for k in range(far)]
    visit, *far_text = lax.optimization_barrier((visit, *far_text))
    mate_visit = swap(visit)
    mate_far = [swap(block) for block in far_text]
    (back,) = call(
        functools.partial(second_kernel, far),
        "second",
        [params, row_targets, image, text, mate_text, visit, mate_visit, *far_text, *mate_far],
        [returns],
    )
    two = [send(back[k], (0, k + 1), behind if k == 0 else stay) for k in range(far)]
    image_part, text_part = call(
        functools.partial(third_kernel, far),
        "third",
        [params, row_targets, targets, image, text, mate_image, mate_text, visit, mate_visit]
        + [*far_text, *mate_far, image_raw, image_inv, text_raw, text_inv],
        [block_f, block_f],
    )
    own = [image_raw, image_inv, image_part, text_raw, text_inv, text_part]
    grads = tangent(far, True, [*own, *one], [], block_f)
    return tuple(tangent(far, False, [*own, *two], grads, block_f))


def solution(mesh):
    return jax.shard_map(
        local,
        mesh=mesh,
        in_specs=(P(("blk", "node"), None), P(("blk", "node"), None), P(), P(), P()),
        out_specs=(P(("blk", "node"), None), P(("blk", "node"), None)),
        check_vma=False,
    )
```

```python
import functools
import math

import jax
import jax.numpy as jnp
from jax import lax
from jax.experimental import pallas as pl
from jax.experimental.pallas import tpu as pltpu
from jax.sharding import PartitionSpec as P

HALF = jnp.bfloat16
FULL = jnp.float32
VMEM_LIMIT = 8 * 1024 * 1024


def roles():
    return lax.rem(lax.axis_index("blk"), 2) == 0, lax.axis_index("node")


def by_role(on_first, on_second):
    first, node = roles()
    pl.when(first)(functools.partial(on_first, node))
    pl.when(jnp.logical_not(first))(functools.partial(on_second, node))


def drawn(params, rows, partners, paired=None):
    vectors = jnp.concatenate([partner[...] for partner in partners], axis=0)
    dots = lax.dot_general(
        rows[...], vectors, (((1,), (1,)), ((), ())), preferred_element_type=FULL
    )
    scale, bias = params[0:1, 0:1], params[1:2, 0:1]
    logits = scale * dots + bias
    if paired is None:
        weights = scale * jax.nn.sigmoid(logits)
    else:
        pairs = paired(logits.shape)
        weights = jnp.where(pairs, -scale, scale) * jax.nn.sigmoid(
            jnp.where(pairs, -logits, logits)
        )
    return jnp.dot(weights.astype(HALF), vectors, preferred_element_type=FULL)


def text_pairs(targets, node):
    def paired(shape):
        rows = shape[0]
        names = lax.broadcasted_iota(jnp.int32, shape, 0) + node * rows
        return names == targets[:, : shape[1]]

    return paired


def image_pairs(targets, node, nodes):
    def paired(shape):
        rows = shape[0]
        columns = lax.broadcasted_iota(jnp.int32, shape, 1)
        names = jnp.where(columns < nodes * rows, columns, -1 - nodes * rows)
        for k in range(nodes):
            here = jnp.logical_and(columns >= k * rows, columns < (k + 1) * rows)
            shift = (lax.rem(node + k, nodes) - k) * rows
            names = jnp.where(here, columns + shift, names)
        return names == targets[...]

    return paired


def inverse_of(values):
    return lax.rsqrt(jnp.sum(values * values, axis=1, keepdims=True) + 1e-06)


def half_rows(raw):
    values = raw[...].astype(FULL)
    return (values * inverse_of(values)).astype(HALF)


def unit_kernel(
    image, text, image_raw, text_raw, image_half, text_half, image_inv, text_inv, sems
):
    blocks = ((image, image_raw, image_half, image_inv), (text, text_raw, text_half, text_inv))
    copies = [
        pltpu.make_async_copy(source, raw, sems.at[i])
        for i, (source, raw, _, _) in enumerate(blocks)
    ]
    for copy in copies:
        copy.start()
    for copy, (_, raw, half, inv) in zip(copies, blocks):
        copy.wait()
        values = raw[...].astype(FULL)
        inverse = inverse_of(values)
        half[...] = (values * inverse).astype(HALF)
        inv[...] = inverse


def prep_kernel(
    names, scale, bias, after, params, row_targets, targets, held, sems
):
    copy = pltpu.make_async_copy(names, held, sems.at[0])
    copy.start()
    row = lax.broadcasted_iota(jnp.int32, params.shape, 0)
    params[...] = jnp.where(row == 0, scale[...], bias[...])
    copy.wait()

    rows = targets.shape[0]
    group, node = lax.axis_index("blk"), lax.axis_index("node")
    nodes = lax.axis_size("node")
    start = (group * nodes + node) * rows
    step = math.gcd(rows, 128)
    lines = -(-(128 - step + rows) // 128)
    window = held[pl.ds(start // 128, lines), :]
    window = jnp.concatenate([window[i : i + 1] for i in range(lines)], axis=1)
    mine = window[:, :rows]
    for at in range(step, 128, step):
        mine = jnp.where(lax.rem(start, 128) == at, window[:, at : at + rows], mine)
    mine = mine - group * nodes * rows
    row_targets[...] = jnp.full(row_targets.shape, -1, jnp.int32)
    row_targets[:, :rows] = mine
    square = (rows, rows)
    same = lax.broadcasted_iota(jnp.int32, square, 0) == lax.broadcasted_iota(
        jnp.int32, square, 1
    )
    turned = jnp.sum(jnp.where(same, mine.astype(FULL), 0.0), axis=1, keepdims=True)
    targets[...] = turned.astype(jnp.int32)


def visit_kernel(raw, after, half):
    half[...] = half_rows(raw)


def first_kernel(far, params, row_targets, image, text, mate_image, mate_text, visit, *refs):
    far_raw, got, back = refs[:far], refs[far], refs[far + 1]
    far_text = [got.at[k + 1] for k in range(far)]
    got[0] = visit[...]
    for k in range(far):
        far_text[k][...] = half_rows(far_raw[k])

    def on_first(node):
        back[0] = drawn(params, visit, [text, *far_text]).astype(HALF)

    def on_second(node):
        for k in range(far):
            pairs = text_pairs(row_targets, lax.rem(node + k + 1, far + 1))
            images = [image, mate_image, visit]
            back[k] = drawn(params, far_text[k], images, pairs).astype(HALF)

    by_role(on_first, on_second)


def parted(far, got):
    return got.at[0], [got.at[k + 1] for k in range(far)]


def second_kernel(far, params, row_targets, image, text, mate_text, got, mate_got, back):
    visit, far_text = parted(far, got)
    mate_visit, mate_far = parted(far, mate_got)

    def on_first(node):
        for k in range(far):
            pairs = text_pairs(row_targets, lax.rem(node + k + 1, far + 1))
            images = [image, visit, mate_visit]
            back[k] = drawn(params, far_text[k], images, pairs).astype(HALF)

    def on_second(node):
        texts = [text, *far_text, mate_text, *mate_far]
        back[0] = drawn(params, visit, texts).astype(HALF)

    by_role(on_first, on_second)


def local_part(raw, inverse, direction):
    inv = inverse[...]
    unit = raw[...].astype(FULL) * inv
    along = jnp.sum(unit * direction, axis=1, keepdims=True)
    return (direction - unit * along) * inv


def third_kernel(
    far, params, row_targets, targets, image, text, mate_image, mate_text, got, mate_got,
    image_raw, image_inv, text_raw, text_inv, image_part, text_part,
):
    visit, far_text = parted(far, got)
    mate_visit, mate_far = parted(far, mate_got)
    nodes = far + 1

    def on_first(node):
        pairs = image_pairs(targets, node, nodes)
        texts = [text, *far_text, mate_text, *mate_far]
        direction = drawn(params, image, texts, pairs)
        image_part[...] = local_part(image_raw, image_inv, direction)
        pairs = text_pairs(row_targets, node)
        direction = drawn(params, text, [image, visit, mate_visit], pairs)
        text_part[...] = local_part(text_raw, text_inv, direction)

    def on_second(node):
        pairs = text_pairs(row_targets, node)
        direction = drawn(params, text, [image, mate_image, visit], pairs)
        text_part[...] = local_part(text_raw, text_inv, direction)
        pairs = image_pairs(targets, node, nodes)
        direction = drawn(params, image, [text, *far_text], pairs)
        image_part[...] = local_part(image_raw, image_inv, direction)

    by_role(on_first, on_second)


def finished(far, received, own, count):
    raw, inverse, part = own
    gradient = received[0][...].astype(FULL)
    for k in range(1, count):
        gradient += received[k][...].astype(FULL)
    inv = inverse[...]
    values = raw[...].astype(FULL)
    along = jnp.sum(values * gradient, axis=1, keepdims=True) * (inv * inv * inv)
    return gradient * inv - values * along + part[...]


def fourth_kernel(far, *refs):
    image, text, received, ready = refs[0:3], refs[3:6], refs[6 : 6 + far], refs[6 + far]

    def on_first(node):
        ready[...] = finished(far, received, image, 1)

    def on_second(node):
        ready[...] = finished(far, received, text, far)

    by_role(on_first, on_second)


def last_kernel(far, ready, *refs):
    image, text, received = refs[0:3], refs[3:6], refs[6 : 6 + far]
    image_grads, text_grads, held, sems = refs[6 + far :]

    def run(own, count, ready_out, out, node):
        early = pltpu.make_async_copy(ready, ready_out, sems.at[0])
        early.start()
        held[...] = finished(far, received, own, count)
        late = pltpu.make_async_copy(held, out, sems.at[1])
        late.start()
        early.wait()
        late.wait()

    by_role(
        functools.partial(run, text, far, image_grads, text_grads),
        functools.partial(run, image, 1, text_grads, image_grads),
    )


def call(kernel, name, operands, shapes, anywhere=0, scratch=()):
    operands = list(operands)
    held = pl.BlockSpec(memory_space=pltpu.VMEM)
    for i in range(anywhere):
        operands[i] = pltpu.with_memory_space_constraint(operands[i], pltpu.HBM)
    return pl.pallas_call(
        kernel,
        name=name,
        out_shape=[pltpu.VMEM(s, d) for s, d in shapes],
        in_specs=[pl.BlockSpec(memory_space=pltpu.HBM)] * anywhere
        + [held] * (len(operands) - anywhere),
        out_specs=[held] * len(shapes),
        scratch_shapes=scratch,
        compiler_params=pltpu.CompilerParams(vmem_limit_bytes=VMEM_LIMIT),
    )(*operands)


def last(far, operands, block):
    anywhere = pl.BlockSpec(memory_space=pl.ANY)
    return pl.pallas_call(
        functools.partial(last_kernel, far),
        name="last",
        out_shape=[jax.ShapeDtypeStruct(*block)] * 2,
        in_specs=[pl.BlockSpec(memory_space=pltpu.VMEM)] * len(operands),
        out_specs=[anywhere] * 2,
        scratch_shapes=[pltpu.VMEM(*block), pltpu.SemaphoreType.DMA((2,))],
        compiler_params=pltpu.CompilerParams(vmem_limit_bytes=VMEM_LIMIT),
    )(*operands)


def local(image_embeds, text_embeds, pair_text, similarity_scale, logit_bias):
    rows, width = image_embeds.shape
    cycle_count = lax.axis_size("blk")
    node_count = lax.axis_size("node")
    far = node_count - 1

    def send(block, even, odd):
        route = []
        for g in range(cycle_count):
            ahead, across = odd if g % 2 else even
            for n in range(node_count):
                to = (g + ahead) % cycle_count * node_count + (n + across) % node_count
                route.append((g * node_count + n, to))
        return lax.ppermute(block, ("blk", "node"), route)

    def swap(block):
        return send(block, (1, 0), (-1, 0))

    stay = (0, 0)
    ahead, behind = (2, 0), (-2, 0)
    block_h = ((rows, width), HALF)
    block_f = ((rows, width), FULL)
    column = ((rows, 1), FULL)
    returns = ((far, rows, width), HALF)

    visit_raw = send(image_embeds, ahead, ahead)
    far_raw = [send(text_embeds, (0, -k), (0, -k)) for k in range(1, node_count)]

    image_raw, text_raw, image, text, image_inv, text_inv = call(
        unit_kernel,
        "unit",
        [image_embeds, text_embeds],
        [block_h, block_h, block_h, block_h, column, column],
        anywhere=2,
        scratch=[pltpu.SemaphoreType.DMA((2,))],
    )
    mate_image = swap(image)
    mate_text = swap(text)
    names = pair_text.reshape(-1, 128)
    params, row_targets, targets = call(
        prep_kernel,
        "prep",
        [names, similarity_scale[:, None], logit_bias[:, None], image_inv],
        [((8, 128), FULL), ((1, 3 * rows), jnp.int32), ((rows, 1), jnp.int32)],
        anywhere=1,
        scratch=[pltpu.VMEM(names.shape, jnp.int32), pltpu.SemaphoreType.DMA((1,))],
    )
    (visit,) = call(visit_kernel, "visit", [visit_raw, params], [block_h])
    *far_raw, visit = lax.optimization_barrier((*far_raw, visit))
    got, back = call(
        functools.partial(first_kernel, far),
        "first",
        [params, row_targets, image, text, mate_image, mate_text, visit, *far_raw],
        [((node_count, rows, width), HALF), returns],
    )
    one = [send(back[k], behind if k == 0 else stay, (0, k + 1)) for k in range(far)]
    mate_got = swap(got)
    (back,) = call(
        functools.partial(second_kernel, far),
        "second",
        [params, row_targets, image, text, mate_text, got, mate_got],
        [returns],
    )
    two = [send(back[k], (0, k + 1), behind if k == 0 else stay) for k in range(far)]
    image_part, text_part = call(
        functools.partial(third_kernel, far),
        "third",
        [params, row_targets, targets, image, text, mate_image, mate_text, got, mate_got]
        + [image_raw, image_inv, text_raw, text_inv],
        [block_f, block_f],
    )
    own = [image_raw, image_inv, image_part, text_raw, text_inv, text_part]
    (ready,) = call(
        functools.partial(fourth_kernel, far), "fourth", [*own, *one], [block_f]
    )
    return tuple(last(far, [ready, *own, *two], block_f))


def solution(mesh):
    return jax.shard_map(
        local,
        mesh=mesh,
        in_specs=(P(("blk", "node"), None), P(("blk", "node"), None), P(), P(), P()),
        out_specs=(P(("blk", "node"), None), P(("blk", "node"), None)),
        check_vma=False,
    )
```

```python
import functools
import math

import jax
import jax.numpy as jnp
from jax import lax
from jax.experimental import pallas as pl
from jax.experimental.pallas import tpu as pltpu
from jax.sharding import PartitionSpec as P

HALF = jnp.bfloat16
FULL = jnp.float32
VMEM_LIMIT = 8 * 1024 * 1024


def roles():
    return lax.rem(lax.axis_index("blk"), 2) == 0, lax.axis_index("node")


def by_role(on_first, on_second):
    first, node = roles()
    pl.when(first)(functools.partial(on_first, node))
    pl.when(jnp.logical_not(first))(functools.partial(on_second, node))


def drawn(params, rows, partners, paired=None):
    vectors = jnp.concatenate([partner[...] for partner in partners], axis=0)
    dots = lax.dot_general(
        rows[...], vectors, (((1,), (1,)), ((), ())), preferred_element_type=FULL
    )
    scale, bias = params[0:1, 0:1], params[1:2, 0:1]
    logits = scale * dots + bias
    if paired is None:
        weights = scale * jax.nn.sigmoid(logits)
    else:
        pairs = paired(logits.shape)
        weights = jnp.where(pairs, -scale, scale) * jax.nn.sigmoid(
            jnp.where(pairs, -logits, logits)
        )
    return jnp.dot(weights.astype(HALF), vectors, preferred_element_type=FULL)


def text_pairs(targets, node):
    def paired(shape):
        rows = shape[0]
        names = lax.broadcasted_iota(jnp.int32, shape, 0) + node * rows
        return names == targets[:, : shape[1]]

    return paired


def image_pairs(targets, node, nodes):
    def paired(shape):
        rows = shape[0]
        columns = lax.broadcasted_iota(jnp.int32, shape, 1)
        names = jnp.where(columns < nodes * rows, columns, -1 - nodes * rows)
        for k in range(nodes):
            here = jnp.logical_and(columns >= k * rows, columns < (k + 1) * rows)
            shift = (lax.rem(node + k, nodes) - k) * rows
            names = jnp.where(here, columns + shift, names)
        return names == targets[...]

    return paired


def inverse_of(values):
    return lax.rsqrt(jnp.sum(values * values, axis=1, keepdims=True) + 1e-06)


def half_rows(raw):
    values = raw[...].astype(FULL)
    return (values * inverse_of(values)).astype(HALF)


def unit_kernel(
    image, text, image_raw, text_raw, image_half, text_half, image_inv, text_inv, sems
):
    blocks = ((image, image_raw, image_half, image_inv), (text, text_raw, text_half, text_inv))
    copies = [
        pltpu.make_async_copy(source, raw, sems.at[i])
        for i, (source, raw, _, _) in enumerate(blocks)
    ]
    for copy in copies:
        copy.start()
    for copy, (_, raw, half, inv) in zip(copies, blocks):
        copy.wait()
        values = raw[...].astype(FULL)
        inverse = inverse_of(values)
        half[...] = (values * inverse).astype(HALF)
        inv[...] = inverse


def prep_kernel(
    names, scale, bias, after, params, row_targets, targets, held, sems
):
    copy = pltpu.make_async_copy(names, held, sems.at[0])
    copy.start()
    row = lax.broadcasted_iota(jnp.int32, params.shape, 0)
    params[...] = jnp.where(row == 0, scale[...], bias[...])
    copy.wait()

    rows = targets.shape[0]
    group, node = lax.axis_index("blk"), lax.axis_index("node")
    nodes = lax.axis_size("node")
    start = (group * nodes + node) * rows
    step = math.gcd(rows, 128)
    lines = -(-(128 - step + rows) // 128)
    window = held[pl.ds(start // 128, lines), :]
    window = jnp.concatenate([window[i : i + 1] for i in range(lines)], axis=1)
    mine = window[:, :rows]
    for at in range(step, 128, step):
        mine = jnp.where(lax.rem(start, 128) == at, window[:, at : at + rows], mine)
    mine = mine - group * nodes * rows
    row_targets[...] = jnp.full(row_targets.shape, -1, jnp.int32)
    row_targets[:, :rows] = mine
    square = (rows, rows)
    same = lax.broadcasted_iota(jnp.int32, square, 0) == lax.broadcasted_iota(
        jnp.int32, square, 1
    )
    turned = jnp.sum(jnp.where(same, mine.astype(FULL), 0.0), axis=1, keepdims=True)
    targets[...] = turned.astype(jnp.int32)


def halves_kernel(count, *refs):
    raws, halves = refs[:count], refs[-count:]
    for raw, half in zip(raws, halves):
        half[...] = half_rows(raw)


def first_kernel(far, params, row_targets, image, text, mate_image, mate_text, visit, *refs):
    far_text, mate_far = refs[:far], refs[far : 2 * far]
    back, later = refs[2 * far :]

    def on_first(node):
        back[0] = drawn(params, visit, [text, *far_text]).astype(HALF)

    def on_second(node):
        for k in range(far):
            pairs = text_pairs(row_targets, lax.rem(node + k + 1, far + 1))
            images = [image, mate_image, visit]
            back[k] = drawn(params, far_text[k], images, pairs).astype(HALF)
        texts = [text, *far_text, mate_text, *mate_far]
        later[...] = drawn(params, visit, texts).astype(HALF)

    by_role(on_first, on_second)


def second_kernel(far, params, row_targets, image, visit, mate_visit, later, *refs):
    far_text, back = refs[:far], refs[far]

    def on_first(node):
        for k in range(far):
            pairs = text_pairs(row_targets, lax.rem(node + k + 1, far + 1))
            images = [image, visit, mate_visit]
            back[k] = drawn(params, far_text[k], images, pairs).astype(HALF)

    def on_second(node):
        back[0] = later[...]

    by_role(on_first, on_second)


def local_part(raw, inverse, direction):
    inv = inverse[...]
    unit = raw[...].astype(FULL) * inv
    along = jnp.sum(unit * direction, axis=1, keepdims=True)
    return (direction - unit * along) * inv


def third_kernel(
    far, params, row_targets, targets, image, text, mate_image, mate_text, visit, mate_visit, *refs
):
    far_text, mate_far = refs[:far], refs[far : 2 * far]
    image_raw, image_inv, text_raw, text_inv, image_part, text_part = refs[2 * far :]
    nodes = far + 1

    def on_first(node):
        pairs = image_pairs(targets, node, nodes)
        texts = [text, *far_text, mate_text, *mate_far]
        direction = drawn(params, image, texts, pairs)
        image_part[...] = local_part(image_raw, image_inv, direction)
        pairs = text_pairs(row_targets, node)
        direction = drawn(params, text, [image, visit, mate_visit], pairs)
        text_part[...] = local_part(text_raw, text_inv, direction)

    def on_second(node):
        pairs = text_pairs(row_targets, node)
        direction = drawn(params, text, [image, mate_image, visit], pairs)
        text_part[...] = local_part(text_raw, text_inv, direction)
        pairs = image_pairs(targets, node, nodes)
        direction = drawn(params, image, [text, *far_text], pairs)
        image_part[...] = local_part(image_raw, image_inv, direction)

    by_role(on_first, on_second)


def finish(received, own, count, out, start, stop):
    raw, inverse, part = own
    step = 16 if (stop - start) % 16 == 0 else stop - start
    for at in range(start, stop, step):
        piece = pl.ds(at, step)
        gradient = received[0][piece, :].astype(FULL)
        for k in range(1, count):
            gradient += received[k][piece, :].astype(FULL)
        inv = inverse[piece, :]
        values = raw[piece, :].astype(FULL)
        along = jnp.sum(values * gradient, axis=1, keepdims=True) * (inv * inv * inv)
        out[piece, :] = gradient * inv - values * along + part[piece, :]


def fourth_kernel(far, *refs):
    image, text, received, ready = refs[0:3], refs[3:6], refs[6 : 6 + far], refs[6 + far]

    def run(own, count, node):
        finish(received, own, count, ready, 0, ready.shape[0])

    by_role(functools.partial(run, image, 1), functools.partial(run, text, far))


def last_kernel(far, ready, *refs):
    image, text, received = refs[0:3], refs[3:6], refs[6 : 6 + far]
    image_grads, text_grads, held, sems = refs[6 + far :]
    rows = held.shape[0]
    part = rows // 2 if rows % 32 == 0 else rows

    def run(own, count, ready_out, out, node):
        copies = [pltpu.make_async_copy(ready, ready_out, sems.at[0])]
        copies[0].start()
        for i, at in enumerate(range(0, rows, part)):
            finish(received, own, count, held, at, at + part)
            piece = pl.ds(at, part)
            copies.append(
                pltpu.make_async_copy(held.at[piece], out.at[piece], sems.at[i + 1])
            )
            copies[-1].start()
        for copy in copies:
            copy.wait()

    by_role(
        functools.partial(run, text, far, image_grads, text_grads),
        functools.partial(run, image, 1, text_grads, image_grads),
    )


def call(kernel, name, operands, shapes, anywhere=0, scratch=()):
    operands = list(operands)
    held = pl.BlockSpec(memory_space=pltpu.VMEM)
    for i in range(anywhere):
        operands[i] = pltpu.with_memory_space_constraint(operands[i], pltpu.HBM)
    return pl.pallas_call(
        kernel,
        name=name,
        out_shape=[pltpu.VMEM(s, d) for s, d in shapes],
        in_specs=[pl.BlockSpec(memory_space=pltpu.HBM)] * anywhere
        + [held] * (len(operands) - anywhere),
        out_specs=[held] * len(shapes),
        scratch_shapes=scratch,
        compiler_params=pltpu.CompilerParams(vmem_limit_bytes=VMEM_LIMIT),
    )(*operands)


def last(far, operands, block):
    anywhere = pl.BlockSpec(memory_space=pl.ANY)
    return pl.pallas_call(
        functools.partial(last_kernel, far),
        name="last",
        out_shape=[jax.ShapeDtypeStruct(*block)] * 2,
        in_specs=[pl.BlockSpec(memory_space=pltpu.VMEM)] * len(operands),
        out_specs=[anywhere] * 2,
        scratch_shapes=[pltpu.VMEM(*block), pltpu.SemaphoreType.DMA((3,))],
        compiler_params=pltpu.CompilerParams(vmem_limit_bytes=VMEM_LIMIT),
    )(*operands)


def local(image_embeds, text_embeds, pair_text, similarity_scale, logit_bias):
    rows, width = image_embeds.shape
    cycle_count = lax.axis_size("blk")
    node_count = lax.axis_size("node")
    far = node_count - 1

    def send(block, even, odd):
        route = []
        for g in range(cycle_count):
            ahead, across = odd if g % 2 else even
            for n in range(node_count):
                to = (g + ahead) % cycle_count * node_count + (n + across) % node_count
                route.append((g * node_count + n, to))
        return lax.ppermute(block, ("blk", "node"), route)

    def swap(block):
        return send(block, (1, 0), (-1, 0))

    stay = (0, 0)
    ahead, behind = (2, 0), (-2, 0)
    block_h = ((rows, width), HALF)
    block_f = ((rows, width), FULL)
    column = ((rows, 1), FULL)
    returns = ((far, rows, width), HALF)

    far_raw = [send(text_embeds, (0, -k), (0, -k)) for k in range(1, node_count)]
    visit_raw = send(image_embeds, ahead, ahead)

    image_raw, text_raw, image, text, image_inv, text_inv = call(
        unit_kernel,
        "unit",
        [image_embeds, text_embeds],
        [block_h, block_h, block_h, block_h, column, column],
        anywhere=2,
        scratch=[pltpu.SemaphoreType.DMA((2,))],
    )
    mate_image = swap(image)
    mate_text = swap(text)
    names = pair_text.reshape(-1, 128)
    params, row_targets, targets = call(
        prep_kernel,
        "prep",
        [names, similarity_scale[:, None], logit_bias[:, None], image_inv],
        [((8, 128), FULL), ((1, 3 * rows), jnp.int32), ((rows, 1), jnp.int32)],
        anywhere=1,
        scratch=[pltpu.VMEM(names.shape, jnp.int32), pltpu.SemaphoreType.DMA((1,))],
    )
    far_text = call(
        functools.partial(halves_kernel, far), "far", [*far_raw, params], [block_h] * far
    )
    mate_far = [swap(block) for block in far_text]
    visit_raw, *far_text = lax.optimization_barrier((visit_raw, *far_text))
    (visit,) = call(functools.partial(halves_kernel, 1), "visit", [visit_raw], [block_h])
    back, later = call(
        functools.partial(first_kernel, far),
        "first",
        [params, row_targets, image, text, mate_image, mate_text, visit, *far_text, *mate_far],
        [returns, block_h],
    )
    one = [send(back[k], behind if k == 0 else stay, (0, k + 1)) for k in range(far)]
    visit, later = lax.optimization_barrier((visit, later))
    mate_visit = swap(visit)
    (back,) = call(
        functools.partial(second_kernel, far),
        "second",
        [params, row_targets, image, visit, mate_visit, later, *far_text],
        [returns],
    )
    two = [send(back[k], (0, k + 1), behind if k == 0 else stay) for k in range(far)]
    image_part, text_part = call(
        functools.partial(third_kernel, far),
        "third",
        [params, row_targets, targets, image, text, mate_image, mate_text, visit, mate_visit]
        + [*far_text, *mate_far, image_raw, image_inv, text_raw, text_inv],
        [block_f, block_f],
    )
    own = [image_raw, image_inv, image_part, text_raw, text_inv, text_part]
    (ready,) = call(
        functools.partial(fourth_kernel, far), "fourth", [*own, *one], [block_f]
    )
    return tuple(last(far, [ready, *own, *two], block_f))


def solution(mesh):
    return jax.shard_map(
        local,
        mesh=mesh,
        in_specs=(P(("blk", "node"), None), P(("blk", "node"), None), P(), P(), P()),
        out_specs=(P(("blk", "node"), None), P(("blk", "node"), None)),
        check_vma=False,
    )
```

```python
import functools
import math

import jax
import jax.numpy as jnp
from jax import lax
from jax.experimental import pallas as pl
from jax.experimental.pallas import tpu as pltpu
from jax.sharding import PartitionSpec as P

HALF = jnp.bfloat16
FULL = jnp.float32
VMEM_LIMIT = 8 * 1024 * 1024


def roles():
    return lax.rem(lax.axis_index("blk"), 2) == 0, lax.axis_index("node")


def by_role(on_first, on_second):
    first, node = roles()
    pl.when(first)(functools.partial(on_first, node))
    pl.when(jnp.logical_not(first))(functools.partial(on_second, node))


def drawn(params, rows, partners, paired=None):
    vectors = jnp.concatenate([partner[...] for partner in partners], axis=0)
    dots = lax.dot_general(
        rows[...], vectors, (((1,), (1,)), ((), ())), preferred_element_type=FULL
    )
    scale, bias = params[0:1, 0:1], params[1:2, 0:1]
    logits = scale * dots + bias
    if paired is None:
        weights = scale * jax.nn.sigmoid(logits)
    else:
        pairs = paired(logits.shape)
        weights = jnp.where(pairs, -scale, scale) * jax.nn.sigmoid(
            jnp.where(pairs, -logits, logits)
        )
    return jnp.dot(weights.astype(HALF), vectors, preferred_element_type=FULL)


def text_pairs(targets, node):
    def paired(shape):
        rows = shape[0]
        names = lax.broadcasted_iota(jnp.int32, shape, 0) + node * rows
        return names == targets[:, : shape[1]]

    return paired


def image_pairs(targets, node, nodes):
    def paired(shape):
        rows = shape[0]
        columns = lax.broadcasted_iota(jnp.int32, shape, 1)
        names = jnp.where(columns < nodes * rows, columns, -1 - nodes * rows)
        for k in range(nodes):
            here = jnp.logical_and(columns >= k * rows, columns < (k + 1) * rows)
            shift = (lax.rem(node + k, nodes) - k) * rows
            names = jnp.where(here, columns + shift, names)
        return names == targets[...]

    return paired


def inverse_of(values):
    return lax.rsqrt(jnp.sum(values * values, axis=1, keepdims=True) + 1e-06)


def half_rows(raw):
    values = raw[...].astype(FULL)
    return (values * inverse_of(values)).astype(HALF)


def unit_kernel(
    image, text, image_raw, text_raw, image_half, text_half, image_inv, text_inv, sems
):
    blocks = ((image, image_raw, image_half, image_inv), (text, text_raw, text_half, text_inv))
    copies = [
        pltpu.make_async_copy(source, raw, sems.at[i])
        for i, (source, raw, _, _) in enumerate(blocks)
    ]
    for copy in copies:
        copy.start()
    for copy, (_, raw, half, inv) in zip(copies, blocks):
        copy.wait()
        values = raw[...].astype(FULL)
        inverse = inverse_of(values)
        half[...] = (values * inverse).astype(HALF)
        inv[...] = inverse


def prep_kernel(
    names, scale, bias, after, params, row_targets, targets, held, sems
):
    copy = pltpu.make_async_copy(names, held, sems.at[0])
    copy.start()
    row = lax.broadcasted_iota(jnp.int32, params.shape, 0)
    params[...] = jnp.where(row == 0, scale[...], bias[...])
    copy.wait()

    rows = targets.shape[0]
    group, node = lax.axis_index("blk"), lax.axis_index("node")
    nodes = lax.axis_size("node")
    start = (group * nodes + node) * rows
    step = math.gcd(rows, 128)
    lines = -(-(128 - step + rows) // 128)
    window = held[pl.ds(start // 128, lines), :]
    window = jnp.concatenate([window[i : i + 1] for i in range(lines)], axis=1)
    mine = window[:, :rows]
    for at in range(step, 128, step):
        mine = jnp.where(lax.rem(start, 128) == at, window[:, at : at + rows], mine)
    mine = mine - group * nodes * rows
    row_targets[...] = jnp.full(row_targets.shape, -1, jnp.int32)
    row_targets[:, :rows] = mine
    square = (rows, rows)
    same = lax.broadcasted_iota(jnp.int32, square, 0) == lax.broadcasted_iota(
        jnp.int32, square, 1
    )
    turned = jnp.sum(jnp.where(same, mine.astype(FULL), 0.0), axis=1, keepdims=True)
    targets[...] = turned.astype(jnp.int32)


def visit_kernel(raw, after, half):
    half[...] = half_rows(raw)


def got_kernel(far, visit, *refs):
    got = refs[-1]
    got[0] = visit[...]
    for k in range(far):
        got[k + 1] = half_rows(refs[k])


def parted(far, got):
    return got.at[0], [got.at[k + 1] for k in range(far)]


def first_kernel(far, params, row_targets, image, text, mate_image, mate_text, got, back):
    visit, far_text = parted(far, got)

    def on_first(node):
        back[0] = drawn(params, visit, [text, *far_text]).astype(HALF)

    def on_second(node):
        for k in range(far):
            pairs = text_pairs(row_targets, lax.rem(node + k + 1, far + 1))
            images = [image, mate_image, visit]
            back[k] = drawn(params, far_text[k], images, pairs).astype(HALF)

    by_role(on_first, on_second)


def second_kernel(far, params, row_targets, image, text, mate_text, got, mate_got, back):
    visit, far_text = parted(far, got)
    mate_visit, mate_far = parted(far, mate_got)

    def on_first(node):
        for k in range(far):
            pairs = text_pairs(row_targets, lax.rem(node + k + 1, far + 1))
            images = [image, visit, mate_visit]
            back[k] = drawn(params, far_text[k], images, pairs).astype(HALF)

    def on_second(node):
        texts = [text, *far_text, mate_text, *mate_far]
        back[0] = drawn(params, visit, texts).astype(HALF)

    by_role(on_first, on_second)


def local_part(raw, inverse, direction):
    inv = inverse[...]
    unit = raw[...].astype(FULL) * inv
    along = jnp.sum(unit * direction, axis=1, keepdims=True)
    return (direction - unit * along) * inv


def third_kernel(
    far, params, row_targets, targets, image, text, mate_image, mate_text, got, mate_got,
    image_raw, image_inv, text_raw, text_inv, image_part, text_part,
):
    visit, far_text = parted(far, got)
    mate_visit, mate_far = parted(far, mate_got)
    nodes = far + 1

    def on_first(node):
        pairs = image_pairs(targets, node, nodes)
        texts = [text, *far_text, mate_text, *mate_far]
        direction = drawn(params, image, texts, pairs)
        image_part[...] = local_part(image_raw, image_inv, direction)
        pairs = text_pairs(row_targets, node)
        direction = drawn(params, text, [image, visit, mate_visit], pairs)
        text_part[...] = local_part(text_raw, text_inv, direction)

    def on_second(node):
        pairs = text_pairs(row_targets, node)
        direction = drawn(params, text, [image, mate_image, visit], pairs)
        text_part[...] = local_part(text_raw, text_inv, direction)
        pairs = image_pairs(targets, node, nodes)
        direction = drawn(params, image, [text, *far_text], pairs)
        image_part[...] = local_part(image_raw, image_inv, direction)

    by_role(on_first, on_second)


def finish(received, own, count, out, start, stop):
    raw, inverse, part = own
    step = 16 if (stop - start) % 16 == 0 else stop - start
    for at in range(start, stop, step):
        piece = pl.ds(at, step)
        gradient = received[0][piece, :].astype(FULL)
        for k in range(1, count):
            gradient += received[k][piece, :].astype(FULL)
        inv = inverse[piece, :]
        values = raw[piece, :].astype(FULL)
        along = jnp.sum(values * gradient, axis=1, keepdims=True) * (inv * inv * inv)
        out[piece, :] = gradient * inv - values * along + part[piece, :]


def fourth_kernel(far, *refs):
    image, text, received, ready = refs[0:3], refs[3:6], refs[6 : 6 + far], refs[6 + far]

    def run(own, count, node):
        finish(received, own, count, ready, 0, ready.shape[0])

    by_role(functools.partial(run, image, 1), functools.partial(run, text, far))


def last_kernel(far, ready, *refs):
    image, text, received = refs[0:3], refs[3:6], refs[6 : 6 + far]
    image_grads, text_grads, held, sems = refs[6 + far :]
    rows = held.shape[0]
    part = rows // 2 if rows % 32 == 0 else rows

    def run(own, count, ready_out, out, node):
        copies = [pltpu.make_async_copy(ready, ready_out, sems.at[0])]
        copies[0].start()
        for i, at in enumerate(range(0, rows, part)):
            finish(received, own, count, held, at, at + part)
            piece = pl.ds(at, part)
            copies.append(
                pltpu.make_async_copy(held.at[piece], out.at[piece], sems.at[i + 1])
            )
            copies[-1].start()
        for copy in copies:
            copy.wait()

    by_role(
        functools.partial(run, text, far, image_grads, text_grads),
        functools.partial(run, image, 1, text_grads, image_grads),
    )


def call(kernel, name, operands, shapes, anywhere=0, scratch=()):
    operands = list(operands)
    held = pl.BlockSpec(memory_space=pltpu.VMEM)
    for i in range(anywhere):
        operands[i] = pltpu.with_memory_space_constraint(operands[i], pltpu.HBM)
    return pl.pallas_call(
        kernel,
        name=name,
        out_shape=[pltpu.VMEM(s, d) for s, d in shapes],
        in_specs=[pl.BlockSpec(memory_space=pltpu.HBM)] * anywhere
        + [held] * (len(operands) - anywhere),
        out_specs=[held] * len(shapes),
        scratch_shapes=scratch,
        compiler_params=pltpu.CompilerParams(vmem_limit_bytes=VMEM_LIMIT),
    )(*operands)


def last(far, operands, block):
    anywhere = pl.BlockSpec(memory_space=pl.ANY)
    return pl.pallas_call(
        functools.partial(last_kernel, far),
        name="last",
        out_shape=[jax.ShapeDtypeStruct(*block)] * 2,
        in_specs=[pl.BlockSpec(memory_space=pltpu.VMEM)] * len(operands),
        out_specs=[anywhere] * 2,
        scratch_shapes=[pltpu.VMEM(*block), pltpu.SemaphoreType.DMA((3,))],
        compiler_params=pltpu.CompilerParams(vmem_limit_bytes=VMEM_LIMIT),
    )(*operands)


def local(image_embeds, text_embeds, pair_text, similarity_scale, logit_bias):
    rows, width = image_embeds.shape
    cycle_count = lax.axis_size("blk")
    node_count = lax.axis_size("node")
    far = node_count - 1

    def send(block, even, odd):
        route = []
        for g in range(cycle_count):
            ahead, across = odd if g % 2 else even
            for n in range(node_count):
                to = (g + ahead) % cycle_count * node_count + (n + across) % node_count
                route.append((g * node_count + n, to))
        return lax.ppermute(block, ("blk", "node"), route)

    def swap(block):
        return send(block, (1, 0), (-1, 0))

    stay = (0, 0)
    ahead, behind = (2, 0), (-2, 0)
    block_h = ((rows, width), HALF)
    block_f = ((rows, width), FULL)
    column = ((rows, 1), FULL)
    returns = ((far, rows, width), HALF)

    visit_raw = send(image_embeds, ahead, ahead)
    far_raw = [send(text_embeds, (0, -k), (0, -k)) for k in range(1, node_count)]

    image_raw, text_raw, image, text, image_inv, text_inv = call(
        unit_kernel,
        "unit",
        [image_embeds, text_embeds],
        [block_h, block_h, block_h, block_h, column, column],
        anywhere=2,
        scratch=[pltpu.SemaphoreType.DMA((2,))],
    )
    mate_image = swap(image)
    mate_text = swap(text)
    names = pair_text.reshape(-1, 128)
    params, row_targets, targets = call(
        prep_kernel,
        "prep",
        [names, similarity_scale[:, None], logit_bias[:, None], image_inv],
        [((8, 128), FULL), ((1, 3 * rows), jnp.int32), ((rows, 1), jnp.int32)],
        anywhere=1,
        scratch=[pltpu.VMEM(names.shape, jnp.int32), pltpu.SemaphoreType.DMA((1,))],
    )
    (visit,) = call(visit_kernel, "visit", [visit_raw, params], [block_h])
    *far_raw, visit = lax.optimization_barrier((*far_raw, visit))
    (got,) = call(
        functools.partial(got_kernel, far),
        "got",
        [visit, *far_raw, mate_image, mate_text],
        [((node_count, rows, width), HALF)],
    )
    (back,) = call(
        functools.partial(first_kernel, far),
        "first",
        [params, row_targets, image, text, mate_image, mate_text, got],
        [returns],
    )
    one = [send(back[k], behind if k == 0 else stay, (0, k + 1)) for k in range(far)]
    mate_got = swap(got)
    (back,) = call(
        functools.partial(second_kernel, far),
        "second",
        [params, row_targets, image, text, mate_text, got, mate_got],
        [returns],
    )
    two = [send(back[k], (0, k + 1), behind if k == 0 else stay) for k in range(far)]
    image_part, text_part = call(
        functools.partial(third_kernel, far),
        "third",
        [params, row_targets, targets, image, text, mate_image, mate_text, got, mate_got]
        + [image_raw, image_inv, text_raw, text_inv],
        [block_f, block_f],
    )
    own = [image_raw, image_inv, image_part, text_raw, text_inv, text_part]
    (ready,) = call(
        functools.partial(fourth_kernel, far), "fourth", [*own, *one], [block_f]
    )
    return tuple(last(far, [ready, *own, *two], block_f))


def solution(mesh):
    return jax.shard_map(
        local,
        mesh=mesh,
        in_specs=(P(("blk", "node"), None), P(("blk", "node"), None), P(), P(), P()),
        out_specs=(P(("blk", "node"), None), P(("blk", "node"), None)),
        check_vma=False,
    )
```

```python
import functools
import math

import jax
import jax.numpy as jnp
from jax import lax
from jax.experimental import pallas as pl
from jax.experimental.pallas import tpu as pltpu
from jax.sharding import PartitionSpec as P

HALF = jnp.bfloat16
FULL = jnp.float32
VMEM_LIMIT = 8 * 1024 * 1024


def roles():
    return lax.rem(lax.axis_index("blk"), 2) == 0, lax.axis_index("node")


def by_role(on_first, on_second):
    first, node = roles()
    pl.when(first)(functools.partial(on_first, node))
    pl.when(jnp.logical_not(first))(functools.partial(on_second, node))


def drawn(params, rows, partners, paired=()):
    scale, bias = params[0:1, 0:1], params[1:2, 0:1]
    total = None
    for i, partner in enumerate(partners):
        dots = lax.dot_general(
            rows[...], partner[...], (((1,), (1,)), ((), ())), preferred_element_type=FULL
        )
        logits = scale * dots + bias
        if i < len(paired):
            pairs = paired[i](logits.shape)
            weights = jnp.where(pairs, -scale, scale) * jax.nn.sigmoid(
                jnp.where(pairs, -logits, logits)
            )
        else:
            weights = scale * jax.nn.sigmoid(logits)
        term = jnp.dot(weights.astype(HALF), partner[...], preferred_element_type=FULL)
        total = term if total is None else total + term
    return total


def text_pairs(targets, node):
    def paired(shape):
        return lax.broadcasted_iota(jnp.int32, shape, 0) + node * shape[0] == targets[...]

    return [paired]


def image_pairs(targets, node, nodes):
    def one(other, shape):
        names = lax.broadcasted_iota(jnp.int32, shape, 1) + other * shape[1]
        return names == targets[...]

    return [functools.partial(one, lax.rem(node + k, nodes)) for k in range(nodes)]


def inverse_of(values):
    return lax.rsqrt(jnp.sum(values * values, axis=1, keepdims=True) + 1e-06)


def half_rows(raw):
    values = raw[...].astype(FULL)
    return (values * inverse_of(values)).astype(HALF)


def unit_kernel(
    image, text, image_raw, text_raw, image_half, text_half, image_inv, text_inv, sems
):
    blocks = ((image, image_raw, image_half, image_inv), (text, text_raw, text_half, text_inv))
    copies = [
        pltpu.make_async_copy(source, raw, sems.at[i])
        for i, (source, raw, _, _) in enumerate(blocks)
    ]
    for copy in copies:
        copy.start()
    for copy, (_, raw, half, inv) in zip(copies, blocks):
        copy.wait()
        values = raw[...].astype(FULL)
        inverse = inverse_of(values)
        half[...] = (values * inverse).astype(HALF)
        inv[...] = inverse


def prep_kernel(
    names, scale, bias, after, params, row_targets, targets, held, sems
):
    copy = pltpu.make_async_copy(names, held, sems.at[0])
    copy.start()
    row = lax.broadcasted_iota(jnp.int32, params.shape, 0)
    params[...] = jnp.where(row == 0, scale[...], bias[...])
    copy.wait()

    rows = targets.shape[0]
    group, node = lax.axis_index("blk"), lax.axis_index("node")
    nodes = lax.axis_size("node")
    start = (group * nodes + node) * rows
    step = math.gcd(rows, 128)
    lines = -(-(128 - step + rows) // 128)
    window = held[pl.ds(start // 128, lines), :]
    window = jnp.concatenate([window[i : i + 1] for i in range(lines)], axis=1)
    mine = window[:, :rows]
    for at in range(step, 128, step):
        mine = jnp.where(lax.rem(start, 128) == at, window[:, at : at + rows], mine)
    mine = mine - group * nodes * rows
    row_targets[...] = mine
    square = (rows, rows)
    same = lax.broadcasted_iota(jnp.int32, square, 0) == lax.broadcasted_iota(
        jnp.int32, square, 1
    )
    turned = jnp.sum(jnp.where(same, mine.astype(FULL), 0.0), axis=1, keepdims=True)
    targets[...] = turned.astype(jnp.int32)


def visit_kernel(raw, after, half):
    half[...] = half_rows(raw)


def got_kernel(far, visit, *refs):
    got = refs[-1]
    got[0] = visit[...]
    for k in range(far):
        got[k + 1] = half_rows(refs[k])


def parted(far, got):
    return got.at[0], [got.at[k + 1] for k in range(far)]


def first_kernel(far, params, row_targets, image, text, mate_image, mate_text, got, back):
    visit, far_text = parted(far, got)

    def on_first(node):
        back[0] = drawn(params, visit, [text, *far_text]).astype(HALF)

    def on_second(node):
        for k in range(far):
            pairs = text_pairs(row_targets, lax.rem(node + k + 1, far + 1))
            images = [image, mate_image, visit]
            back[k] = drawn(params, far_text[k], images, pairs).astype(HALF)

    by_role(on_first, on_second)


def second_kernel(far, params, row_targets, image, text, mate_text, got, mate_got, back):
    visit, far_text = parted(far, got)
    mate_visit, mate_far = parted(far, mate_got)

    def on_first(node):
        for k in range(far):
            pairs = text_pairs(row_targets, lax.rem(node + k + 1, far + 1))
            images = [image, visit, mate_visit]
            back[k] = drawn(params, far_text[k], images, pairs).astype(HALF)

    def on_second(node):
        texts = [text, *far_text, mate_text, *mate_far]
        back[0] = drawn(params, visit, texts).astype(HALF)

    by_role(on_first, on_second)


def local_part(raw, inverse, direction):
    inv = inverse[...]
    unit = raw[...].astype(FULL) * inv
    along = jnp.sum(unit * direction, axis=1, keepdims=True)
    return (direction - unit * along) * inv


def third_kernel(
    far, params, row_targets, targets, image, text, mate_image, mate_text, got, mate_got,
    image_raw, image_inv, text_raw, text_inv, image_part, text_part,
):
    visit, far_text = parted(far, got)
    mate_visit, mate_far = parted(far, mate_got)
    nodes = far + 1

    def on_first(node):
        pairs = image_pairs(targets, node, nodes)
        texts = [text, *far_text, mate_text, *mate_far]
        direction = drawn(params, image, texts, pairs)
        image_part[...] = local_part(image_raw, image_inv, direction)
        pairs = text_pairs(row_targets, node)
        direction = drawn(params, text, [image, visit, mate_visit], pairs)
        text_part[...] = local_part(text_raw, text_inv, direction)

    def on_second(node):
        pairs = text_pairs(row_targets, node)
        direction = drawn(params, text, [image, mate_image, visit], pairs)
        text_part[...] = local_part(text_raw, text_inv, direction)
        pairs = image_pairs(targets, node, nodes)
        direction = drawn(params, image, [text, *far_text], pairs)
        image_part[...] = local_part(image_raw, image_inv, direction)

    by_role(on_first, on_second)


def finish(received, own, count, out, start, stop):
    raw, inverse, part = own
    step = 16 if (stop - start) % 16 == 0 else stop - start
    for at in range(start, stop, step):
        piece = pl.ds(at, step)
        gradient = received[0][piece, :].astype(FULL)
        for k in range(1, count):
            gradient += received[k][piece, :].astype(FULL)
        inv = inverse[piece, :]
        values = raw[piece, :].astype(FULL)
        along = jnp.sum(values * gradient, axis=1, keepdims=True) * (inv * inv * inv)
        out[piece, :] = gradient * inv - values * along + part[piece, :]


def fourth_kernel(far, *refs):
    image, text, received, ready = refs[0:3], refs[3:6], refs[6 : 6 + far], refs[6 + far]

    def run(own, count, node):
        finish(received, own, count, ready, 0, ready.shape[0])

    by_role(functools.partial(run, image, 1), functools.partial(run, text, far))


def last_kernel(far, ready, *refs):
    image, text, received = refs[0:3], refs[3:6], refs[6 : 6 + far]
    image_grads, text_grads, held, sems = refs[6 + far :]
    rows = held.shape[0]
    part = rows // 2 if rows % 32 == 0 else rows

    def run(own, count, ready_out, out, node):
        copies = [pltpu.make_async_copy(ready, ready_out, sems.at[0])]
        copies[0].start()
        for i, at in enumerate(range(0, rows, part)):
            finish(received, own, count, held, at, at + part)
            piece = pl.ds(at, part)
            copies.append(
                pltpu.make_async_copy(held.at[piece], out.at[piece], sems.at[i + 1])
            )
            copies[-1].start()
        for copy in copies:
            copy.wait()

    by_role(
        functools.partial(run, text, far, image_grads, text_grads),
        functools.partial(run, image, 1, text_grads, image_grads),
    )


def call(kernel, name, operands, shapes, anywhere=0, scratch=()):
    operands = list(operands)
    held = pl.BlockSpec(memory_space=pltpu.VMEM)
    for i in range(anywhere):
        operands[i] = pltpu.with_memory_space_constraint(operands[i], pltpu.HBM)
    return pl.pallas_call(
        kernel,
        name=name,
        out_shape=[pltpu.VMEM(s, d) for s, d in shapes],
        in_specs=[pl.BlockSpec(memory_space=pltpu.HBM)] * anywhere
        + [held] * (len(operands) - anywhere),
        out_specs=[held] * len(shapes),
        scratch_shapes=scratch,
        compiler_params=pltpu.CompilerParams(vmem_limit_bytes=VMEM_LIMIT),
    )(*operands)


def last(far, operands, block):
    anywhere = pl.BlockSpec(memory_space=pl.ANY)
    return pl.pallas_call(
        functools.partial(last_kernel, far),
        name="last",
        out_shape=[jax.ShapeDtypeStruct(*block)] * 2,
        in_specs=[pl.BlockSpec(memory_space=pltpu.VMEM)] * len(operands),
        out_specs=[anywhere] * 2,
        scratch_shapes=[pltpu.VMEM(*block), pltpu.SemaphoreType.DMA((3,))],
        compiler_params=pltpu.CompilerParams(vmem_limit_bytes=VMEM_LIMIT),
    )(*operands)


def local(image_embeds, text_embeds, pair_text, similarity_scale, logit_bias):
    rows, width = image_embeds.shape
    cycle_count = lax.axis_size("blk")
    node_count = lax.axis_size("node")
    far = node_count - 1

    def send(block, even, odd):
        route = []
        for g in range(cycle_count):
            ahead, across = odd if g % 2 else even
            for n in range(node_count):
                to = (g + ahead) % cycle_count * node_count + (n + across) % node_count
                route.append((g * node_count + n, to))
        return lax.ppermute(block, ("blk", "node"), route)

    def swap(block):
        return send(block, (1, 0), (-1, 0))

    stay = (0, 0)
    ahead, behind = (2, 0), (-2, 0)
    block_h = ((rows, width), HALF)
    block_f = ((rows, width), FULL)
    column = ((rows, 1), FULL)
    returns = ((far, rows, width), HALF)

    visit_raw = send(image_embeds, ahead, ahead)
    far_raw = [send(text_embeds, (0, -k), (0, -k)) for k in range(1, node_count)]

    image_raw, text_raw, image, text, image_inv, text_inv = call(
        unit_kernel,
        "unit",
        [image_embeds, text_embeds],
        [block_h, block_h, block_h, block_h, column, column],
        anywhere=2,
        scratch=[pltpu.SemaphoreType.DMA((2,))],
    )
    mate_image = swap(image)
    mate_text = swap(text)
    names = pair_text.reshape(-1, 128)
    params, row_targets, targets = call(
        prep_kernel,
        "prep",
        [names, similarity_scale[:, None], logit_bias[:, None], image_inv],
        [((8, 128), FULL), ((1, rows), jnp.int32), ((rows, 1), jnp.int32)],
        anywhere=1,
        scratch=[pltpu.VMEM(names.shape, jnp.int32), pltpu.SemaphoreType.DMA((1,))],
    )
    (visit,) = call(visit_kernel, "visit", [visit_raw, params], [block_h])
    *far_raw, visit = lax.optimization_barrier((*far_raw, visit))
    (got,) = call(
        functools.partial(got_kernel, far),
        "got",
        [visit, *far_raw, mate_image, mate_text],
        [((node_count, rows, width), HALF)],
    )
    (back,) = call(
        functools.partial(first_kernel, far),
        "first",
        [params, row_targets, image, text, mate_image, mate_text, got],
        [returns],
    )
    one = [send(back[k], behind if k == 0 else stay, (0, k + 1)) for k in range(far)]
    mate_got = swap(got)
    (back,) = call(
        functools.partial(second_kernel, far),
        "second",
        [params, row_targets, image, text, mate_text, got, mate_got],
        [returns],
    )
    two = [send(back[k], (0, k + 1), behind if k == 0 else stay) for k in range(far)]
    image_part, text_part = call(
        functools.partial(third_kernel, far),
        "third",
        [params, row_targets, targets, image, text, mate_image, mate_text, got, mate_got]
        + [image_raw, image_inv, text_raw, text_inv],
        [block_f, block_f],
    )
    own = [image_raw, image_inv, image_part, text_raw, text_inv, text_part]
    (ready,) = call(
        functools.partial(fourth_kernel, far), "fourth", [*own, *one], [block_f]
    )
    return tuple(last(far, [ready, *own, *two], block_f))


def solution(mesh):
    return jax.shard_map(
        local,
        mesh=mesh,
        in_specs=(P(("blk", "node"), None), P(("blk", "node"), None), P(), P(), P()),
        out_specs=(P(("blk", "node"), None), P(("blk", "node"), None)),
        check_vma=False,
    )
```

```python
import functools
import math

import jax
import jax.numpy as jnp
from jax import lax
from jax.experimental import pallas as pl
from jax.experimental.pallas import tpu as pltpu
from jax.sharding import PartitionSpec as P

HALF = jnp.bfloat16
FULL = jnp.float32
VMEM_LIMIT = 8 * 1024 * 1024


def roles():
    return lax.rem(lax.axis_index("blk"), 2) == 0, lax.axis_index("node")


def by_role(on_first, on_second):
    first, node = roles()
    pl.when(first)(functools.partial(on_first, node))
    pl.when(jnp.logical_not(first))(functools.partial(on_second, node))


def drawn(params, rows, partners, paired=None):
    vectors = jnp.concatenate([partner[...] for partner in partners], axis=0)
    dots = lax.dot_general(
        rows[...], vectors, (((1,), (1,)), ((), ())), preferred_element_type=FULL
    )
    scale, bias = params[0:1, 0:1], params[1:2, 0:1]
    logits = scale * dots + bias
    if paired is None:
        weights = scale * jax.nn.sigmoid(logits)
    else:
        pairs = paired(logits.shape)
        weights = jnp.where(pairs, -scale, scale) * jax.nn.sigmoid(
            jnp.where(pairs, -logits, logits)
        )
    return jnp.dot(weights.astype(HALF), vectors, preferred_element_type=FULL)


def text_pairs(targets, node):
    def paired(shape):
        rows = shape[0]
        names = lax.broadcasted_iota(jnp.int32, shape, 0) + node * rows
        return names == targets[:, : shape[1]]

    return paired


def image_pairs(targets, node, nodes):
    def paired(shape):
        rows = shape[0]
        columns = lax.broadcasted_iota(jnp.int32, shape, 1)
        names = jnp.where(columns < nodes * rows, columns, -1 - nodes * rows)
        for k in range(nodes):
            here = jnp.logical_and(columns >= k * rows, columns < (k + 1) * rows)
            shift = (lax.rem(node + k, nodes) - k) * rows
            names = jnp.where(here, columns + shift, names)
        return names == targets[...]

    return paired


def inverse_of(values):
    return lax.rsqrt(jnp.sum(values * values, axis=1, keepdims=True) + 1e-06)


def half_rows(raw):
    values = raw[...].astype(FULL)
    return (values * inverse_of(values)).astype(HALF)


def unit_kernel(
    image, text, image_raw, text_raw, image_half, text_half, image_inv, text_inv, sems
):
    blocks = ((image, image_raw, image_half, image_inv), (text, text_raw, text_half, text_inv))
    copies = [
        pltpu.make_async_copy(source, raw, sems.at[i])
        for i, (source, raw, _, _) in enumerate(blocks)
    ]
    for copy in copies:
        copy.start()
    for copy, (_, raw, half, inv) in zip(copies, blocks):
        copy.wait()
        values = raw[...].astype(FULL)
        inverse = inverse_of(values)
        half[...] = (values * inverse).astype(HALF)
        inv[...] = inverse


def prep_kernel(
    names, scale, bias, after, params, row_targets, targets, held, sems
):
    copy = pltpu.make_async_copy(names, held, sems.at[0])
    copy.start()
    row = lax.broadcasted_iota(jnp.int32, params.shape, 0)
    params[...] = jnp.where(row == 0, scale[...], bias[...])
    copy.wait()

    rows = targets.shape[0]
    group, node = lax.axis_index("blk"), lax.axis_index("node")
    nodes = lax.axis_size("node")
    start = (group * nodes + node) * rows
    step = math.gcd(rows, 128)
    lines = -(-(128 - step + rows) // 128)
    window = held[pl.ds(start // 128, lines), :]
    window = jnp.concatenate([window[i : i + 1] for i in range(lines)], axis=1)
    mine = window[:, :rows]
    for at in range(step, 128, step):
        mine = jnp.where(lax.rem(start, 128) == at, window[:, at : at + rows], mine)
    mine = mine - group * nodes * rows
    row_targets[...] = jnp.full(row_targets.shape, -1, jnp.int32)
    row_targets[:, :rows] = mine
    square = (rows, rows)
    same = lax.broadcasted_iota(jnp.int32, square, 0) == lax.broadcasted_iota(
        jnp.int32, square, 1
    )
    turned = jnp.sum(jnp.where(same, mine.astype(FULL), 0.0), axis=1, keepdims=True)
    targets[...] = turned.astype(jnp.int32)


def visit_kernel(raw, after, half):
    half[...] = half_rows(raw)


def got_kernel(far, visit, *refs):
    got = refs[-1]
    got[0] = visit[...]
    for k in range(far):
        got[k + 1] = half_rows(refs[k])


def parted(far, got):
    return got.at[0], [got.at[k + 1] for k in range(far)]


def first_kernel(far, params, row_targets, image, text, mate_image, mate_text, got, back):
    visit, far_text = parted(far, got)

    def on_first(node):
        total = drawn(params, visit, [text])
        for k in range(far):
            total += drawn(params, visit, [far_text[k]])
        back[0] = total.astype(HALF)

    def on_second(node):
        for k in range(far):
            pairs = text_pairs(row_targets, lax.rem(node + k + 1, far + 1))
            images = [image, mate_image, visit]
            back[k] = drawn(params, far_text[k], images, pairs).astype(HALF)

    by_role(on_first, on_second)


def second_kernel(far, params, row_targets, image, text, mate_text, got, mate_got, back):
    visit, far_text = parted(far, got)
    mate_visit, mate_far = parted(far, mate_got)

    def on_first(node):
        for k in range(far):
            pairs = text_pairs(row_targets, lax.rem(node + k + 1, far + 1))
            images = [image, visit, mate_visit]
            back[k] = drawn(params, far_text[k], images, pairs).astype(HALF)

    def on_second(node):
        texts = [text, *far_text, mate_text, *mate_far]
        back[0] = drawn(params, visit, texts).astype(HALF)

    by_role(on_first, on_second)


def local_part(raw, inverse, direction):
    inv = inverse[...]
    unit = raw[...].astype(FULL) * inv
    along = jnp.sum(unit * direction, axis=1, keepdims=True)
    return (direction - unit * along) * inv


def third_kernel(
    far, params, row_targets, targets, image, text, mate_image, mate_text, got, mate_got,
    image_raw, image_inv, text_raw, text_inv, image_part, text_part,
):
    visit, far_text = parted(far, got)
    mate_visit, mate_far = parted(far, mate_got)
    nodes = far + 1

    def on_first(node):
        pairs = image_pairs(targets, node, nodes)
        texts = [text, *far_text, mate_text, *mate_far]
        direction = drawn(params, image, texts, pairs)
        image_part[...] = local_part(image_raw, image_inv, direction)
        pairs = text_pairs(row_targets, node)
        direction = drawn(params, text, [image, visit, mate_visit], pairs)
        text_part[...] = local_part(text_raw, text_inv, direction)

    def on_second(node):
        pairs = text_pairs(row_targets, node)
        direction = drawn(params, text, [image, mate_image, visit], pairs)
        text_part[...] = local_part(text_raw, text_inv, direction)
        pairs = image_pairs(targets, node, nodes)
        direction = drawn(params, image, [text, *far_text], pairs)
        image_part[...] = local_part(image_raw, image_inv, direction)

    by_role(on_first, on_second)


def finish(received, own, count, out, start, stop):
    raw, inverse, part = own
    step = 16 if (stop - start) % 16 == 0 else stop - start
    for at in range(start, stop, step):
        piece = pl.ds(at, step)
        gradient = received[0][piece, :].astype(FULL)
        for k in range(1, count):
            gradient += received[k][piece, :].astype(FULL)
        inv = inverse[piece, :]
        values = raw[piece, :].astype(FULL)
        along = jnp.sum(values * gradient, axis=1, keepdims=True) * (inv * inv * inv)
        out[piece, :] = gradient * inv - values * along + part[piece, :]


def fourth_kernel(far, *refs):
    image, text, received, ready = refs[0:3], refs[3:6], refs[6 : 6 + far], refs[6 + far]

    def run(own, count, node):
        finish(received, own, count, ready, 0, ready.shape[0])

    by_role(functools.partial(run, image, 1), functools.partial(run, text, far))


def last_kernel(far, ready, *refs):
    image, text, received = refs[0:3], refs[3:6], refs[6 : 6 + far]
    image_grads, text_grads, held, sems = refs[6 + far :]
    rows = held.shape[0]
    part = rows // 2 if rows % 32 == 0 else rows

    def run(own, count, ready_out, out, node):
        copies = [pltpu.make_async_copy(ready, ready_out, sems.at[0])]
        copies[0].start()
        for i, at in enumerate(range(0, rows, part)):
            finish(received, own, count, held, at, at + part)
            piece = pl.ds(at, part)
            copies.append(
                pltpu.make_async_copy(held.at[piece], out.at[piece], sems.at[i + 1])
            )
            copies[-1].start()
        for copy in copies:
            copy.wait()

    by_role(
        functools.partial(run, text, far, image_grads, text_grads),
        functools.partial(run, image, 1, text_grads, image_grads),
    )


def call(kernel, name, operands, shapes, anywhere=0, scratch=()):
    operands = list(operands)
    held = pl.BlockSpec(memory_space=pltpu.VMEM)
    for i in range(anywhere):
        operands[i] = pltpu.with_memory_space_constraint(operands[i], pltpu.HBM)
    return pl.pallas_call(
        kernel,
        name=name,
        out_shape=[pltpu.VMEM(s, d) for s, d in shapes],
        in_specs=[pl.BlockSpec(memory_space=pltpu.HBM)] * anywhere
        + [held] * (len(operands) - anywhere),
        out_specs=[held] * len(shapes),
        scratch_shapes=scratch,
        compiler_params=pltpu.CompilerParams(vmem_limit_bytes=VMEM_LIMIT),
    )(*operands)


def last(far, operands, block):
    anywhere = pl.BlockSpec(memory_space=pl.ANY)
    return pl.pallas_call(
        functools.partial(last_kernel, far),
        name="last",
        out_shape=[jax.ShapeDtypeStruct(*block)] * 2,
        in_specs=[pl.BlockSpec(memory_space=pltpu.VMEM)] * len(operands),
        out_specs=[anywhere] * 2,
        scratch_shapes=[pltpu.VMEM(*block), pltpu.SemaphoreType.DMA((3,))],
        compiler_params=pltpu.CompilerParams(vmem_limit_bytes=VMEM_LIMIT),
    )(*operands)


def local(image_embeds, text_embeds, pair_text, similarity_scale, logit_bias):
    rows, width = image_embeds.shape
    cycle_count = lax.axis_size("blk")
    node_count = lax.axis_size("node")
    far = node_count - 1

    def send(block, even, odd):
        route = []
        for g in range(cycle_count):
            ahead, across = odd if g % 2 else even
            for n in range(node_count):
                to = (g + ahead) % cycle_count * node_count + (n + across) % node_count
                route.append((g * node_count + n, to))
        return lax.ppermute(block, ("blk", "node"), route)

    def swap(block):
        return send(block, (1, 0), (-1, 0))

    stay = (0, 0)
    ahead, behind = (2, 0), (-2, 0)
    block_h = ((rows, width), HALF)
    block_f = ((rows, width), FULL)
    column = ((rows, 1), FULL)
    returns = ((far, rows, width), HALF)

    visit_raw = send(image_embeds, ahead, ahead)

    image_raw, text_raw, image, text, image_inv, text_inv = call(
        unit_kernel,
        "unit",
        [image_embeds, text_embeds],
        [block_h, block_h, block_h, block_h, column, column],
        anywhere=2,
        scratch=[pltpu.SemaphoreType.DMA((2,))],
    )
    reports, image_inv = lax.optimization_barrier((text_embeds, image_inv))
    far_raw = [send(reports, (0, -k), (0, -k)) for k in range(1, node_count)]
    mate_image = swap(image)
    mate_text = swap(text)
    names = pair_text.reshape(-1, 128)
    params, row_targets, targets = call(
        prep_kernel,
        "prep",
        [names, similarity_scale[:, None], logit_bias[:, None], image_inv],
        [((8, 128), FULL), ((1, 3 * rows), jnp.int32), ((rows, 1), jnp.int32)],
        anywhere=1,
        scratch=[pltpu.VMEM(names.shape, jnp.int32), pltpu.SemaphoreType.DMA((1,))],
    )
    (visit,) = call(visit_kernel, "visit", [visit_raw, params], [block_h])
    *far_raw, visit = lax.optimization_barrier((*far_raw, visit))
    (got,) = call(
        functools.partial(got_kernel, far),
        "got",
        [visit, *far_raw, mate_image, mate_text],
        [((node_count, rows, width), HALF)],
    )
    (back,) = call(
        functools.partial(first_kernel, far),
        "first",
        [params, row_targets, image, text, mate_image, mate_text, got],
        [returns],
    )
    one = [send(back[k], behind if k == 0 else stay, (0, k + 1)) for k in range(far)]
    mate_got = swap(got)
    (back,) = call(
        functools.partial(second_kernel, far),
        "second",
        [params, row_targets, image, text, mate_text, got, mate_got],
        [returns],
    )
    two = [send(back[k], (0, k + 1), behind if k == 0 else stay) for k in range(far)]
    image_part, text_part = call(
        functools.partial(third_kernel, far),
        "third",
        [params, row_targets, targets, image, text, mate_image, mate_text, got, mate_got]
        + [image_raw, image_inv, text_raw, text_inv],
        [block_f, block_f],
    )
    own = [image_raw, image_inv, image_part, text_raw, text_inv, text_part]
    (ready,) = call(
        functools.partial(fourth_kernel, far), "fourth", [*own, *one], [block_f]
    )
    return tuple(last(far, [ready, *own, *two], block_f))


def solution(mesh):
    return jax.shard_map(
        local,
        mesh=mesh,
        in_specs=(P(("blk", "node"), None), P(("blk", "node"), None), P(), P(), P()),
        out_specs=(P(("blk", "node"), None), P(("blk", "node"), None)),
        check_vma=False,
    )
```

```python
import functools
import math

import jax
import jax.numpy as jnp
from jax import lax
from jax.experimental import pallas as pl
from jax.experimental.pallas import tpu as pltpu
from jax.sharding import PartitionSpec as P

HALF = jnp.bfloat16
FULL = jnp.float32
VMEM_LIMIT = 8 * 1024 * 1024


def roles():
    return lax.rem(lax.axis_index("blk"), 2) == 0, lax.axis_index("node")


def by_role(on_first, on_second):
    first, node = roles()
    pl.when(first)(functools.partial(on_first, node))
    pl.when(jnp.logical_not(first))(functools.partial(on_second, node))


def drawn(params, rows, partners, paired=None):
    vectors = jnp.concatenate([partner[...] for partner in partners], axis=0)
    dots = lax.dot_general(
        rows[...], vectors, (((1,), (1,)), ((), ())), preferred_element_type=FULL
    )
    scale, bias = params[0:1, 0:1], params[1:2, 0:1]
    logits = scale * dots + bias
    if paired is None:
        weights = scale * jax.nn.sigmoid(logits)
    else:
        pairs = paired(logits.shape)
        weights = jnp.where(pairs, -scale, scale) * jax.nn.sigmoid(
            jnp.where(pairs, -logits, logits)
        )
    return jnp.dot(weights.astype(HALF), vectors, preferred_element_type=FULL)


def text_pairs(targets, node):
    def paired(shape):
        rows = shape[0]
        names = lax.broadcasted_iota(jnp.int32, shape, 0) + node * rows
        return names == targets[:, : shape[1]]

    return paired


def image_pairs(targets, node, nodes):
    def paired(shape):
        rows = shape[0]
        columns = lax.broadcasted_iota(jnp.int32, shape, 1)
        names = jnp.where(columns < nodes * rows, columns, -1 - nodes * rows)
        for k in range(nodes):
            here = jnp.logical_and(columns >= k * rows, columns < (k + 1) * rows)
            shift = (lax.rem(node + k, nodes) - k) * rows
            names = jnp.where(here, columns + shift, names)
        return names == targets[...]

    return paired


def inverse_of(values):
    return lax.rsqrt(jnp.sum(values * values, axis=1, keepdims=True) + 1e-06)


def half_rows(raw):
    values = raw[...].astype(FULL)
    return (values * inverse_of(values)).astype(HALF)


def unit_kernel(
    image, text, image_raw, text_raw, image_half, text_half, image_inv, text_inv, sems
):
    blocks = ((image, image_raw, image_half, image_inv), (text, text_raw, text_half, text_inv))
    copies = [
        pltpu.make_async_copy(source, raw, sems.at[i])
        for i, (source, raw, _, _) in enumerate(blocks)
    ]
    for copy in copies:
        copy.start()
    for copy, (_, raw, half, inv) in zip(copies, blocks):
        copy.wait()
        values = raw[...].astype(FULL)
        inverse = inverse_of(values)
        half[...] = (values * inverse).astype(HALF)
        inv[...] = inverse


def prep_kernel(
    names, scale, bias, after, params, row_targets, targets, held, sems
):
    copy = pltpu.make_async_copy(names, held, sems.at[0])
    copy.start()
    row = lax.broadcasted_iota(jnp.int32, params.shape, 0)
    params[...] = jnp.where(row == 0, scale[...], bias[...])
    copy.wait()

    rows = targets.shape[0]
    group, node = lax.axis_index("blk"), lax.axis_index("node")
    nodes = lax.axis_size("node")
    start = (group * nodes + node) * rows
    step = math.gcd(rows, 128)
    lines = -(-(128 - step + rows) // 128)
    window = held[pl.ds(start // 128, lines), :]
    window = jnp.concatenate([window[i : i + 1] for i in range(lines)], axis=1)
    mine = window[:, :rows]
    for at in range(step, 128, step):
        mine = jnp.where(lax.rem(start, 128) == at, window[:, at : at + rows], mine)
    mine = mine - group * nodes * rows
    row_targets[...] = jnp.full(row_targets.shape, -1, jnp.int32)
    row_targets[:, :rows] = mine
    square = (rows, rows)
    same = lax.broadcasted_iota(jnp.int32, square, 0) == lax.broadcasted_iota(
        jnp.int32, square, 1
    )
    turned = jnp.sum(jnp.where(same, mine.astype(FULL), 0.0), axis=1, keepdims=True)
    targets[...] = turned.astype(jnp.int32)


def visit_kernel(raw, after, half):
    half[...] = half_rows(raw)


def got_kernel(far, visit, *refs):
    got = refs[-1]
    got[0] = visit[...]
    for k in range(far):
        got[k + 1] = half_rows(refs[k])


def parted(far, got):
    return got.at[0], [got.at[k + 1] for k in range(far)]


def ahead_kernel(
    far, params, row_targets, image, text, mate_image, mate_text, got, back, part
):
    visit, far_text = parted(far, got)

    def on_first(node):
        pass

    def on_second(node):
        for k in range(far):
            pairs = text_pairs(row_targets, lax.rem(node + k + 1, far + 1))
            images = [image, mate_image, visit]
            back[k] = drawn(params, far_text[k], images, pairs).astype(HALF)
        part[...] = drawn(params, visit, [text, *far_text, mate_text])

    by_role(on_first, on_second)


def first_kernel(far, params, text, got, early, back):
    visit, far_text = parted(far, got)

    def on_first(node):
        total = drawn(params, visit, [text])
        for k in range(far):
            total += drawn(params, visit, [far_text[k]])
        back[0] = total.astype(HALF)

    def on_second(node):
        back[...] = early[...]

    by_role(on_first, on_second)


def second_kernel(far, params, row_targets, image, got, mate_got, part, back):
    visit, far_text = parted(far, got)
    mate_visit, mate_far = parted(far, mate_got)

    def on_first(node):
        for k in range(far):
            pairs = text_pairs(row_targets, lax.rem(node + k + 1, far + 1))
            images = [image, visit, mate_visit]
            back[k] = drawn(params, far_text[k], images, pairs).astype(HALF)

    def on_second(node):
        back[0] = (part[...] + drawn(params, visit, mate_far)).astype(HALF)

    by_role(on_first, on_second)


def local_part(raw, inverse, direction):
    inv = inverse[...]
    unit = raw[...].astype(FULL) * inv
    along = jnp.sum(unit * direction, axis=1, keepdims=True)
    return (direction - unit * along) * inv


def third_kernel(
    far, params, row_targets, targets, image, text, mate_image, mate_text, got, mate_got,
    image_raw, image_inv, text_raw, text_inv, image_part, text_part,
):
    visit, far_text = parted(far, got)
    mate_visit, mate_far = parted(far, mate_got)
    nodes = far + 1

    def on_first(node):
        pairs = image_pairs(targets, node, nodes)
        texts = [text, *far_text, mate_text, *mate_far]
        direction = drawn(params, image, texts, pairs)
        image_part[...] = local_part(image_raw, image_inv, direction)
        pairs = text_pairs(row_targets, node)
        direction = drawn(params, text, [image, visit, mate_visit], pairs)
        text_part[...] = local_part(text_raw, text_inv, direction)

    def on_second(node):
        pairs = text_pairs(row_targets, node)
        direction = drawn(params, text, [image, mate_image, visit], pairs)
        text_part[...] = local_part(text_raw, text_inv, direction)
        pairs = image_pairs(targets, node, nodes)
        direction = drawn(params, image, [text, *far_text], pairs)
        image_part[...] = local_part(image_raw, image_inv, direction)

    by_role(on_first, on_second)


def finish(received, own, count, out, start, stop):
    raw, inverse, part = own
    step = 16 if (stop - start) % 16 == 0 else stop - start
    for at in range(start, stop, step):
        piece = pl.ds(at, step)
        gradient = received[0][piece, :].astype(FULL)
        for k in range(1, count):
            gradient += received[k][piece, :].astype(FULL)
        inv = inverse[piece, :]
        values = raw[piece, :].astype(FULL)
        along = jnp.sum(values * gradient, axis=1, keepdims=True) * (inv * inv * inv)
        out[piece, :] = gradient * inv - values * along + part[piece, :]


def fourth_kernel(far, *refs):
    image, text, received, ready = refs[0:3], refs[3:6], refs[6 : 6 + far], refs[6 + far]

    def run(own, count, node):
        finish(received, own, count, ready, 0, ready.shape[0])

    by_role(functools.partial(run, image, 1), functools.partial(run, text, far))


def last_kernel(far, ready, *refs):
    image, text, received = refs[0:3], refs[3:6], refs[6 : 6 + far]
    image_grads, text_grads, held, sems = refs[6 + far :]
    rows = held.shape[0]
    part = rows // 2 if rows % 32 == 0 else rows

    def run(own, count, ready_out, out, node):
        copies = [pltpu.make_async_copy(ready, ready_out, sems.at[0])]
        copies[0].start()
        for i, at in enumerate(range(0, rows, part)):
            finish(received, own, count, held, at, at + part)
            piece = pl.ds(at, part)
            copies.append(
                pltpu.make_async_copy(held.at[piece], out.at[piece], sems.at[i + 1])
            )
            copies[-1].start()
        for copy in copies:
            copy.wait()

    by_role(
        functools.partial(run, text, far, image_grads, text_grads),
        functools.partial(run, image, 1, text_grads, image_grads),
    )


def call(kernel, name, operands, shapes, anywhere=0, scratch=()):
    operands = list(operands)
    held = pl.BlockSpec(memory_space=pltpu.VMEM)
    for i in range(anywhere):
        operands[i] = pltpu.with_memory_space_constraint(operands[i], pltpu.HBM)
    return pl.pallas_call(
        kernel,
        name=name,
        out_shape=[pltpu.VMEM(s, d) for s, d in shapes],
        in_specs=[pl.BlockSpec(memory_space=pltpu.HBM)] * anywhere
        + [held] * (len(operands) - anywhere),
        out_specs=[held] * len(shapes),
        scratch_shapes=scratch,
        compiler_params=pltpu.CompilerParams(vmem_limit_bytes=VMEM_LIMIT),
    )(*operands)


def last(far, operands, block):
    anywhere = pl.BlockSpec(memory_space=pl.ANY)
    return pl.pallas_call(
        functools.partial(last_kernel, far),
        name="last",
        out_shape=[jax.ShapeDtypeStruct(*block)] * 2,
        in_specs=[pl.BlockSpec(memory_space=pltpu.VMEM)] * len(operands),
        out_specs=[anywhere] * 2,
        scratch_shapes=[pltpu.VMEM(*block), pltpu.SemaphoreType.DMA((3,))],
        compiler_params=pltpu.CompilerParams(vmem_limit_bytes=VMEM_LIMIT),
    )(*operands)


def local(image_embeds, text_embeds, pair_text, similarity_scale, logit_bias):
    rows, width = image_embeds.shape
    cycle_count = lax.axis_size("blk")
    node_count = lax.axis_size("node")
    far = node_count - 1

    def send(block, even, odd):
        route = []
        for g in range(cycle_count):
            ahead, across = odd if g % 2 else even
            for n in range(node_count):
                to = (g + ahead) % cycle_count * node_count + (n + across) % node_count
                route.append((g * node_count + n, to))
        return lax.ppermute(block, ("blk", "node"), route)

    def swap(block):
        return send(block, (1, 0), (-1, 0))

    stay = (0, 0)
    ahead, behind = (2, 0), (-2, 0)
    block_h = ((rows, width), HALF)
    block_f = ((rows, width), FULL)
    column = ((rows, 1), FULL)
    returns = ((far, rows, width), HALF)

    visit_raw = send(image_embeds, ahead, ahead)
    far_raw = [send(text_embeds, (0, -k), (0, -k)) for k in range(1, node_count)]

    image_raw, text_raw, image, text, image_inv, text_inv = call(
        unit_kernel,
        "unit",
        [image_embeds, text_embeds],
        [block_h, block_h, block_h, block_h, column, column],
        anywhere=2,
        scratch=[pltpu.SemaphoreType.DMA((2,))],
    )
    mate_image = swap(image)
    mate_text = swap(text)
    names = pair_text.reshape(-1, 128)
    params, row_targets, targets = call(
        prep_kernel,
        "prep",
        [names, similarity_scale[:, None], logit_bias[:, None], image_inv],
        [((8, 128), FULL), ((1, 3 * rows), jnp.int32), ((rows, 1), jnp.int32)],
        anywhere=1,
        scratch=[pltpu.VMEM(names.shape, jnp.int32), pltpu.SemaphoreType.DMA((1,))],
    )
    (visit,) = call(visit_kernel, "visit", [visit_raw, params], [block_h])
    *far_raw, visit = lax.optimization_barrier((*far_raw, visit))
    (got,) = call(
        functools.partial(got_kernel, far),
        "got",
        [visit, *far_raw, mate_image, mate_text],
        [((node_count, rows, width), HALF)],
    )
    early, part = call(
        functools.partial(ahead_kernel, far),
        "ahead",
        [params, row_targets, image, text, mate_image, mate_text, got],
        [returns, block_f],
    )
    got, early = lax.optimization_barrier((got, early))
    mate_got = swap(got)
    (back,) = call(
        functools.partial(first_kernel, far), "first", [params, text, got, early], [returns]
    )
    one = [send(back[k], behind if k == 0 else stay, (0, k + 1)) for k in range(far)]
    (back,) = call(
        functools.partial(second_kernel, far),
        "second",
        [params, row_targets, image, got, mate_got, part],
        [returns],
    )
    two = [send(back[k], (0, k + 1), behind if k == 0 else stay) for k in range(far)]
    image_part, text_part = call(
        functools.partial(third_kernel, far),
        "third",
        [params, row_targets, targets, image, text, mate_image, mate_text, got, mate_got]
        + [image_raw, image_inv, text_raw, text_inv],
        [block_f, block_f],
    )
    own = [image_raw, image_inv, image_part, text_raw, text_inv, text_part]
    (ready,) = call(
        functools.partial(fourth_kernel, far), "fourth", [*own, *one], [block_f]
    )
    return tuple(last(far, [ready, *own, *two], block_f))


def solution(mesh):
    return jax.shard_map(
        local,
        mesh=mesh,
        in_specs=(P(("blk", "node"), None), P(("blk", "node"), None), P(), P(), P()),
        out_specs=(P(("blk", "node"), None), P(("blk", "node"), None)),
        check_vma=False,
    )
```

```python
import functools
import math

import jax
import jax.numpy as jnp
from jax import lax
from jax.experimental import pallas as pl
from jax.experimental.pallas import tpu as pltpu
from jax.sharding import PartitionSpec as P

HALF = jnp.bfloat16
FULL = jnp.float32
VMEM_LIMIT = 8 * 1024 * 1024


def roles():
    return lax.rem(lax.axis_index("blk"), 2) == 0, lax.axis_index("node")


def by_role(on_first, on_second):
    first, node = roles()
    pl.when(first)(functools.partial(on_first, node))
    pl.when(jnp.logical_not(first))(functools.partial(on_second, node))


def drawn(params, rows, partners, paired=None):
    vectors = jnp.concatenate([partner[...] for partner in partners], axis=0)
    dots = lax.dot_general(
        rows[...], vectors, (((1,), (1,)), ((), ())), preferred_element_type=FULL
    )
    scale, bias = params[0:1, 0:1], params[1:2, 0:1]
    logits = scale * dots + bias
    if paired is None:
        weights = scale * jax.nn.sigmoid(logits)
    else:
        pairs = paired(logits.shape)
        weights = jnp.where(pairs, -scale, scale) * jax.nn.sigmoid(
            jnp.where(pairs, -logits, logits)
        )
    return jnp.dot(weights.astype(HALF), vectors, preferred_element_type=FULL)


def text_pairs(targets, node):
    def paired(shape):
        rows = shape[0]
        names = lax.broadcasted_iota(jnp.int32, shape, 0) + node * rows
        return names == targets[:, : shape[1]]

    return paired


def image_pairs(targets, node, nodes):
    def paired(shape):
        rows = shape[0]
        columns = lax.broadcasted_iota(jnp.int32, shape, 1)
        names = jnp.where(columns < nodes * rows, columns, -1 - nodes * rows)
        for k in range(nodes):
            here = jnp.logical_and(columns >= k * rows, columns < (k + 1) * rows)
            shift = (lax.rem(node + k, nodes) - k) * rows
            names = jnp.where(here, columns + shift, names)
        return names == targets[...]

    return paired


def inverse_of(values):
    return lax.rsqrt(jnp.sum(values * values, axis=1, keepdims=True) + 1e-06)


def half_rows(raw):
    values = raw[...].astype(FULL)
    return (values * inverse_of(values)).astype(HALF)


def unit_kernel(
    image, text, image_raw, text_raw, image_half, text_half, image_inv, text_inv, sems
):
    blocks = ((image, image_raw, image_half, image_inv), (text, text_raw, text_half, text_inv))
    copies = [
        pltpu.make_async_copy(source, raw, sems.at[i])
        for i, (source, raw, _, _) in enumerate(blocks)
    ]
    for copy in copies:
        copy.start()
    for copy, (_, raw, half, inv) in zip(copies, blocks):
        copy.wait()
        values = raw[...].astype(FULL)
        inverse = inverse_of(values)
        half[...] = (values * inverse).astype(HALF)
        inv[...] = inverse


def prep_kernel(
    names, scale, bias, after, params, row_targets, targets, held, sems
):
    copy = pltpu.make_async_copy(names, held, sems.at[0])
    copy.start()
    row = lax.broadcasted_iota(jnp.int32, params.shape, 0)
    params[...] = jnp.where(row == 0, scale[...], bias[...])
    copy.wait()

    rows = targets.shape[0]
    group, node = lax.axis_index("blk"), lax.axis_index("node")
    nodes = lax.axis_size("node")
    start = (group * nodes + node) * rows
    step = math.gcd(rows, 128)
    lines = -(-(128 - step + rows) // 128)
    window = held[pl.ds(start // 128, lines), :]
    window = jnp.concatenate([window[i : i + 1] for i in range(lines)], axis=1)
    mine = window[:, :rows]
    for at in range(step, 128, step):
        mine = jnp.where(lax.rem(start, 128) == at, window[:, at : at + rows], mine)
    mine = mine - group * nodes * rows
    row_targets[...] = jnp.full(row_targets.shape, -1, jnp.int32)
    row_targets[:, :rows] = mine
    square = (rows, rows)
    same = lax.broadcasted_iota(jnp.int32, square, 0) == lax.broadcasted_iota(
        jnp.int32, square, 1
    )
    turned = jnp.sum(jnp.where(same, mine.astype(FULL), 0.0), axis=1, keepdims=True)
    targets[...] = turned.astype(jnp.int32)


def visit_kernel(raw, after, half):
    half[...] = half_rows(raw)


def got_kernel(far, visit, *refs):
    got = refs[-1]
    got[0] = visit[...]
    for k in range(far):
        got[k + 1] = half_rows(refs[k])


def parted(far, got):
    return got.at[0], [got.at[k + 1] for k in range(far)]


def first_kernel(
    far, params, row_targets, image, text, mate_image, mate_text, got, back, part
):
    visit, far_text = parted(far, got)

    def on_first(node):
        total = drawn(params, visit, [text])
        for k in range(far):
            total += drawn(params, visit, [far_text[k]])
        back[0] = total.astype(HALF)

    def on_second(node):
        for k in range(far):
            pairs = text_pairs(row_targets, lax.rem(node + k + 1, far + 1))
            images = [image, mate_image, visit]
            back[k] = drawn(params, far_text[k], images, pairs).astype(HALF)
        part[...] = drawn(params, visit, [text, *far_text, mate_text])

    by_role(on_first, on_second)


def second_kernel(far, params, row_targets, image, got, mate_got, part, back):
    visit, far_text = parted(far, got)
    mate_visit, mate_far = parted(far, mate_got)

    def on_first(node):
        for k in range(far):
            pairs = text_pairs(row_targets, lax.rem(node + k + 1, far + 1))
            images = [image, visit, mate_visit]
            back[k] = drawn(params, far_text[k], images, pairs).astype(HALF)

    def on_second(node):
        back[0] = (part[...] + drawn(params, visit, mate_far)).astype(HALF)

    by_role(on_first, on_second)


def local_part(raw, inverse, direction):
    inv = inverse[...]
    unit = raw[...].astype(FULL) * inv
    along = jnp.sum(unit * direction, axis=1, keepdims=True)
    return (direction - unit * along) * inv


def third_kernel(
    far, params, row_targets, targets, image, text, mate_image, mate_text, got, mate_got,
    image_raw, image_inv, text_raw, text_inv, image_part, text_part,
):
    visit, far_text = parted(far, got)
    mate_visit, mate_far = parted(far, mate_got)
    nodes = far + 1

    def on_first(node):
        pairs = image_pairs(targets, node, nodes)
        texts = [text, *far_text, mate_text, *mate_far]
        direction = drawn(params, image, texts, pairs)
        image_part[...] = local_part(image_raw, image_inv, direction)
        pairs = text_pairs(row_targets, node)
        direction = drawn(params, text, [image, visit, mate_visit], pairs)
        text_part[...] = local_part(text_raw, text_inv, direction)

    def on_second(node):
        pairs = text_pairs(row_targets, node)
        direction = drawn(params, text, [image, mate_image, visit], pairs)
        text_part[...] = local_part(text_raw, text_inv, direction)
        pairs = image_pairs(targets, node, nodes)
        direction = drawn(params, image, [text, *far_text], pairs)
        image_part[...] = local_part(image_raw, image_inv, direction)

    by_role(on_first, on_second)


def finish(received, own, count, out, start, stop):
    raw, inverse, part = own
    step = 16 if (stop - start) % 16 == 0 else stop - start
    for at in range(start, stop, step):
        piece = pl.ds(at, step)
        gradient = received[0][piece, :].astype(FULL)
        for k in range(1, count):
            gradient += received[k][piece, :].astype(FULL)
        inv = inverse[piece, :]
        values = raw[piece, :].astype(FULL)
        along = jnp.sum(values * gradient, axis=1, keepdims=True) * (inv * inv * inv)
        out[piece, :] = gradient * inv - values * along + part[piece, :]


def fourth_kernel(far, *refs):
    image, text, received, ready = refs[0:3], refs[3:6], refs[6 : 6 + far], refs[6 + far]

    def run(own, count, node):
        finish(received, own, count, ready, 0, ready.shape[0])

    by_role(functools.partial(run, image, 1), functools.partial(run, text, far))


def last_kernel(far, ready, *refs):
    image, text, received = refs[0:3], refs[3:6], refs[6 : 6 + far]
    image_grads, text_grads, held, sems = refs[6 + far :]
    rows = held.shape[0]
    part = rows // 5 if rows % 80 == 0 else rows

    def run(own, count, ready_out, out, node):
        copies = [pltpu.make_async_copy(ready, ready_out, sems.at[0])]
        copies[0].start()
        for i, at in enumerate(range(0, rows, part)):
            finish(received, own, count, held, at, at + part)
            piece = pl.ds(at, part)
            copies.append(
                pltpu.make_async_copy(held.at[piece], out.at[piece], sems.at[i + 1])
            )
            copies[-1].start()
        for copy in copies:
            copy.wait()

    by_role(
        functools.partial(run, text, far, image_grads, text_grads),
        functools.partial(run, image, 1, text_grads, image_grads),
    )


def call(kernel, name, operands, shapes, anywhere=0, scratch=()):
    operands = list(operands)
    held = pl.BlockSpec(memory_space=pltpu.VMEM)
    for i in range(anywhere):
        operands[i] = pltpu.with_memory_space_constraint(operands[i], pltpu.HBM)
    return pl.pallas_call(
        kernel,
        name=name,
        out_shape=[pltpu.VMEM(s, d) for s, d in shapes],
        in_specs=[pl.BlockSpec(memory_space=pltpu.HBM)] * anywhere
        + [held] * (len(operands) - anywhere),
        out_specs=[held] * len(shapes),
        scratch_shapes=scratch,
        compiler_params=pltpu.CompilerParams(vmem_limit_bytes=VMEM_LIMIT),
    )(*operands)


def last(far, operands, block):
    anywhere = pl.BlockSpec(memory_space=pl.ANY)
    return pl.pallas_call(
        functools.partial(last_kernel, far),
        name="last",
        out_shape=[jax.ShapeDtypeStruct(*block)] * 2,
        in_specs=[pl.BlockSpec(memory_space=pltpu.VMEM)] * len(operands),
        out_specs=[anywhere] * 2,
        scratch_shapes=[pltpu.VMEM(*block), pltpu.SemaphoreType.DMA((6,))],
        compiler_params=pltpu.CompilerParams(vmem_limit_bytes=VMEM_LIMIT),
    )(*operands)


def local(image_embeds, text_embeds, pair_text, similarity_scale, logit_bias):
    rows, width = image_embeds.shape
    cycle_count = lax.axis_size("blk")
    node_count = lax.axis_size("node")
    far = node_count - 1

    def send(block, even, odd):
        route = []
        for g in range(cycle_count):
            ahead, across = odd if g % 2 else even
            for n in range(node_count):
                to = (g + ahead) % cycle_count * node_count + (n + across) % node_count
                route.append((g * node_count + n, to))
        return lax.ppermute(block, ("blk", "node"), route)

    def swap(block):
        return send(block, (1, 0), (-1, 0))

    stay = (0, 0)
    ahead, behind = (2, 0), (-2, 0)
    block_h = ((rows, width), HALF)
    block_f = ((rows, width), FULL)
    column = ((rows, 1), FULL)
    returns = ((far, rows, width), HALF)

    visit_raw = send(image_embeds, ahead, ahead)
    far_raw = [send(text_embeds, (0, -k), (0, -k)) for k in range(1, node_count)]

    image_raw, text_raw, image, text, image_inv, text_inv = call(
        unit_kernel,
        "unit",
        [image_embeds, text_embeds],
        [block_h, block_h, block_h, block_h, column, column],
        anywhere=2,
        scratch=[pltpu.SemaphoreType.DMA((2,))],
    )
    mate_image = swap(image)
    mate_text = swap(text)
    names = pair_text.reshape(-1, 128)
    params, row_targets, targets = call(
        prep_kernel,
        "prep",
        [names, similarity_scale[:, None], logit_bias[:, None], image_inv],
        [((8, 128), FULL), ((1, 3 * rows), jnp.int32), ((rows, 1), jnp.int32)],
        anywhere=1,
        scratch=[pltpu.VMEM(names.shape, jnp.int32), pltpu.SemaphoreType.DMA((1,))],
    )
    (visit,) = call(visit_kernel, "visit", [visit_raw, params], [block_h])
    *far_raw, visit = lax.optimization_barrier((*far_raw, visit))
    (got,) = call(
        functools.partial(got_kernel, far),
        "got",
        [visit, *far_raw, mate_image, mate_text],
        [((node_count, rows, width), HALF)],
    )
    back, part = call(
        functools.partial(first_kernel, far),
        "first",
        [params, row_targets, image, text, mate_image, mate_text, got],
        [returns, block_f],
    )
    got, part = lax.optimization_barrier((got, part))
    mate_got = swap(got)
    one = [send(back[k], behind if k == 0 else stay, (0, k + 1)) for k in range(far)]
    (back,) = call(
        functools.partial(second_kernel, far),
        "second",
        [params, row_targets, image, got, mate_got, part],
        [returns],
    )
    two = [send(back[k], (0, k + 1), behind if k == 0 else stay) for k in range(far)]
    image_part, text_part = call(
        functools.partial(third_kernel, far),
        "third",
        [params, row_targets, targets, image, text, mate_image, mate_text, got, mate_got]
        + [image_raw, image_inv, text_raw, text_inv],
        [block_f, block_f],
    )
    own = [image_raw, image_inv, image_part, text_raw, text_inv, text_part]
    (ready,) = call(
        functools.partial(fourth_kernel, far), "fourth", [*own, *one], [block_f]
    )
    return tuple(last(far, [ready, *own, *two], block_f))


def solution(mesh):
    return jax.shard_map(
        local,
        mesh=mesh,
        in_specs=(P(("blk", "node"), None), P(("blk", "node"), None), P(), P(), P()),
        out_specs=(P(("blk", "node"), None), P(("blk", "node"), None)),
        check_vma=False,
    )
```

```python
import functools
import math

import jax
import jax.numpy as jnp
from jax import lax
from jax.experimental import pallas as pl
from jax.experimental.pallas import tpu as pltpu
from jax.sharding import PartitionSpec as P

HALF = jnp.bfloat16
FULL = jnp.float32
VMEM_LIMIT = 8 * 1024 * 1024


def roles():
    return lax.rem(lax.axis_index("blk"), 2) == 0, lax.axis_index("node")


def by_role(on_first, on_second):
    first, node = roles()
    pl.when(first)(functools.partial(on_first, node))
    pl.when(jnp.logical_not(first))(functools.partial(on_second, node))


def drawn(params, rows, partners, paired=None):
    vectors = jnp.concatenate([partner[...] for partner in partners], axis=0)
    dots = lax.dot_general(
        rows[...], vectors, (((1,), (1,)), ((), ())), preferred_element_type=FULL
    )
    scale, bias = params[0:1, 0:1], params[1:2, 0:1]
    logits = scale * dots + bias
    if paired is None:
        weights = scale * jax.nn.sigmoid(logits)
    else:
        pairs = paired(logits.shape)
        weights = jnp.where(pairs, -scale, scale) * jax.nn.sigmoid(
            jnp.where(pairs, -logits, logits)
        )
    return jnp.dot(weights.astype(HALF), vectors, preferred_element_type=FULL)


def drawn_apart(params, rows, partners):
    scale, bias = params[0:1, 0:1], params[1:2, 0:1]
    dots = [
        lax.dot_general(
            rows[...], partner[...], (((1,), (1,)), ((), ())), preferred_element_type=FULL
        )
        for partner in partners
    ]
    weights = [(scale * jax.nn.sigmoid(scale * dot + bias)).astype(HALF) for dot in dots]
    total = None
    for weight, partner in zip(weights, partners):
        term = jnp.dot(weight, partner[...], preferred_element_type=FULL)
        total = term if total is None else total + term
    return total


def text_pairs(targets, node):
    def paired(shape):
        rows = shape[0]
        names = lax.broadcasted_iota(jnp.int32, shape, 0) + node * rows
        return names == targets[:, : shape[1]]

    return paired


def image_pairs(targets, node, nodes):
    def paired(shape):
        rows = shape[0]
        columns = lax.broadcasted_iota(jnp.int32, shape, 1)
        names = jnp.where(columns < nodes * rows, columns, -1 - nodes * rows)
        for k in range(nodes):
            here = jnp.logical_and(columns >= k * rows, columns < (k + 1) * rows)
            shift = (lax.rem(node + k, nodes) - k) * rows
            names = jnp.where(here, columns + shift, names)
        return names == targets[...]

    return paired


def inverse_of(values):
    return lax.rsqrt(jnp.sum(values * values, axis=1, keepdims=True) + 1e-06)


def half_rows(raw):
    values = raw[...].astype(FULL)
    return (values * inverse_of(values)).astype(HALF)


def unit_kernel(
    image, text, image_raw, text_raw, image_half, text_half, image_inv, text_inv, sems
):
    blocks = ((image, image_raw, image_half, image_inv), (text, text_raw, text_half, text_inv))
    copies = [
        pltpu.make_async_copy(source, raw, sems.at[i])
        for i, (source, raw, _, _) in enumerate(blocks)
    ]
    for copy in copies:
        copy.start()
    for copy, (_, raw, half, inv) in zip(copies, blocks):
        copy.wait()
        values = raw[...].astype(FULL)
        inverse = inverse_of(values)
        half[...] = (values * inverse).astype(HALF)
        inv[...] = inverse


def prep_kernel(
    names, scale, bias, after, params, row_targets, targets, held, sems
):
    copy = pltpu.make_async_copy(names, held, sems.at[0])
    copy.start()
    row = lax.broadcasted_iota(jnp.int32, params.shape, 0)
    params[...] = jnp.where(row == 0, scale[...], bias[...])
    copy.wait()

    rows = targets.shape[0]
    group, node = lax.axis_index("blk"), lax.axis_index("node")
    nodes = lax.axis_size("node")
    start = (group * nodes + node) * rows
    step = math.gcd(rows, 128)
    lines = -(-(128 - step + rows) // 128)
    window = held[pl.ds(start // 128, lines), :]
    window = jnp.concatenate([window[i : i + 1] for i in range(lines)], axis=1)
    mine = window[:, :rows]
    for at in range(step, 128, step):
        mine = jnp.where(lax.rem(start, 128) == at, window[:, at : at + rows], mine)
    mine = mine - group * nodes * rows
    row_targets[...] = jnp.full(row_targets.shape, -1, jnp.int32)
    row_targets[:, :rows] = mine
    square = (rows, rows)
    same = lax.broadcasted_iota(jnp.int32, square, 0) == lax.broadcasted_iota(
        jnp.int32, square, 1
    )
    turned = jnp.sum(jnp.where(same, mine.astype(FULL), 0.0), axis=1, keepdims=True)
    targets[...] = turned.astype(jnp.int32)


def visit_kernel(raw, after, half):
    half[...] = half_rows(raw)


def got_kernel(far, visit, *refs):
    got = refs[-1]
    got[0] = visit[...]
    for k in range(far):
        got[k + 1] = half_rows(refs[k])


def parted(far, got):
    return got.at[0], [got.at[k + 1] for k in range(far)]


def first_kernel(
    far, params, row_targets, image, text, mate_image, mate_text, got, back, part
):
    visit, far_text = parted(far, got)

    def on_first(node):
        back[0] = drawn_apart(params, visit, [text, *far_text]).astype(HALF)

    def on_second(node):
        for k in range(far):
            pairs = text_pairs(row_targets, lax.rem(node + k + 1, far + 1))
            images = [image, mate_image, visit]
            back[k] = drawn(params, far_text[k], images, pairs).astype(HALF)
        part[...] = drawn(params, visit, [text, *far_text, mate_text])

    by_role(on_first, on_second)


def second_kernel(far, params, row_targets, image, got, mate_got, part, back):
    visit, far_text = parted(far, got)
    mate_visit, mate_far = parted(far, mate_got)

    def on_first(node):
        for k in range(far):
            pairs = text_pairs(row_targets, lax.rem(node + k + 1, far + 1))
            images = [image, visit, mate_visit]
            back[k] = drawn(params, far_text[k], images, pairs).astype(HALF)

    def on_second(node):
        back[0] = (part[...] + drawn(params, visit, mate_far)).astype(HALF)

    by_role(on_first, on_second)


def local_part(raw, inverse, direction):
    inv = inverse[...]
    unit = raw[...].astype(FULL) * inv
    along = jnp.sum(unit * direction, axis=1, keepdims=True)
    return (direction - unit * along) * inv


def third_kernel(
    far, params, row_targets, targets, image, text, mate_image, mate_text, got, mate_got,
    image_raw, image_inv, text_raw, text_inv, image_part, text_part,
):
    visit, far_text = parted(far, got)
    mate_visit, mate_far = parted(far, mate_got)
    nodes = far + 1

    def on_first(node):
        pairs = image_pairs(targets, node, nodes)
        texts = [text, *far_text, mate_text, *mate_far]
        direction = drawn(params, image, texts, pairs)
        image_part[...] = local_part(image_raw, image_inv, direction)
        pairs = text_pairs(row_targets, node)
        direction = drawn(params, text, [image, visit, mate_visit], pairs)
        text_part[...] = local_part(text_raw, text_inv, direction)

    def on_second(node):
        pairs = text_pairs(row_targets, node)
        direction = drawn(params, text, [image, mate_image, visit], pairs)
        text_part[...] = local_part(text_raw, text_inv, direction)
        pairs = image_pairs(targets, node, nodes)
        direction = drawn(params, image, [text, *far_text], pairs)
        image_part[...] = local_part(image_raw, image_inv, direction)

    by_role(on_first, on_second)


def finish(received, own, count, out, start, stop):
    raw, inverse, part = own
    step = 16 if (stop - start) % 16 == 0 else stop - start
    for at in range(start, stop, step):
        piece = pl.ds(at, step)
        gradient = received[0][piece, :].astype(FULL)
        for k in range(1, count):
            gradient += received[k][piece, :].astype(FULL)
        inv = inverse[piece, :]
        values = raw[piece, :].astype(FULL)
        along = jnp.sum(values * gradient, axis=1, keepdims=True) * (inv * inv * inv)
        out[piece, :] = gradient * inv - values * along + part[piece, :]


def out_kernel(far, image_on_first, *refs):
    image, text, received = refs[0:3], refs[3:6], refs[6 : 6 + far]
    image_grads, text_grads, held, sems = refs[-4:]
    rows = held.shape[0]
    part = rows // 5 if rows % 80 == 0 else rows

    def run(own, count, out, node):
        copies = []
        for i, at in enumerate(range(0, rows, part)):
            finish(received, own, count, held, at, at + part)
            piece = pl.ds(at, part)
            copies.append(pltpu.make_async_copy(held.at[piece], out.at[piece], sems.at[i]))
            copies[-1].start()
        for copy in copies:
            copy.wait()

    on_images = functools.partial(run, image, 1, image_grads)
    on_texts = functools.partial(run, text, far, text_grads)
    if image_on_first:
        by_role(on_images, on_texts)
    else:
        by_role(on_texts, on_images)


def call(kernel, name, operands, shapes, anywhere=0, scratch=()):
    operands = list(operands)
    held = pl.BlockSpec(memory_space=pltpu.VMEM)
    for i in range(anywhere):
        operands[i] = pltpu.with_memory_space_constraint(operands[i], pltpu.HBM)
    return pl.pallas_call(
        kernel,
        name=name,
        out_shape=[pltpu.VMEM(s, d) for s, d in shapes],
        in_specs=[pl.BlockSpec(memory_space=pltpu.HBM)] * anywhere
        + [held] * (len(operands) - anywhere),
        out_specs=[held] * len(shapes),
        scratch_shapes=scratch,
        compiler_params=pltpu.CompilerParams(vmem_limit_bytes=VMEM_LIMIT),
    )(*operands)


def write_out(far, image_on_first, operands, grads, block):
    anywhere = pl.BlockSpec(memory_space=pl.ANY)
    count = len(operands)
    return pl.pallas_call(
        functools.partial(out_kernel, far, image_on_first),
        name="out",
        out_shape=[jax.ShapeDtypeStruct(*block)] * 2,
        in_specs=[pl.BlockSpec(memory_space=pltpu.VMEM)] * count + [anywhere] * len(grads),
        out_specs=[anywhere] * 2,
        scratch_shapes=[pltpu.VMEM(*block), pltpu.SemaphoreType.DMA((5,))],
        input_output_aliases={count + i: i for i in range(len(grads))},
        compiler_params=pltpu.CompilerParams(vmem_limit_bytes=VMEM_LIMIT),
    )(*operands, *grads)


def local(image_embeds, text_embeds, pair_text, similarity_scale, logit_bias):
    rows, width = image_embeds.shape
    cycle_count = lax.axis_size("blk")
    node_count = lax.axis_size("node")
    far = node_count - 1

    def send(block, even, odd):
        route = []
        for g in range(cycle_count):
            ahead, across = odd if g % 2 else even
            for n in range(node_count):
                to = (g + ahead) % cycle_count * node_count + (n + across) % node_count
                route.append((g * node_count + n, to))
        return lax.ppermute(block, ("blk", "node"), route)

    def swap(block):
        return send(block, (1, 0), (-1, 0))

    stay = (0, 0)
    ahead, behind = (2, 0), (-2, 0)
    block_h = ((rows, width), HALF)
    block_f = ((rows, width), FULL)
    column = ((rows, 1), FULL)
    returns = ((far, rows, width), HALF)

    visit_raw = send(image_embeds, ahead, ahead)
    far_raw = [send(text_embeds, (0, -k), (0, -k)) for k in range(1, node_count)]

    image_raw, text_raw, image, text, image_inv, text_inv = call(
        unit_kernel,
        "unit",
        [image_embeds, text_embeds],
        [block_h, block_h, block_h, block_h, column, column],
        anywhere=2,
        scratch=[pltpu.SemaphoreType.DMA((2,))],
    )
    mate_image = swap(image)
    mate_text = swap(text)
    names = pair_text.reshape(-1, 128)
    params, row_targets, targets = call(
        prep_kernel,
        "prep",
        [names, similarity_scale[:, None], logit_bias[:, None], image_inv],
        [((8, 128), FULL), ((1, 3 * rows), jnp.int32), ((rows, 1), jnp.int32)],
        anywhere=1,
        scratch=[pltpu.VMEM(names.shape, jnp.int32), pltpu.SemaphoreType.DMA((1,))],
    )
    (visit,) = call(visit_kernel, "visit", [visit_raw, params], [block_h])
    *far_raw, visit = lax.optimization_barrier((*far_raw, visit))
    (got,) = call(
        functools.partial(got_kernel, far),
        "got",
        [visit, *far_raw, mate_image, mate_text],
        [((node_count, rows, width), HALF)],
    )
    back, part = call(
        functools.partial(first_kernel, far),
        "first",
        [params, row_targets, image, text, mate_image, mate_text, got],
        [returns, block_f],
    )
    got, part = lax.optimization_barrier((got, part))
    mate_got = swap(got)
    one = [send(back[k], behind if k == 0 else stay, (0, k + 1)) for k in range(far)]
    (back,) = call(
        functools.partial(second_kernel, far),
        "second",
        [params, row_targets, image, got, mate_got, part],
        [returns],
    )
    two = [send(back[k], (0, k + 1), behind if k == 0 else stay) for k in range(far)]
    image_part, text_part = call(
        functools.partial(third_kernel, far),
        "third",
        [params, row_targets, targets, image, text, mate_image, mate_text, got, mate_got]
        + [image_raw, image_inv, text_raw, text_inv],
        [block_f, block_f],
    )
    own = [image_raw, image_inv, image_part, text_raw, text_inv, text_part]
    grads = write_out(far, True, [*own, *one], [], block_f)
    return tuple(write_out(far, False, [*own, *two], grads, block_f))


def solution(mesh):
    return jax.shard_map(
        local,
        mesh=mesh,
        in_specs=(P(("blk", "node"), None), P(("blk", "node"), None), P(), P(), P()),
        out_specs=(P(("blk", "node"), None), P(("blk", "node"), None)),
        check_vma=False,
    )
```

```python
import functools
import math

import jax
import jax.numpy as jnp
from jax import lax
from jax.experimental import pallas as pl
from jax.experimental.pallas import tpu as pltpu
from jax.sharding import PartitionSpec as P

HALF = jnp.bfloat16
FULL = jnp.float32
VMEM_LIMIT = 8 * 1024 * 1024


def roles():
    return lax.rem(lax.axis_index("blk"), 2) == 0, lax.axis_index("node")


def by_role(on_first, on_second):
    first, node = roles()
    pl.when(first)(functools.partial(on_first, node))
    pl.when(jnp.logical_not(first))(functools.partial(on_second, node))


def drawn(params, rows, partners, paired=None):
    vectors = jnp.concatenate([partner[...] for partner in partners], axis=0)
    dots = lax.dot_general(
        rows[...], vectors, (((1,), (1,)), ((), ())), preferred_element_type=FULL
    )
    scale, bias = params[0:1, 0:1], params[1:2, 0:1]
    logits = scale * dots + bias
    if paired is None:
        weights = scale * jax.nn.sigmoid(logits)
    else:
        pairs = paired(logits.shape)
        weights = jnp.where(pairs, -scale, scale) * jax.nn.sigmoid(
            jnp.where(pairs, -logits, logits)
        )
    return jnp.dot(weights.astype(HALF), vectors, preferred_element_type=FULL)


def drawn_apart(params, rows, partners, paired=()):
    scale, bias = params[0:1, 0:1], params[1:2, 0:1]
    weights = []
    for i, partner in enumerate(partners):
        dots = lax.dot_general(
            rows[...], partner[...], (((1,), (1,)), ((), ())), preferred_element_type=FULL
        )
        logits = scale * dots + bias
        if i < len(paired):
            pairs = paired[i](logits.shape)
            weight = jnp.where(pairs, -scale, scale) * jax.nn.sigmoid(
                jnp.where(pairs, -logits, logits)
            )
        else:
            weight = scale * jax.nn.sigmoid(logits)
        weights.append(weight.astype(HALF))
    total = None
    for weight, partner in zip(weights, partners):
        term = jnp.dot(weight, partner[...], preferred_element_type=FULL)
        total = term if total is None else total + term
    return total


def own_pairs(targets, node):
    def paired(shape):
        return lax.broadcasted_iota(jnp.int32, shape, 0) + node * shape[0] == (
            targets[:, : shape[1]]
        )

    return [paired]


def text_pairs(targets, node):
    def paired(shape):
        rows = shape[0]
        names = lax.broadcasted_iota(jnp.int32, shape, 0) + node * rows
        return names == targets[:, : shape[1]]

    return paired


def image_pairs(targets, node, nodes):
    def paired(shape):
        rows = shape[0]
        columns = lax.broadcasted_iota(jnp.int32, shape, 1)
        names = jnp.where(columns < nodes * rows, columns, -1 - nodes * rows)
        for k in range(nodes):
            here = jnp.logical_and(columns >= k * rows, columns < (k + 1) * rows)
            shift = (lax.rem(node + k, nodes) - k) * rows
            names = jnp.where(here, columns + shift, names)
        return names == targets[...]

    return paired


def inverse_of(values):
    return lax.rsqrt(jnp.sum(values * values, axis=1, keepdims=True) + 1e-06)


def half_rows(raw):
    values = raw[...].astype(FULL)
    return (values * inverse_of(values)).astype(HALF)


def unit_kernel(
    image, text, image_raw, text_raw, image_half, text_half, image_inv, text_inv, sems
):
    blocks = ((image, image_raw, image_half, image_inv), (text, text_raw, text_half, text_inv))
    copies = [
        pltpu.make_async_copy(source, raw, sems.at[i])
        for i, (source, raw, _, _) in enumerate(blocks)
    ]
    for copy in copies:
        copy.start()
    for copy, (_, raw, half, inv) in zip(copies, blocks):
        copy.wait()
        values = raw[...].astype(FULL)
        inverse = inverse_of(values)
        half[...] = (values * inverse).astype(HALF)
        inv[...] = inverse


def prep_kernel(
    names, scale, bias, after, params, row_targets, targets, held, sems
):
    copy = pltpu.make_async_copy(names, held, sems.at[0])
    copy.start()
    row = lax.broadcasted_iota(jnp.int32, params.shape, 0)
    params[...] = jnp.where(row == 0, scale[...], bias[...])
    copy.wait()

    rows = targets.shape[0]
    group, node = lax.axis_index("blk"), lax.axis_index("node")
    nodes = lax.axis_size("node")
    start = (group * nodes + node) * rows
    step = math.gcd(rows, 128)
    lines = -(-(128 - step + rows) // 128)
    window = held[pl.ds(start // 128, lines), :]
    window = jnp.concatenate([window[i : i + 1] for i in range(lines)], axis=1)
    mine = window[:, :rows]
    for at in range(step, 128, step):
        mine = jnp.where(lax.rem(start, 128) == at, window[:, at : at + rows], mine)
    mine = mine - group * nodes * rows
    row_targets[...] = jnp.full(row_targets.shape, -1, jnp.int32)
    row_targets[:, :rows] = mine
    square = (rows, rows)
    same = lax.broadcasted_iota(jnp.int32, square, 0) == lax.broadcasted_iota(
        jnp.int32, square, 1
    )
    turned = jnp.sum(jnp.where(same, mine.astype(FULL), 0.0), axis=1, keepdims=True)
    targets[...] = turned.astype(jnp.int32)


def visit_kernel(raw, after, half):
    half[...] = half_rows(raw)


def got_kernel(far, visit, *refs):
    got = refs[-1]
    got[0] = visit[...]
    for k in range(far):
        got[k + 1] = half_rows(refs[k])


def parted(far, got):
    return got.at[0], [got.at[k + 1] for k in range(far)]


def first_kernel(
    far, params, row_targets, image, text, mate_image, mate_text, got, back, part
):
    visit, far_text = parted(far, got)

    def on_first(node):
        back[0] = drawn_apart(params, visit, [text, *far_text]).astype(HALF)

    def on_second(node):
        for k in range(far):
            pairs = text_pairs(row_targets, lax.rem(node + k + 1, far + 1))
            images = [image, mate_image, visit]
            back[k] = drawn(params, far_text[k], images, pairs).astype(HALF)
        part[...] = drawn(params, visit, [text, *far_text, mate_text])

    by_role(on_first, on_second)


def middle_kernel(far, params, row_targets, image, got, begun, sums):
    visit, far_text = parted(far, got)

    def on_first(node):
        for k in range(far):
            pairs = own_pairs(row_targets, lax.rem(node + k + 1, far + 1))
            sums[k] = drawn_apart(params, far_text[k], [image, visit], pairs)

    def on_second(node):
        pass

    by_role(on_first, on_second)


def second_kernel(far, params, got, mate_got, part, sums, back):
    visit, far_text = parted(far, got)
    mate_visit, mate_far = parted(far, mate_got)

    def on_first(node):
        for k in range(far):
            total = sums[k] + drawn_apart(params, far_text[k], [mate_visit])
            back[k] = total.astype(HALF)

    def on_second(node):
        back[0] = (part[...] + drawn_apart(params, visit, mate_far)).astype(HALF)

    by_role(on_first, on_second)


def local_part(raw, inverse, direction):
    inv = inverse[...]
    unit = raw[...].astype(FULL) * inv
    along = jnp.sum(unit * direction, axis=1, keepdims=True)
    return (direction - unit * along) * inv


def third_kernel(
    far, params, row_targets, targets, image, text, mate_image, mate_text, got, mate_got,
    image_raw, image_inv, text_raw, text_inv, image_part, text_part,
):
    visit, far_text = parted(far, got)
    mate_visit, mate_far = parted(far, mate_got)
    nodes = far + 1

    def on_first(node):
        pairs = image_pairs(targets, node, nodes)
        texts = [text, *far_text, mate_text, *mate_far]
        direction = drawn(params, image, texts, pairs)
        image_part[...] = local_part(image_raw, image_inv, direction)
        pairs = text_pairs(row_targets, node)
        direction = drawn(params, text, [image, visit, mate_visit], pairs)
        text_part[...] = local_part(text_raw, text_inv, direction)

    def on_second(node):
        pairs = text_pairs(row_targets, node)
        direction = drawn(params, text, [image, mate_image, visit], pairs)
        text_part[...] = local_part(text_raw, text_inv, direction)
        pairs = image_pairs(targets, node, nodes)
        direction = drawn(params, image, [text, *far_text], pairs)
        image_part[...] = local_part(image_raw, image_inv, direction)

    by_role(on_first, on_second)


def finish(received, own, count, out, start, stop):
    raw, inverse, part = own
    step = 16 if (stop - start) % 16 == 0 else stop - start
    for at in range(start, stop, step):
        piece = pl.ds(at, step)
        gradient = received[0][piece, :].astype(FULL)
        for k in range(1, count):
            gradient += received[k][piece, :].astype(FULL)
        inv = inverse[piece, :]
        values = raw[piece, :].astype(FULL)
        along = jnp.sum(values * gradient, axis=1, keepdims=True) * (inv * inv * inv)
        out[piece, :] = gradient * inv - values * along + part[piece, :]


def out_kernel(far, image_on_first, *refs):
    image, text, received = refs[0:3], refs[3:6], refs[6 : 6 + far]
    image_grads, text_grads, held, sems = refs[-4:]
    rows = held.shape[0]
    part = rows // 5 if rows % 80 == 0 else rows

    def run(own, count, out, node):
        copies = []
        for i, at in enumerate(range(0, rows, part)):
            finish(received, own, count, held, at, at + part)
            piece = pl.ds(at, part)
            copies.append(pltpu.make_async_copy(held.at[piece], out.at[piece], sems.at[i]))
            copies[-1].start()
        for copy in copies:
            copy.wait()

    on_images = functools.partial(run, image, 1, image_grads)
    on_texts = functools.partial(run, text, far, text_grads)
    if image_on_first:
        by_role(on_images, on_texts)
    else:
        by_role(on_texts, on_images)


def call(kernel, name, operands, shapes, anywhere=0, scratch=()):
    operands = list(operands)
    held = pl.BlockSpec(memory_space=pltpu.VMEM)
    for i in range(anywhere):
        operands[i] = pltpu.with_memory_space_constraint(operands[i], pltpu.HBM)
    return pl.pallas_call(
        kernel,
        name=name,
        out_shape=[pltpu.VMEM(s, d) for s, d in shapes],
        in_specs=[pl.BlockSpec(memory_space=pltpu.HBM)] * anywhere
        + [held] * (len(operands) - anywhere),
        out_specs=[held] * len(shapes),
        scratch_shapes=scratch,
        compiler_params=pltpu.CompilerParams(vmem_limit_bytes=VMEM_LIMIT),
    )(*operands)


def write_out(far, image_on_first, operands, grads, block):
    anywhere = pl.BlockSpec(memory_space=pl.ANY)
    count = len(operands)
    return pl.pallas_call(
        functools.partial(out_kernel, far, image_on_first),
        name="out",
        out_shape=[jax.ShapeDtypeStruct(*block)] * 2,
        in_specs=[pl.BlockSpec(memory_space=pltpu.VMEM)] * count + [anywhere] * len(grads),
        out_specs=[anywhere] * 2,
        scratch_shapes=[pltpu.VMEM(*block), pltpu.SemaphoreType.DMA((5,))],
        input_output_aliases={count + i: i for i in range(len(grads))},
        compiler_params=pltpu.CompilerParams(vmem_limit_bytes=VMEM_LIMIT),
    )(*operands, *grads)


def local(image_embeds, text_embeds, pair_text, similarity_scale, logit_bias):
    rows, width = image_embeds.shape
    cycle_count = lax.axis_size("blk")
    node_count = lax.axis_size("node")
    far = node_count - 1

    def send(block, even, odd):
        route = []
        for g in range(cycle_count):
            ahead, across = odd if g % 2 else even
            for n in range(node_count):
                to = (g + ahead) % cycle_count * node_count + (n + across) % node_count
                route.append((g * node_count + n, to))
        return lax.ppermute(block, ("blk", "node"), route)

    def swap(block):
        return send(block, (1, 0), (-1, 0))

    stay = (0, 0)
    ahead, behind = (2, 0), (-2, 0)
    block_h = ((rows, width), HALF)
    block_f = ((rows, width), FULL)
    column = ((rows, 1), FULL)
    returns = ((far, rows, width), HALF)

    visit_raw = send(image_embeds, ahead, ahead)
    far_raw = [send(text_embeds, (0, -k), (0, -k)) for k in range(1, node_count)]

    image_raw, text_raw, image, text, image_inv, text_inv = call(
        unit_kernel,
        "unit",
        [image_embeds, text_embeds],
        [block_h, block_h, block_h, block_h, column, column],
        anywhere=2,
        scratch=[pltpu.SemaphoreType.DMA((2,))],
    )
    mate_image = swap(image)
    mate_text = swap(text)
    names = pair_text.reshape(-1, 128)
    params, row_targets, targets = call(
        prep_kernel,
        "prep",
        [names, similarity_scale[:, None], logit_bias[:, None], image_inv],
        [((8, 128), FULL), ((1, 3 * rows), jnp.int32), ((rows, 1), jnp.int32)],
        anywhere=1,
        scratch=[pltpu.VMEM(names.shape, jnp.int32), pltpu.SemaphoreType.DMA((1,))],
    )
    (visit,) = call(visit_kernel, "visit", [visit_raw, params], [block_h])
    *far_raw, visit = lax.optimization_barrier((*far_raw, visit))
    (got,) = call(
        functools.partial(got_kernel, far),
        "got",
        [visit, *far_raw, mate_image, mate_text],
        [((node_count, rows, width), HALF)],
    )
    back, part = call(
        functools.partial(first_kernel, far),
        "first",
        [params, row_targets, image, text, mate_image, mate_text, got],
        [returns, block_f],
    )
    got, part = lax.optimization_barrier((got, part))
    mate_got = swap(got)
    one = [send(back[k], behind if k == 0 else stay, (0, k + 1)) for k in range(far)]
    (sums,) = call(
        functools.partial(middle_kernel, far),
        "middle",
        [params, row_targets, image, got, part],
        [((far, rows, width), FULL)],
    )
    (back,) = call(
        functools.partial(second_kernel, far),
        "second",
        [params, got, mate_got, part, sums],
        [returns],
    )
    two = [send(back[k], (0, k + 1), behind if k == 0 else stay) for k in range(far)]
    image_part, text_part = call(
        functools.partial(third_kernel, far),
        "third",
        [params, row_targets, targets, image, text, mate_image, mate_text, got, mate_got]
        + [image_raw, image_inv, text_raw, text_inv],
        [block_f, block_f],
    )
    own = [image_raw, image_inv, image_part, text_raw, text_inv, text_part]
    grads = write_out(far, True, [*own, *one], [], block_f)
    return tuple(write_out(far, False, [*own, *two], grads, block_f))


def solution(mesh):
    return jax.shard_map(
        local,
        mesh=mesh,
        in_specs=(P(("blk", "node"), None), P(("blk", "node"), None), P(), P(), P()),
        out_specs=(P(("blk", "node"), None), P(("blk", "node"), None)),
        check_vma=False,
    )
```

```python
import functools
import math

import jax
import jax.numpy as jnp
from jax import lax
from jax.experimental import pallas as pl
from jax.experimental.pallas import tpu as pltpu
from jax.sharding import PartitionSpec as P

HALF = jnp.bfloat16
FULL = jnp.float32
VMEM_LIMIT = 8 * 1024 * 1024


def roles():
    return lax.rem(lax.axis_index("blk"), 2) == 0, lax.axis_index("node")


def by_role(on_first, on_second):
    first, node = roles()
    pl.when(first)(functools.partial(on_first, node))
    pl.when(jnp.logical_not(first))(functools.partial(on_second, node))


def drawn(params, rows, partners, paired=None):
    vectors = jnp.concatenate([partner[...] for partner in partners], axis=0)
    dots = lax.dot_general(
        rows[...], vectors, (((1,), (1,)), ((), ())), preferred_element_type=FULL
    )
    scale, bias = params[0:1, 0:1], params[1:2, 0:1]
    logits = scale * dots + bias
    if paired is None:
        weights = scale * jax.nn.sigmoid(logits)
    else:
        pairs = paired(logits.shape)
        weights = jnp.where(pairs, -scale, scale) * jax.nn.sigmoid(
            jnp.where(pairs, -logits, logits)
        )
    return jnp.dot(weights.astype(HALF), vectors, preferred_element_type=FULL)


def drawn_apart(params, rows, partners):
    scale, bias = params[0:1, 0:1], params[1:2, 0:1]
    dots = [
        lax.dot_general(
            rows[...], partner[...], (((1,), (1,)), ((), ())), preferred_element_type=FULL
        )
        for partner in partners
    ]
    weights = [(scale * jax.nn.sigmoid(scale * dot + bias)).astype(HALF) for dot in dots]
    total = None
    for weight, partner in zip(weights, partners):
        term = jnp.dot(weight, partner[...], preferred_element_type=FULL)
        total = term if total is None else total + term
    return total


def text_pairs(targets, node):
    def paired(shape):
        rows = shape[0]
        names = lax.broadcasted_iota(jnp.int32, shape, 0) + node * rows
        return names == targets[:, : shape[1]]

    return paired


def image_pairs(targets, node, nodes):
    def paired(shape):
        rows = shape[0]
        columns = lax.broadcasted_iota(jnp.int32, shape, 1)
        names = jnp.where(columns < nodes * rows, columns, -1 - nodes * rows)
        for k in range(nodes):
            here = jnp.logical_and(columns >= k * rows, columns < (k + 1) * rows)
            shift = (lax.rem(node + k, nodes) - k) * rows
            names = jnp.where(here, columns + shift, names)
        return names == targets[...]

    return paired


def inverse_of(values):
    return lax.rsqrt(jnp.sum(values * values, axis=1, keepdims=True) + 1e-06)


def half_rows(raw):
    values = raw[...].astype(FULL)
    return (values * inverse_of(values)).astype(HALF)


def unit_kernel(
    image, text, image_raw, text_raw, image_half, text_half, image_inv, text_inv, sems
):
    blocks = ((image, image_raw, image_half, image_inv), (text, text_raw, text_half, text_inv))
    copies = [
        pltpu.make_async_copy(source, raw, sems.at[i])
        for i, (source, raw, _, _) in enumerate(blocks)
    ]
    for copy in copies:
        copy.start()
    for copy, (_, raw, half, inv) in zip(copies, blocks):
        copy.wait()
        values = raw[...].astype(FULL)
        inverse = inverse_of(values)
        half[...] = (values * inverse).astype(HALF)
        inv[...] = inverse


def prep_kernel(
    names, scale, bias, after, params, row_targets, targets, held, sems
):
    copy = pltpu.make_async_copy(names, held, sems.at[0])
    copy.start()
    row = lax.broadcasted_iota(jnp.int32, params.shape, 0)
    params[...] = jnp.where(row == 0, scale[...], bias[...])
    copy.wait()

    rows = targets.shape[0]
    group, node = lax.axis_index("blk"), lax.axis_index("node")
    nodes = lax.axis_size("node")
    start = (group * nodes + node) * rows
    step = math.gcd(rows, 128)
    lines = -(-(128 - step + rows) // 128)
    window = held[pl.ds(start // 128, lines), :]
    window = jnp.concatenate([window[i : i + 1] for i in range(lines)], axis=1)
    mine = window[:, :rows]
    for at in range(step, 128, step):
        mine = jnp.where(lax.rem(start, 128) == at, window[:, at : at + rows], mine)
    mine = mine - group * nodes * rows
    row_targets[...] = jnp.full(row_targets.shape, -1, jnp.int32)
    row_targets[:, :rows] = mine
    square = (rows, rows)
    same = lax.broadcasted_iota(jnp.int32, square, 0) == lax.broadcasted_iota(
        jnp.int32, square, 1
    )
    turned = jnp.sum(jnp.where(same, mine.astype(FULL), 0.0), axis=1, keepdims=True)
    targets[...] = turned.astype(jnp.int32)


def visit_kernel(raw, after, half):
    half[...] = half_rows(raw)


def parted(far, got):
    return got.at[0], [got.at[k + 1] for k in range(far)]


def first_kernel(far, params, row_targets, image, text, mate_image, mate_text, visit, *refs):
    far_raw, (got, back, part) = refs[:far], refs[far:]
    _, far_text = parted(far, got)
    for k in range(far):
        far_text[k][...] = half_rows(far_raw[k])

    def on_first(node):
        back[0] = drawn_apart(params, visit, [text, *far_text]).astype(HALF)

    def on_second(node):
        for k in range(far):
            pairs = text_pairs(row_targets, lax.rem(node + k + 1, far + 1))
            images = [image, mate_image, visit]
            back[k] = drawn(params, far_text[k], images, pairs).astype(HALF)
        part[...] = drawn(params, visit, [text, *far_text, mate_text])

    by_role(on_first, on_second)
    got[0] = visit[...]


def second_kernel(far, params, row_targets, image, got, mate_got, part, back):
    visit, far_text = parted(far, got)
    mate_visit, mate_far = parted(far, mate_got)

    def on_first(node):
        for k in range(far):
            pairs = text_pairs(row_targets, lax.rem(node + k + 1, far + 1))
            images = [image, visit, mate_visit]
            back[k] = drawn(params, far_text[k], images, pairs).astype(HALF)

    def on_second(node):
        back[0] = (part[...] + drawn(params, visit, mate_far)).astype(HALF)

    by_role(on_first, on_second)


def local_part(raw, inverse, direction):
    inv = inverse[...]
    unit = raw[...].astype(FULL) * inv
    along = jnp.sum(unit * direction, axis=1, keepdims=True)
    return (direction - unit * along) * inv


def third_kernel(
    far, params, row_targets, targets, image, text, mate_image, mate_text, got, mate_got,
    image_raw, image_inv, text_raw, text_inv, image_part, text_part,
):
    visit, far_text = parted(far, got)
    mate_visit, mate_far = parted(far, mate_got)
    nodes = far + 1

    def on_first(node):
        pairs = image_pairs(targets, node, nodes)
        texts = [text, *far_text, mate_text, *mate_far]
        direction = drawn(params, image, texts, pairs)
        image_part[...] = local_part(image_raw, image_inv, direction)
        pairs = text_pairs(row_targets, node)
        direction = drawn(params, text, [image, visit, mate_visit], pairs)
        text_part[...] = local_part(text_raw, text_inv, direction)

    def on_second(node):
        pairs = text_pairs(row_targets, node)
        direction = drawn(params, text, [image, mate_image, visit], pairs)
        text_part[...] = local_part(text_raw, text_inv, direction)
        pairs = image_pairs(targets, node, nodes)
        direction = drawn(params, image, [text, *far_text], pairs)
        image_part[...] = local_part(image_raw, image_inv, direction)

    by_role(on_first, on_second)


def finish(received, own, count, out, start, stop):
    raw, inverse, part = own
    step = 16 if (stop - start) % 16 == 0 else stop - start
    for at in range(start, stop, step):
        piece = pl.ds(at, step)
        gradient = received[0][piece, :].astype(FULL)
        for k in range(1, count):
            gradient += received[k][piece, :].astype(FULL)
        inv = inverse[piece, :]
        values = raw[piece, :].astype(FULL)
        along = jnp.sum(values * gradient, axis=1, keepdims=True) * (inv * inv * inv)
        out[piece, :] = gradient * inv - values * along + part[piece, :]


def out_kernel(far, image_on_first, *refs):
    image, text, received = refs[0:3], refs[3:6], refs[6 : 6 + far]
    image_grads, text_grads, held, sems = refs[-4:]
    rows = held.shape[0]
    part = rows // 5 if rows % 80 == 0 else rows

    def run(own, count, out, node):
        copies = []
        for i, at in enumerate(range(0, rows, part)):
            finish(received, own, count, held, at, at + part)
            piece = pl.ds(at, part)
            copies.append(pltpu.make_async_copy(held.at[piece], out.at[piece], sems.at[i]))
            copies[-1].start()
        for copy in copies:
            copy.wait()

    on_images = functools.partial(run, image, 1, image_grads)
    on_texts = functools.partial(run, text, far, text_grads)
    if image_on_first:
        by_role(on_images, on_texts)
    else:
        by_role(on_texts, on_images)


def call(kernel, name, operands, shapes, anywhere=0, scratch=()):
    operands = list(operands)
    held = pl.BlockSpec(memory_space=pltpu.VMEM)
    for i in range(anywhere):
        operands[i] = pltpu.with_memory_space_constraint(operands[i], pltpu.HBM)
    return pl.pallas_call(
        kernel,
        name=name,
        out_shape=[pltpu.VMEM(s, d) for s, d in shapes],
        in_specs=[pl.BlockSpec(memory_space=pltpu.HBM)] * anywhere
        + [held] * (len(operands) - anywhere),
        out_specs=[held] * len(shapes),
        scratch_shapes=scratch,
        compiler_params=pltpu.CompilerParams(vmem_limit_bytes=VMEM_LIMIT),
    )(*operands)


def write_out(far, image_on_first, operands, grads, block):
    anywhere = pl.BlockSpec(memory_space=pl.ANY)
    count = len(operands)
    return pl.pallas_call(
        functools.partial(out_kernel, far, image_on_first),
        name="out",
        out_shape=[jax.ShapeDtypeStruct(*block)] * 2,
        in_specs=[pl.BlockSpec(memory_space=pltpu.VMEM)] * count + [anywhere] * len(grads),
        out_specs=[anywhere] * 2,
        scratch_shapes=[pltpu.VMEM(*block), pltpu.SemaphoreType.DMA((5,))],
        input_output_aliases={count + i: i for i in range(len(grads))},
        compiler_params=pltpu.CompilerParams(vmem_limit_bytes=VMEM_LIMIT),
    )(*operands, *grads)


def local(image_embeds, text_embeds, pair_text, similarity_scale, logit_bias):
    rows, width = image_embeds.shape
    cycle_count = lax.axis_size("blk")
    node_count = lax.axis_size("node")
    far = node_count - 1

    def send(block, even, odd):
        route = []
        for g in range(cycle_count):
            ahead, across = odd if g % 2 else even
            for n in range(node_count):
                to = (g + ahead) % cycle_count * node_count + (n + across) % node_count
                route.append((g * node_count + n, to))
        return lax.ppermute(block, ("blk", "node"), route)

    def swap(block):
        return send(block, (1, 0), (-1, 0))

    stay = (0, 0)
    ahead, behind = (2, 0), (-2, 0)
    block_h = ((rows, width), HALF)
    block_f = ((rows, width), FULL)
    column = ((rows, 1), FULL)
    returns = ((far, rows, width), HALF)

    visit_raw = send(image_embeds, ahead, ahead)
    far_raw = [send(text_embeds, (0, -k), (0, -k)) for k in range(1, node_count)]

    image_raw, text_raw, image, text, image_inv, text_inv = call(
        unit_kernel,
        "unit",
        [image_embeds, text_embeds],
        [block_h, block_h, block_h, block_h, column, column],
        anywhere=2,
        scratch=[pltpu.SemaphoreType.DMA((2,))],
    )
    mate_image = swap(image)
    mate_text = swap(text)
    names = pair_text.reshape(-1, 128)
    params, row_targets, targets = call(
        prep_kernel,
        "prep",
        [names, similarity_scale[:, None], logit_bias[:, None], image_inv],
        [((8, 128), FULL), ((1, 3 * rows), jnp.int32), ((rows, 1), jnp.int32)],
        anywhere=1,
        scratch=[pltpu.VMEM(names.shape, jnp.int32), pltpu.SemaphoreType.DMA((1,))],
    )
    (visit,) = call(visit_kernel, "visit", [visit_raw, params], [block_h])
    *far_raw, visit = lax.optimization_barrier((*far_raw, visit))
    got, back, part = call(
        functools.partial(first_kernel, far),
        "first",
        [params, row_targets, image, text, mate_image, mate_text, visit, *far_raw],
        [((node_count, rows, width), HALF), returns, block_f],
    )
    got, part = lax.optimization_barrier((got, part))
    mate_got = swap(got)
    one = [send(back[k], behind if k == 0 else stay, (0, k + 1)) for k in range(far)]
    (back,) = call(
        functools.partial(second_kernel, far),
        "second",
        [params, row_targets, image, got, mate_got, part],
        [returns],
    )
    two = [send(back[k], (0, k + 1), behind if k == 0 else stay) for k in range(far)]
    image_part, text_part = call(
        functools.partial(third_kernel, far),
        "third",
        [params, row_targets, targets, image, text, mate_image, mate_text, got, mate_got]
        + [image_raw, image_inv, text_raw, text_inv],
        [block_f, block_f],
    )
    own = [image_raw, image_inv, image_part, text_raw, text_inv, text_part]
    grads = write_out(far, True, [*own, *one], [], block_f)
    return tuple(write_out(far, False, [*own, *two], grads, block_f))


def solution(mesh):
    return jax.shard_map(
        local,
        mesh=mesh,
        in_specs=(P(("blk", "node"), None), P(("blk", "node"), None), P(), P(), P()),
        out_specs=(P(("blk", "node"), None), P(("blk", "node"), None)),
        check_vma=False,
    )
```

```python
import functools
import math

import jax
import jax.numpy as jnp
from jax import lax
from jax.experimental import pallas as pl
from jax.experimental.pallas import tpu as pltpu
from jax.sharding import PartitionSpec as P

HALF = jnp.bfloat16
FULL = jnp.float32
VMEM_LIMIT = 8 * 1024 * 1024


def roles():
    return lax.rem(lax.axis_index("blk"), 2) == 0, lax.axis_index("node")


def by_role(on_first, on_second):
    first, node = roles()
    pl.when(first)(functools.partial(on_first, node))
    pl.when(jnp.logical_not(first))(functools.partial(on_second, node))


def drawn(params, rows, partners, paired=None):
    vectors = jnp.concatenate([partner[...] for partner in partners], axis=0)
    dots = lax.dot_general(
        rows[...], vectors, (((1,), (1,)), ((), ())), preferred_element_type=FULL
    )
    scale, bias = params[0:1, 0:1], params[1:2, 0:1]
    logits = scale * dots + bias
    if paired is None:
        weights = scale * jax.nn.sigmoid(logits)
    else:
        pairs = paired(logits.shape)
        weights = jnp.where(pairs, -scale, scale) * jax.nn.sigmoid(
            jnp.where(pairs, -logits, logits)
        )
    return jnp.dot(weights.astype(HALF), vectors, preferred_element_type=FULL)


def drawn_apart(params, rows, partners):
    scale, bias = params[0:1, 0:1], params[1:2, 0:1]
    dots = [
        lax.dot_general(
            rows[...], partner[...], (((1,), (1,)), ((), ())), preferred_element_type=FULL
        )
        for partner in partners
    ]
    weights = [(scale * jax.nn.sigmoid(scale * dot + bias)).astype(HALF) for dot in dots]
    total = None
    for weight, partner in zip(weights, partners):
        term = jnp.dot(weight, partner[...], preferred_element_type=FULL)
        total = term if total is None else total + term
    return total


def text_pairs(targets, node):
    def paired(shape):
        rows = shape[0]
        names = lax.broadcasted_iota(jnp.int32, shape, 0) + node * rows
        return names == targets[:, : shape[1]]

    return paired


def image_pairs(targets, node, nodes):
    def paired(shape):
        rows = shape[0]
        columns = lax.broadcasted_iota(jnp.int32, shape, 1)
        names = jnp.where(columns < nodes * rows, columns, -1 - nodes * rows)
        for k in range(nodes):
            here = jnp.logical_and(columns >= k * rows, columns < (k + 1) * rows)
            shift = (lax.rem(node + k, nodes) - k) * rows
            names = jnp.where(here, columns + shift, names)
        return names == targets[...]

    return paired


def inverse_of(values):
    return lax.rsqrt(jnp.sum(values * values, axis=1, keepdims=True) + 1e-06)


def half_rows(raw):
    values = raw[...].astype(FULL)
    return (values * inverse_of(values)).astype(HALF)


def unit_kernel(
    image, text, image_raw, text_raw, image_half, text_half, image_inv, text_inv, sems
):
    blocks = ((image, image_raw, image_half, image_inv), (text, text_raw, text_half, text_inv))
    copies = [
        pltpu.make_async_copy(source, raw, sems.at[i])
        for i, (source, raw, _, _) in enumerate(blocks)
    ]
    for copy in copies:
        copy.start()
    for copy, (_, raw, half, inv) in zip(copies, blocks):
        copy.wait()
        values = raw[...].astype(FULL)
        inverse = inverse_of(values)
        half[...] = (values * inverse).astype(HALF)
        inv[...] = inverse


def prep_kernel(
    names, scale, bias, after, params, row_targets, targets, held, sems
):
    copy = pltpu.make_async_copy(names, held, sems.at[0])
    copy.start()
    row = lax.broadcasted_iota(jnp.int32, params.shape, 0)
    params[...] = jnp.where(row == 0, scale[...], bias[...])
    copy.wait()

    rows = targets.shape[0]
    group, node = lax.axis_index("blk"), lax.axis_index("node")
    nodes = lax.axis_size("node")
    start = (group * nodes + node) * rows
    step = math.gcd(rows, 128)
    lines = -(-(128 - step + rows) // 128)
    window = held[pl.ds(start // 128, lines), :]
    window = jnp.concatenate([window[i : i + 1] for i in range(lines)], axis=1)
    mine = window[:, :rows]
    for at in range(step, 128, step):
        mine = jnp.where(lax.rem(start, 128) == at, window[:, at : at + rows], mine)
    mine = mine - group * nodes * rows
    row_targets[...] = jnp.full(row_targets.shape, -1, jnp.int32)
    row_targets[:, :rows] = mine
    square = (rows, rows)
    same = lax.broadcasted_iota(jnp.int32, square, 0) == lax.broadcasted_iota(
        jnp.int32, square, 1
    )
    turned = jnp.sum(jnp.where(same, mine.astype(FULL), 0.0), axis=1, keepdims=True)
    targets[...] = turned.astype(jnp.int32)


def visit_kernel(raw, after, half):
    half[...] = half_rows(raw)


def got_kernel(far, visit, *refs):
    got = refs[-1]
    got[0] = visit[...]
    for k in range(far):
        got[k + 1] = half_rows(refs[k])


def parted(far, got):
    return got.at[0], [got.at[k + 1] for k in range(far)]


def first_kernel(
    far, params, row_targets, image, text, mate_image, mate_text, got, back, part
):
    visit, far_text = parted(far, got)

    def on_first(node):
        back[0] = drawn_apart(params, visit, [text, *far_text]).astype(HALF)

    def on_second(node):
        for k in range(far):
            pairs = text_pairs(row_targets, lax.rem(node + k + 1, far + 1))
            images = [image, mate_image, visit]
            back[k] = drawn(params, far_text[k], images, pairs).astype(HALF)
        part[...] = drawn(params, visit, [text, *far_text, mate_text])

    by_role(on_first, on_second)


def second_kernel(far, params, row_targets, image, got, mate_got, part, back):
    visit, far_text = parted(far, got)
    mate_visit, mate_far = parted(far, mate_got)

    def on_first(node):
        for k in range(far):
            pairs = text_pairs(row_targets, lax.rem(node + k + 1, far + 1))
            images = [image, visit, mate_visit]
            back[k] = drawn(params, far_text[k], images, pairs).astype(HALF)

    def on_second(node):
        back[0] = (part[...] + drawn(params, visit, mate_far)).astype(HALF)

    by_role(on_first, on_second)


def local_part(raw, inverse, direction):
    inv = inverse[...]
    unit = raw[...].astype(FULL) * inv
    along = jnp.sum(unit * direction, axis=1, keepdims=True)
    return (direction - unit * along) * inv


def third_kernel(
    far, params, row_targets, targets, image, text, mate_image, mate_text, got, mate_got,
    image_raw, image_inv, text_raw, text_inv, image_part, text_part,
):
    visit, far_text = parted(far, got)
    mate_visit, mate_far = parted(far, mate_got)
    nodes = far + 1

    def on_first(node):
        pairs = image_pairs(targets, node, nodes)
        texts = [text, *far_text, mate_text, *mate_far]
        direction = drawn(params, image, texts, pairs)
        image_part[...] = local_part(image_raw, image_inv, direction)
        pairs = text_pairs(row_targets, node)
        direction = drawn(params, text, [image, visit, mate_visit], pairs)
        text_part[...] = local_part(text_raw, text_inv, direction)

    def on_second(node):
        pairs = text_pairs(row_targets, node)
        direction = drawn(params, text, [image, mate_image, visit], pairs)
        text_part[...] = local_part(text_raw, text_inv, direction)
        pairs = image_pairs(targets, node, nodes)
        direction = drawn(params, image, [text, *far_text], pairs)
        image_part[...] = local_part(image_raw, image_inv, direction)

    by_role(on_first, on_second)


def finish(received, own, count, out, start, stop):
    raw, inverse, part = own
    step = 16 if (stop - start) % 16 == 0 else stop - start
    for at in range(start, stop, step):
        piece = pl.ds(at, step)
        gradient = received[0][piece, :].astype(FULL)
        for k in range(1, count):
            gradient += received[k][piece, :].astype(FULL)
        inv = inverse[piece, :]
        values = raw[piece, :].astype(FULL)
        along = jnp.sum(values * gradient, axis=1, keepdims=True) * (inv * inv * inv)
        out[piece, :] = gradient * inv - values * along + part[piece, :]


def out_kernel(far, image_on_first, *refs):
    image, text, received = refs[0:3], refs[3:6], refs[6 : 6 + far]
    image_grads, text_grads, held, sems = refs[-4:]
    rows = held.shape[0]
    part = rows // 10 if rows % 160 == 0 else rows

    def run(own, count, out, node):
        copies = []
        for i, at in enumerate(range(0, rows, part)):
            finish(received, own, count, held, at, at + part)
            piece = pl.ds(at, part)
            copies.append(pltpu.make_async_copy(held.at[piece], out.at[piece], sems.at[i]))
            copies[-1].start()
        for copy in copies:
            copy.wait()

    on_images = functools.partial(run, image, 1, image_grads)
    on_texts = functools.partial(run, text, far, text_grads)
    if image_on_first:
        by_role(on_images, on_texts)
    else:
        by_role(on_texts, on_images)


def call(kernel, name, operands, shapes, anywhere=0, scratch=()):
    operands = list(operands)
    held = pl.BlockSpec(memory_space=pltpu.VMEM)
    for i in range(anywhere):
        operands[i] = pltpu.with_memory_space_constraint(operands[i], pltpu.HBM)
    return pl.pallas_call(
        kernel,
        name=name,
        out_shape=[pltpu.VMEM(s, d) for s, d in shapes],
        in_specs=[pl.BlockSpec(memory_space=pltpu.HBM)] * anywhere
        + [held] * (len(operands) - anywhere),
        out_specs=[held] * len(shapes),
        scratch_shapes=scratch,
        compiler_params=pltpu.CompilerParams(vmem_limit_bytes=VMEM_LIMIT),
    )(*operands)


def write_out(far, image_on_first, operands, grads, block):
    anywhere = pl.BlockSpec(memory_space=pl.ANY)
    count = len(operands)
    return pl.pallas_call(
        functools.partial(out_kernel, far, image_on_first),
        name="out",
        out_shape=[jax.ShapeDtypeStruct(*block)] * 2,
        in_specs=[pl.BlockSpec(memory_space=pltpu.VMEM)] * count + [anywhere] * len(grads),
        out_specs=[anywhere] * 2,
        scratch_shapes=[pltpu.VMEM(*block), pltpu.SemaphoreType.DMA((10,))],
        input_output_aliases={count + i: i for i in range(len(grads))},
        compiler_params=pltpu.CompilerParams(vmem_limit_bytes=VMEM_LIMIT),
    )(*operands, *grads)


def local(image_embeds, text_embeds, pair_text, similarity_scale, logit_bias):
    rows, width = image_embeds.shape
    cycle_count = lax.axis_size("blk")
    node_count = lax.axis_size("node")
    far = node_count - 1

    def send(block, even, odd):
        route = []
        for g in range(cycle_count):
            ahead, across = odd if g % 2 else even
            for n in range(node_count):
                to = (g + ahead) % cycle_count * node_count + (n + across) % node_count
                route.append((g * node_count + n, to))
        return lax.ppermute(block, ("blk", "node"), route)

    def swap(block):
        return send(block, (1, 0), (-1, 0))

    stay = (0, 0)
    ahead, behind = (2, 0), (-2, 0)
    block_h = ((rows, width), HALF)
    block_f = ((rows, width), FULL)
    column = ((rows, 1), FULL)
    returns = ((far, rows, width), HALF)

    visit_raw = send(image_embeds, ahead, ahead)
    far_raw = [send(text_embeds, (0, -k), (0, -k)) for k in range(1, node_count)]

    image_raw, text_raw, image, text, image_inv, text_inv = call(
        unit_kernel,
        "unit",
        [image_embeds, text_embeds],
        [block_h, block_h, block_h, block_h, column, column],
        anywhere=2,
        scratch=[pltpu.SemaphoreType.DMA((2,))],
    )
    mate_image = swap(image)
    mate_text = swap(text)
    names = pair_text.reshape(-1, 128)
    params, row_targets, targets = call(
        prep_kernel,
        "prep",
        [names, similarity_scale[:, None], logit_bias[:, None], image_inv],
        [((8, 128), FULL), ((1, 3 * rows), jnp.int32), ((rows, 1), jnp.int32)],
        anywhere=1,
        scratch=[pltpu.VMEM(names.shape, jnp.int32), pltpu.SemaphoreType.DMA((1,))],
    )
    (visit,) = call(visit_kernel, "visit", [visit_raw, params], [block_h])
    *far_raw, visit = lax.optimization_barrier((*far_raw, visit))
    (got,) = call(
        functools.partial(got_kernel, far),
        "got",
        [visit, *far_raw, mate_image, mate_text],
        [((node_count, rows, width), HALF)],
    )
    back, part = call(
        functools.partial(first_kernel, far),
        "first",
        [params, row_targets, image, text, mate_image, mate_text, got],
        [returns, block_f],
    )
    got, part = lax.optimization_barrier((got, part))
    mate_got = swap(got)
    one = [send(back[k], behind if k == 0 else stay, (0, k + 1)) for k in range(far)]
    (back,) = call(
        functools.partial(second_kernel, far),
        "second",
        [params, row_targets, image, got, mate_got, part],
        [returns],
    )
    two = [send(back[k], (0, k + 1), behind if k == 0 else stay) for k in range(far)]
    image_part, text_part = call(
        functools.partial(third_kernel, far),
        "third",
        [params, row_targets, targets, image, text, mate_image, mate_text, got, mate_got]
        + [image_raw, image_inv, text_raw, text_inv],
        [block_f, block_f],
    )
    own = [image_raw, image_inv, image_part, text_raw, text_inv, text_part]
    grads = write_out(far, True, [*own, *one], [], block_f)
    return tuple(write_out(far, False, [*own, *two], grads, block_f))


def solution(mesh):
    return jax.shard_map(
        local,
        mesh=mesh,
        in_specs=(P(("blk", "node"), None), P(("blk", "node"), None), P(), P(), P()),
        out_specs=(P(("blk", "node"), None), P(("blk", "node"), None)),
        check_vma=False,
    )
```

```python
import functools
import math

import jax
import jax.numpy as jnp
from jax import lax
from jax.experimental import pallas as pl
from jax.experimental.pallas import tpu as pltpu
from jax.sharding import PartitionSpec as P

HALF = jnp.bfloat16
FULL = jnp.float32
VMEM_LIMIT = 8 * 1024 * 1024


def roles():
    return lax.rem(lax.axis_index("blk"), 2) == 0, lax.axis_index("node")


def by_role(on_first, on_second):
    first, node = roles()
    pl.when(first)(functools.partial(on_first, node))
    pl.when(jnp.logical_not(first))(functools.partial(on_second, node))


def drawn(params, rows, partners, paired=None):
    vectors = jnp.concatenate([partner[...] for partner in partners], axis=0)
    dots = lax.dot_general(
        rows[...], vectors, (((1,), (1,)), ((), ())), preferred_element_type=FULL
    )
    scale, bias = params[0:1, 0:1], params[1:2, 0:1]
    logits = scale * dots + bias
    if paired is None:
        weights = scale * jax.nn.sigmoid(logits)
    else:
        pairs = paired(logits.shape)
        weights = jnp.where(pairs, -scale, scale) * jax.nn.sigmoid(
            jnp.where(pairs, -logits, logits)
        )
    return jnp.dot(weights.astype(HALF), vectors, preferred_element_type=FULL)


def drawn_apart(params, rows, partners):
    scale, bias = params[0:1, 0:1], params[1:2, 0:1]
    dots = [
        lax.dot_general(
            rows[...], partner[...], (((1,), (1,)), ((), ())), preferred_element_type=FULL
        )
        for partner in partners
    ]
    weights = [(scale * jax.nn.sigmoid(scale * dot + bias)).astype(HALF) for dot in dots]
    total = None
    for weight, partner in zip(weights, partners):
        term = jnp.dot(weight, partner[...], preferred_element_type=FULL)
        total = term if total is None else total + term
    return total


def text_pairs(targets, node):
    def paired(shape):
        rows = shape[0]
        names = lax.broadcasted_iota(jnp.int32, shape, 0) + node * rows
        return names == targets[:, : shape[1]]

    return paired


def image_pairs(targets, node, nodes):
    def paired(shape):
        rows = shape[0]
        columns = lax.broadcasted_iota(jnp.int32, shape, 1)
        names = jnp.where(columns < nodes * rows, columns, -1 - nodes * rows)
        for k in range(nodes):
            here = jnp.logical_and(columns >= k * rows, columns < (k + 1) * rows)
            shift = (lax.rem(node + k, nodes) - k) * rows
            names = jnp.where(here, columns + shift, names)
        return names == targets[...]

    return paired


def inverse_of(values):
    return lax.rsqrt(jnp.sum(values * values, axis=1, keepdims=True) + 1e-06)


def half_rows(raw):
    values = raw[...].astype(FULL)
    return (values * inverse_of(values)).astype(HALF)


def unit_kernel(
    image, text, image_raw, text_raw, image_half, text_half, image_inv, text_inv, sems
):
    blocks = ((image, image_raw, image_half, image_inv), (text, text_raw, text_half, text_inv))
    copies = [
        pltpu.make_async_copy(source, raw, sems.at[i])
        for i, (source, raw, _, _) in enumerate(blocks)
    ]
    for copy in copies:
        copy.start()
    for copy, (_, raw, half, inv) in zip(copies, blocks):
        copy.wait()
        values = raw[...].astype(FULL)
        inverse = inverse_of(values)
        half[...] = (values * inverse).astype(HALF)
        inv[...] = inverse


def prep_kernel(
    names, scale, bias, after, params, row_targets, targets, held, sems
):
    copy = pltpu.make_async_copy(names, held, sems.at[0])
    copy.start()
    row = lax.broadcasted_iota(jnp.int32, params.shape, 0)
    params[...] = jnp.where(row == 0, scale[...], bias[...])
    copy.wait()

    rows = targets.shape[0]
    group, node = lax.axis_index("blk"), lax.axis_index("node")
    nodes = lax.axis_size("node")
    start = (group * nodes + node) * rows
    step = math.gcd(rows, 128)
    lines = -(-(128 - step + rows) // 128)
    window = held[pl.ds(start // 128, lines), :]
    window = jnp.concatenate([window[i : i + 1] for i in range(lines)], axis=1)
    mine = window[:, :rows]
    for at in range(step, 128, step):
        mine = jnp.where(lax.rem(start, 128) == at, window[:, at : at + rows], mine)
    mine = mine - group * nodes * rows
    row_targets[...] = jnp.full(row_targets.shape, -1, jnp.int32)
    row_targets[:, :rows] = mine
    square = (rows, rows)
    same = lax.broadcasted_iota(jnp.int32, square, 0) == lax.broadcasted_iota(
        jnp.int32, square, 1
    )
    turned = jnp.sum(jnp.where(same, mine.astype(FULL), 0.0), axis=1, keepdims=True)
    targets[...] = turned.astype(jnp.int32)


def visit_kernel(raw, after, half):
    half[...] = half_rows(raw)


def got_kernel(far, visit, *refs):
    got = refs[-1]
    got[0] = visit[...]
    for k in range(far):
        got[k + 1] = half_rows(refs[k])


def parted(far, got):
    return got.at[0], [got.at[k + 1] for k in range(far)]


def first_kernel(
    far, params, row_targets, image, text, mate_image, mate_text, got, back, part
):
    visit, far_text = parted(far, got)

    def on_first(node):
        back[0] = drawn_apart(params, visit, [text, *far_text]).astype(HALF)

    def on_second(node):
        for k in range(far):
            pairs = text_pairs(row_targets, lax.rem(node + k + 1, far + 1))
            images = [image, mate_image, visit]
            back[k] = drawn(params, far_text[k], images, pairs).astype(HALF)
        part[...] = drawn(params, visit, [text, *far_text, mate_text])

    by_role(on_first, on_second)


def second_kernel(far, params, row_targets, image, got, mate_got, part, back):
    visit, far_text = parted(far, got)
    mate_visit, mate_far = parted(far, mate_got)

    def on_first(node):
        for k in range(far):
            pairs = text_pairs(row_targets, lax.rem(node + k + 1, far + 1))
            images = [image, visit, mate_visit]
            back[k] = drawn(params, far_text[k], images, pairs).astype(HALF)

    def on_second(node):
        back[0] = (part[...] + drawn(params, visit, mate_far)).astype(HALF)

    by_role(on_first, on_second)


def local_part(raw, inverse, direction):
    inv = inverse[...]
    unit = raw[...].astype(FULL) * inv
    along = jnp.sum(unit * direction, axis=1, keepdims=True)
    return (direction - unit * along) * inv


def third_kernel(
    far, params, row_targets, targets, image, text, mate_image, mate_text, got, mate_got,
    image_raw, image_inv, text_raw, text_inv, image_part, text_part,
):
    visit, far_text = parted(far, got)
    mate_visit, mate_far = parted(far, mate_got)
    nodes = far + 1

    def on_first(node):
        pairs = image_pairs(targets, node, nodes)
        texts = [text, *far_text, mate_text, *mate_far]
        direction = drawn(params, image, texts, pairs)
        image_part[...] = local_part(image_raw, image_inv, direction)
        pairs = text_pairs(row_targets, node)
        direction = drawn(params, text, [image, visit, mate_visit], pairs)
        text_part[...] = local_part(text_raw, text_inv, direction)

    def on_second(node):
        pairs = text_pairs(row_targets, node)
        direction = drawn(params, text, [image, mate_image, visit], pairs)
        text_part[...] = local_part(text_raw, text_inv, direction)
        pairs = image_pairs(targets, node, nodes)
        direction = drawn(params, image, [text, *far_text], pairs)
        image_part[...] = local_part(image_raw, image_inv, direction)

    by_role(on_first, on_second)


def finish(received, own, count, out, start, stop):
    raw, inverse, part = own
    step = 16 if (stop - start) % 16 == 0 else stop - start
    for at in range(start, stop, step):
        piece = pl.ds(at, step)
        gradient = received[0][piece, :].astype(FULL)
        for k in range(1, count):
            gradient += received[k][piece, :].astype(FULL)
        inv = inverse[piece, :]
        values = raw[piece, :].astype(FULL)
        along = jnp.sum(values * gradient, axis=1, keepdims=True) * (inv * inv * inv)
        out[piece, :] = gradient * inv - values * along + part[piece, :]


def out_kernel(far, image_on_first, *refs):
    image, text, received = refs[0:3], refs[3:6], refs[6 : 6 + far]
    image_grads, text_grads, held, sems = refs[-4:]
    rows = held.shape[0]
    part = rows // 2 if rows % 32 == 0 else rows

    def run(own, count, out, node):
        copies = []
        for i, at in enumerate(range(0, rows, part)):
            finish(received, own, count, held, at, at + part)
            piece = pl.ds(at, part)
            copies.append(pltpu.make_async_copy(held.at[piece], out.at[piece], sems.at[i]))
            copies[-1].start()
        for copy in copies:
            copy.wait()

    on_images = functools.partial(run, image, 1, image_grads)
    on_texts = functools.partial(run, text, far, text_grads)
    if image_on_first:
        by_role(on_images, on_texts)
    else:
        by_role(on_texts, on_images)


def call(kernel, name, operands, shapes, anywhere=0, scratch=()):
    operands = list(operands)
    held = pl.BlockSpec(memory_space=pltpu.VMEM)
    for i in range(anywhere):
        operands[i] = pltpu.with_memory_space_constraint(operands[i], pltpu.HBM)
    return pl.pallas_call(
        kernel,
        name=name,
        out_shape=[pltpu.VMEM(s, d) for s, d in shapes],
        in_specs=[pl.BlockSpec(memory_space=pltpu.HBM)] * anywhere
        + [held] * (len(operands) - anywhere),
        out_specs=[held] * len(shapes),
        scratch_shapes=scratch,
        compiler_params=pltpu.CompilerParams(vmem_limit_bytes=VMEM_LIMIT),
    )(*operands)


def write_out(far, image_on_first, operands, grads, block):
    anywhere = pl.BlockSpec(memory_space=pl.ANY)
    count = len(operands)
    return pl.pallas_call(
        functools.partial(out_kernel, far, image_on_first),
        name="out",
        out_shape=[jax.ShapeDtypeStruct(*block)] * 2,
        in_specs=[pl.BlockSpec(memory_space=pltpu.VMEM)] * count + [anywhere] * len(grads),
        out_specs=[anywhere] * 2,
        scratch_shapes=[pltpu.VMEM(*block), pltpu.SemaphoreType.DMA((2,))],
        input_output_aliases={count + i: i for i in range(len(grads))},
        compiler_params=pltpu.CompilerParams(vmem_limit_bytes=VMEM_LIMIT),
    )(*operands, *grads)


def local(image_embeds, text_embeds, pair_text, similarity_scale, logit_bias):
    rows, width = image_embeds.shape
    cycle_count = lax.axis_size("blk")
    node_count = lax.axis_size("node")
    far = node_count - 1

    def send(block, even, odd):
        route = []
        for g in range(cycle_count):
            ahead, across = odd if g % 2 else even
            for n in range(node_count):
                to = (g + ahead) % cycle_count * node_count + (n + across) % node_count
                route.append((g * node_count + n, to))
        return lax.ppermute(block, ("blk", "node"), route)

    def swap(block):
        return send(block, (1, 0), (-1, 0))

    stay = (0, 0)
    ahead, behind = (2, 0), (-2, 0)
    block_h = ((rows, width), HALF)
    block_f = ((rows, width), FULL)
    column = ((rows, 1), FULL)
    returns = ((far, rows, width), HALF)

    visit_raw = send(image_embeds, ahead, ahead)
    far_raw = [send(text_embeds, (0, -k), (0, -k)) for k in range(1, node_count)]

    image_raw, text_raw, image, text, image_inv, text_inv = call(
        unit_kernel,
        "unit",
        [image_embeds, text_embeds],
        [block_h, block_h, block_h, block_h, column, column],
        anywhere=2,
        scratch=[pltpu.SemaphoreType.DMA((2,))],
    )
    mate_image = swap(image)
    mate_text = swap(text)
    names = pair_text.reshape(-1, 128)
    params, row_targets, targets = call(
        prep_kernel,
        "prep",
        [names, similarity_scale[:, None], logit_bias[:, None], image_inv],
        [((8, 128), FULL), ((1, 3 * rows), jnp.int32), ((rows, 1), jnp.int32)],
        anywhere=1,
        scratch=[pltpu.VMEM(names.shape, jnp.int32), pltpu.SemaphoreType.DMA((1,))],
    )
    (visit,) = call(visit_kernel, "visit", [visit_raw, params], [block_h])
    *far_raw, visit = lax.optimization_barrier((*far_raw, visit))
    (got,) = call(
        functools.partial(got_kernel, far),
        "got",
        [visit, *far_raw, mate_image, mate_text],
        [((node_count, rows, width), HALF)],
    )
    back, part = call(
        functools.partial(first_kernel, far),
        "first",
        [params, row_targets, image, text, mate_image, mate_text, got],
        [returns, block_f],
    )
    got, part = lax.optimization_barrier((got, part))
    mate_got = swap(got)
    one = [send(back[k], behind if k == 0 else stay, (0, k + 1)) for k in range(far)]
    (back,) = call(
        functools.partial(second_kernel, far),
        "second",
        [params, row_targets, image, got, mate_got, part],
        [returns],
    )
    two = [send(back[k], (0, k + 1), behind if k == 0 else stay) for k in range(far)]
    image_part, text_part = call(
        functools.partial(third_kernel, far),
        "third",
        [params, row_targets, targets, image, text, mate_image, mate_text, got, mate_got]
        + [image_raw, image_inv, text_raw, text_inv],
        [block_f, block_f],
    )
    own = [image_raw, image_inv, image_part, text_raw, text_inv, text_part]
    grads = write_out(far, True, [*own, *one], [], block_f)
    return tuple(write_out(far, False, [*own, *two], grads, block_f))


def solution(mesh):
    return jax.shard_map(
        local,
        mesh=mesh,
        in_specs=(P(("blk", "node"), None), P(("blk", "node"), None), P(), P(), P()),
        out_specs=(P(("blk", "node"), None), P(("blk", "node"), None)),
        check_vma=False,
    )
```
